32 devices in a mesh: groups: 2 (over x), gx: 16 (over z, y, core).
Axes of the slice: x: 2, y: 2, z: 4, core: 2. Of those that a mesh axis runs over, the one named last changes fastest.
Arguments:
- activations: bfloat16 [768, 8192], P('groups', 'gx'), parts along dimension 0, may hold values from -320 to 320, as said below
- norm_gain: bfloat16 [8192], P('gx'), may hold values from 0.25 to 1.75
- gate_weight: bfloat16 [8192, 26624], P(None, 'gx'), may hold values from -0.09375 to 0.09375
- up_weight: bfloat16 [8192, 26624], P(None, 'gx'), may hold values from -0.0625 to 0.0625
- down_weight: bfloat16 [26624, 8192], P('gx'), may hold values from -0.0546875 to 0.0546875
Outputs:
- updated: bfloat16 [768, 8192], P('groups', 'gx'), parts along dimension 0
The draws below stay inside these ranges and needn't reach their ends.
There are 2 independent parts, one for each index of `groups`. The reference program is written for one: setup_inputs(seed, part) draws one part's arguments, and reference() takes and returns one part's arrays. A program takes and returns all parts, laid end to end along the dimension named above; an argument that names none is the same for every part. Nothing has to cross between parts.
Inputs may be any that keep to these rules, and one draw needn't show every extreme that they name: real-valued activations of each replica.
All inputs are finite; a program needn't handle non-finite values.
Results may differ from the reference program's by a relative error of at most 0.0015.
Values may be sent and summed in bfloat16 or wider, within the bound.
No kernel may reach another device: no remote copies, remote signals or barrier semaphores. Data moves between devices by JAX's collectives and lax.ppermute only.
A program may use at most 192 MiB of HBM per device.

```python
import math
import jax
import jax.numpy as jnp
from jax import lax

D = 8192
FF = 26624
ROWS = 384


def draw_activations(key, part):
    key = jax.random.fold_in(key, 11)
    row_key, col_key, base_key = jax.random.split(key, 3)
    row_scale = jnp.exp(jax.random.uniform(row_key, (ROWS, 1), jnp.float32, 0.0, math.log(10.0)))
    rough = jnp.exp(jax.random.uniform(col_key, (1, D), jnp.float32, math.log(0.5), math.log(2.0)))
    base = jnp.clip(jax.random.normal(base_key, (ROWS, D), jnp.float32), -4.0, 4.0)
    rise = math.log(3.0)
    position = jnp.arange(D, dtype=jnp.float32)[None, :] / D
    col_scale = jnp.exp(rise * position) * rough
    return (base * row_scale * col_scale).astype(jnp.bfloat16)


def raised(result, rng, source, target, shards_of, factor):
    owner, partner = [(jnp.arange(result.shape[dim]) // (result.shape[dim] // shards_of)).reshape([-1 if axis == dim else 1 for axis in range(result.ndim)]) for dim in (source, target)]
    chosen = jax.random.permutation(rng, shards_of)[partner]
    strong = (owner == chosen) | (owner == (partner + shards_of // 2) % shards_of)
    return jnp.where(strong, factor * result, result)


def shard_levels(own_key, dims, cuts, smallest, largest):
    loudness = 1.0
    for dim, shards_of in cuts:
        heights = jax.random.uniform(jax.random.fold_in(jax.random.fold_in(own_key, 6), dim), (shards_of,), jnp.float32, smallest / len(cuts), largest / len(cuts))
        loudness = loudness * jnp.repeat(jnp.exp(heights), dims[dim] // shards_of).reshape((-1,) + (1,) * (len(dims) - 1 - dim))
    return loudness


def gaussian(rng, shape, width, limit, cuts=(), kind=jnp.bfloat16):
    values = width * jax.random.normal(rng, shape, jnp.float32)
    if cuts:
        values = values * shard_levels(rng, shape, cuts, -0.22, 0.18)
    return jnp.clip(values, -limit, limit).astype(kind)


def noise_with(key, extent, width, bound, cuts, heavy, kind=jnp.bfloat16):
    result = width * jax.random.normal(key, extent, jnp.float32)
    if cuts:
        result = result * shard_levels(key, extent, cuts, -0.22, 0.18)
    return jnp.clip(raised(result, jax.random.fold_in(key, 3), *heavy), -bound, bound).astype(kind)


def setup_inputs(seed: int = 0, part: int = 0) -> dict:
    arg_keys = jax.random.split(jax.random.key(seed), 6)
    part_splits = jax.random.split(jax.random.fold_in(arg_keys[5], part), 6)
    return {
        "activations": draw_activations(jax.random.fold_in(jax.random.fold_in(arg_keys[5], part), 71), part),
        "norm_gain": jnp.clip(1.0 + 0.15 * jax.random.normal(arg_keys[1], (D,), jnp.float32), 0.25, 1.75).astype(jnp.bfloat16),
        "gate_weight": noise_with(arg_keys[2], (D, FF), D ** -0.5, 0.09375, ((1, 16),), (0, 1, 16, 2.0)),
        "up_weight": gaussian(arg_keys[3], (D, FF), D ** -0.5, 0.0625, ((1, 16),)),
        "down_weight": noise_with(arg_keys[4], (FF, D), FF ** -0.5, 0.0546875, ((0, 16),), (0, 1, 16, 2.0)),
    }


epsilon = 1e-05

def reference(activations, norm_gain, gate_weight, up_weight, down_weight):
    resident = activations.astype(jnp.float32)
    factor = jax.lax.rsqrt(lax.optimization_barrier(jnp.mean(resident * resident, axis=1, keepdims=True)) + epsilon)
    normed = (resident * factor * norm_gain.astype(jnp.float32)[None, :]).astype(jnp.bfloat16)
    gate_sum = jnp.dot(normed, gate_weight, preferred_element_type=jnp.float32)
    up_sum = jnp.dot(normed, up_weight, preferred_element_type=jnp.float32)
    hidden = (jax.nn.silu(gate_sum) * up_sum).astype(jnp.bfloat16)
    branch = jnp.dot(hidden, down_weight, preferred_element_type=jnp.float32)
    return (resident + branch).astype(jnp.bfloat16)
```

```python
import functools

import jax
import jax.numpy as jnp
from jax import lax
from jax.experimental import pallas as pl
from jax.experimental.pallas import tpu as pltpu
from jax.sharding import PartitionSpec as P

epsilon = 1e-05
INNER = 4
GAIN_ROWS = 16
VMEM_LIMIT = 56 * 1024 * 1024


def swap(x, mask, n):
    return lax.ppermute(x, "gx", [(i, i ^ mask) for i in range(n)])


def gate_up_body(first, last, rows, idx_ref, *refs):
    blocks = refs[:INNER]
    factor_ref, gate_ref, up_ref = refs[INNER : INNER + 3]
    rest = refs[INNER + 3 :]
    if not first:
        gate_in, up_in = rest[:2]
        rest = rest[2:]
    if last:
        hidden_ref, gate_acc, up_acc = rest
    else:
        gate_acc, up_acc = rest
    step = pl.program_id(0)

    for s in range(INNER):

        @pl.when(step == s)
        def _(s=s):
            x = blocks[s][:rows, :].astype(jnp.float32)
            gain = blocks[s][rows : rows + GAIN_ROWS, :].astype(jnp.float32)[:1, :]
            normed = (x * factor_ref[:, :1] * gain).astype(jnp.bfloat16)
            g = jnp.dot(normed, gate_ref[...], preferred_element_type=jnp.float32)
            u = jnp.dot(normed, up_ref[...], preferred_element_type=jnp.float32)
            if s == 0:
                if first:
                    gate_acc[...] = g
                    up_acc[...] = u
                else:
                    gate_acc[...] = gate_in[...] + g
                    up_acc[...] = up_in[...] + u
            elif s == INNER - 1 and last:
                g = gate_acc[...] + g
                u = up_acc[...] + u
                hidden_ref[...] = (g / (1.0 + jnp.exp(-g)) * u).astype(jnp.bfloat16)
            else:
                gate_acc[...] += g
                up_acc[...] += u


def gate_up(idx, blocks, factor, gate_weight, up_weight, acc, last):
    rows = factor.shape[0]
    depth = blocks[0].shape[1]
    ff = gate_weight.shape[1]
    first = acc is None
    whole = lambda shape: pl.BlockSpec(shape, lambda s, idx: (0, 0))
    weight = pl.BlockSpec((depth, ff), lambda s, idx: (idx[s], 0))
    in_specs = [whole(b.shape) for b in blocks] + [whole(factor.shape), weight, weight]
    args = list(blocks) + [factor, gate_weight, up_weight]
    if not first:
        in_specs += [whole((rows, ff))] * 2
        args += list(acc)
    if last:
        out_shape = [jax.ShapeDtypeStruct((rows, ff), jnp.bfloat16)]
        out_specs = [whole((rows, ff))]
        scratch = [pltpu.VMEM((rows, ff), jnp.float32)] * 2
    else:
        out_shape = [jax.ShapeDtypeStruct((rows, ff), jnp.float32)] * 2
        out_specs = [whole((rows, ff))] * 2
        scratch = []
    return pl.pallas_call(
        functools.partial(gate_up_body, first, last, rows),
        grid_spec=pltpu.PrefetchScalarGridSpec(
            num_scalar_prefetch=1,
            grid=(INNER,),
            in_specs=in_specs,
            out_specs=out_specs,
            scratch_shapes=scratch,
        ),
        out_shape=out_shape,
        compiler_params=pltpu.CompilerParams(vmem_limit_bytes=VMEM_LIMIT),
        cost_estimate=pl.CostEstimate(
            flops=4 * rows * depth * INNER * ff,
            bytes_accessed=4 * depth * INNER * ff + 8 * rows * ff,
            transcendentals=0,
        ),
        name="gate_up",
    )(idx, *args)


def down_body(idx_ref, hidden_ref, weight_ref, out_ref):
    out_ref[0] = jnp.dot(
        hidden_ref[...], weight_ref[...], preferred_element_type=jnp.float32
    ).astype(out_ref.dtype)


def down(idx, hidden, down_weight, width, dtype):
    rows, ff = hidden.shape
    count = idx.shape[0]
    return pl.pallas_call(
        down_body,
        grid_spec=pltpu.PrefetchScalarGridSpec(
            num_scalar_prefetch=1,
            grid=(count,),
            in_specs=[
                pl.BlockSpec((rows, ff), lambda s, idx: (0, 0)),
                pl.BlockSpec((ff, width), lambda s, idx: (0, idx[s])),
            ],
            out_specs=pl.BlockSpec((1, rows, width), lambda s, idx: (s, 0, 0)),
        ),
        out_shape=jax.ShapeDtypeStruct((count, rows, width), dtype),
        compiler_params=pltpu.CompilerParams(vmem_limit_bytes=VMEM_LIMIT),
        cost_estimate=pl.CostEstimate(
            flops=2 * rows * ff * width * count,
            bytes_accessed=2 * ff * width * count + 4 * rows * width * count,
            transcendentals=0,
        ),
        name="down",
    )(idx, hidden, down_weight)


def overlapped(n, activations, norm_gain, gate_weight, up_weight, down_weight):
    rows, width = activations.shape
    outer = n // INNER
    me = lax.axis_index("gx")
    resident = activations.astype(jnp.float32)

    gains = jnp.broadcast_to(norm_gain[None, :], (GAIN_ROWS, width))
    shard = jnp.concatenate([activations, gains], axis=0)

    total = jnp.sum(resident * resident, axis=1)
    total = total + sum(swap(total, INNER * k, n) for k in range(1, outer))
    total = total + swap(total, 2, n)
    total = total + swap(total, 1, n)
    factor = lax.rsqrt(total / (width * n) + epsilon)
    factor = jnp.broadcast_to(factor[:, None], (rows, 128))

    acc = None
    for k in range(outer):
        a = shard if k == 0 else swap(shard, INNER * k, n)
        b = swap(a, 2, n)
        blocks = [a, b, swap(a, 1, n), swap(b, 1, n)]
        idx = jnp.stack([me ^ (INNER * k + q) for q in (0, 2, 1, 3)]).astype(jnp.int32)
        acc = gate_up(idx, blocks, factor, gate_weight, up_weight, acc, k == outer - 1)
    hidden = acc[0]

    branch = None
    for k in reversed(range(outer)):
        away = jnp.stack([me ^ (INNER * k + q) for q in (3, 1)]).astype(jnp.int32)
        stay = jnp.stack([me ^ (INNER * k + q) for q in (2, 0)]).astype(jnp.int32)
        sent = down(away, hidden, down_weight, width, jnp.bfloat16)
        kept = down(stay, hidden, down_weight, width, jnp.float32)
        got = swap(sent, 1, n).astype(jnp.float32)
        far = (kept[0] + got[0]).astype(jnp.bfloat16)
        near = kept[1] + got[1]
        near = near + swap(far, 2, n).astype(jnp.float32)
        if k:
            near = swap(near.astype(jnp.bfloat16), INNER * k, n).astype(jnp.float32)
        branch = near if branch is None else branch + near
    return (resident + branch).astype(jnp.bfloat16)


def plain(activations, norm_gain, gate_weight, up_weight, down_weight):
    resident = activations.astype(jnp.float32)
    totals = lax.psum(jnp.sum(resident * resident, axis=1), "gx")
    factor = lax.rsqrt(totals / (resident.shape[1] * lax.axis_size("gx")) + epsilon)
    normed = (resident * factor[:, None] * norm_gain.astype(jnp.float32)[None, :]).astype(
        jnp.bfloat16
    )
    pieces = lax.all_gather(normed, "gx", axis=1, tiled=True)
    gate_sum = jnp.dot(pieces, gate_weight, preferred_element_type=jnp.float32)
    up_sum = jnp.dot(pieces, up_weight, preferred_element_type=jnp.float32)
    hidden = (jax.nn.silu(gate_sum) * up_sum).astype(jnp.bfloat16)
    summed = lax.psum_scatter(
        lax.dot_general(
            down_weight, hidden, (((0,), (1,)), ((), ())), preferred_element_type=jnp.float32
        ),
        "gx",
        scatter_dimension=0,
        tiled=True,
    )
    return (resident + summed.T).astype(jnp.bfloat16)


def per_device(n, activations, norm_gain, gate_weight, up_weight, down_weight):
    args = (activations, norm_gain, gate_weight, up_weight, down_weight)
    outer = n // INNER
    aligned = activations.shape[1] % 128 == 0 and gate_weight.shape[1] % 128 == 0
    if aligned and n == INNER * outer and outer & (outer - 1) == 0 and outer <= 8:
        return overlapped(n, *args)
    return plain(*args)


def solution(mesh):
    in_specs = (P("groups", "gx"), P("gx"), P(None, "gx"), P(None, "gx"), P("gx", None))
    out_specs = P("groups", "gx")
    return jax.shard_map(
        functools.partial(per_device, mesh.shape["gx"]),
        mesh=mesh,
        in_specs=in_specs,
        out_specs=out_specs,
        check_vma=False,
    )
```

```python
import functools

import jax
import jax.numpy as jnp
from jax import lax
from jax.experimental import pallas as pl
from jax.experimental.pallas import tpu as pltpu
from jax.sharding import PartitionSpec as P

epsilon = 1e-05
INNER = 4
LINE = 4
VMEM_LIMIT = 30 * 1024 * 1024

PAIRS = ((0, 1), (1, 0), (2, 3), (3, 2))
MIDDLE = ((1, 2), (2, 1))
OUTWARD = ((1, 0), (2, 3))
INWARD = ((0, 1), (3, 2))


def swap(x, mask):
    return lax.ppermute(x, "gx", [(i, i ^ mask) for i in range(INNER * LINE)])


def along(x, pairs):
    moves = [(a * INNER + q, b * INNER + q) for a, b in pairs for q in range(INNER)]
    return lax.ppermute(x, "gx", moves)


def pick(table, s):
    value = jnp.int32(table[0])
    for i, entry in enumerate(table[1:], 1):
        value = jnp.where(s == i, jnp.int32(entry), value)
    return value


def gate_up_body(codes, first, last, rows, main, features, me_ref, *refs):
    count = len(codes)
    blocks = refs[:count]
    stats_ref, gate_ref, up_ref = refs[count : count + 3]
    rest = refs[count + 3 :]
    if not first:
        before = rest[:3]
        rest = rest[3:]
    if last:
        hidden_ref, *rest = rest
    gate_acc, up_acc, mixed_acc, factor_ref = rest[-4:]
    step = pl.program_id(0)

    @pl.when(step == 0)
    def _():
        total = jnp.sum(stats_ref[:, :rows], axis=0, keepdims=True)
        factor = lax.rsqrt(total / features + epsilon)
        factor_ref[...] = jnp.broadcast_to(factor, (128, rows)).T

    for s in range(count):

        @pl.when(step == s)
        def _(s=s):
            gain = stats_ref[pl.ds(me_ref[0] ^ codes[s], 1), rows:]
            x = blocks[s][...].astype(jnp.float32)
            normed = (x * factor_ref[:, :1] * gain).astype(jnp.bfloat16)
            gate = gate_ref[...]
            up = up_ref[...]
            mixed = jnp.concatenate([gate[:, main:], up[:, main:]], axis=1)
            sums = []
            for acc, old, weight in zip(
                (gate_acc, up_acc, mixed_acc),
                (None,) * 3 if first else before,
                (gate[:, :main], up[:, :main], mixed),
            ):
                value = jnp.dot(normed, weight, preferred_element_type=jnp.float32)
                if s:
                    value = acc[...] + value
                elif old is not None:
                    value = old[...] + value
                if s == count - 1 and last:
                    sums.append(value)
                else:
                    acc[...] = value
            if sums:
                g, u, m = sums
                rem = m.shape[1] // 2
                hidden_ref[:, :main] = (g / (1.0 + jnp.exp(-g)) * u).astype(jnp.bfloat16)
                g, u = m[:, :rem], m[:, rem:]
                hidden_ref[:, main:] = (g / (1.0 + jnp.exp(-g)) * u).astype(jnp.bfloat16)


def gate_up(me, blocks, codes, stats, gate_weight, up_weight, acc, last):
    rows, depth = blocks[0].shape
    features, ff = gate_weight.shape
    main = ff // 256 * 256 if ff % 256 else ff - 256
    rem = ff - main
    first = acc is None
    count = len(blocks)
    whole = lambda shape: pl.BlockSpec(shape, lambda s, me: (0, 0))
    weight = pl.BlockSpec((depth, ff), lambda s, me: (me[0] ^ pick(codes, s), 0))
    in_specs = [whole(b.shape) for b in blocks] + [whole(stats.shape), weight, weight]
    args = list(blocks) + [stats, gate_weight, up_weight]
    shapes = [(rows, main), (rows, main), (rows, 2 * rem)]
    if not first:
        in_specs += [whole(s) for s in shapes]
        args += list(acc)
    scratch = [pltpu.VMEM((rows, 128), jnp.float32)]
    if last:
        out_shape = [jax.ShapeDtypeStruct((rows, ff), jnp.bfloat16)]
        out_specs = [whole((rows, ff))]
        scratch = [pltpu.VMEM(s, jnp.float32) for s in shapes] + scratch
    else:
        out_shape = [jax.ShapeDtypeStruct(s, jnp.float32) for s in shapes]
        out_specs = [whole(s) for s in shapes]
    return pl.pallas_call(
        functools.partial(gate_up_body, codes, first, last, rows, main, features),
        grid_spec=pltpu.PrefetchScalarGridSpec(
            num_scalar_prefetch=1,
            grid=(count,),
            in_specs=in_specs,
            out_specs=out_specs,
            scratch_shapes=scratch,
        ),
        out_shape=out_shape,
        compiler_params=pltpu.CompilerParams(vmem_limit_bytes=VMEM_LIMIT),
        cost_estimate=pl.CostEstimate(
            flops=4 * rows * depth * count * ff,
            bytes_accessed=4 * depth * count * ff,
            transcendentals=0,
        ),
        name="gate_up",
    )(me, *args)


def down_block(hidden_ref, weight_ref):
    ff = hidden_ref.shape[1]
    main = ff // 256 * 256
    value = jnp.dot(
        hidden_ref[:, :main], weight_ref[:main, :], preferred_element_type=jnp.float32
    )
    if main < ff:
        value = value + jnp.dot(
            hidden_ref[:, main:], weight_ref[main:, :], preferred_element_type=jnp.float32
        )
    return value


def away_body(me_ref, hidden_ref, weight_ref, after_ref, out_ref):
    out_ref[0] = down_block(hidden_ref, weight_ref).astype(out_ref.dtype)


def stay_body(me_ref, hidden_ref, weight_ref, got_ref, far_ref, near_ref):
    value = down_block(hidden_ref, weight_ref) + got_ref[0].astype(jnp.float32)

    @pl.when(pl.program_id(0) == 0)
    def _():
        far_ref[...] = value.astype(far_ref.dtype)

    @pl.when(pl.program_id(0) == 1)
    def _():
        near_ref[...] = value


def down(body, me, codes, hidden, down_weight, width, extra, extra_spec, out_shape, out_specs):
    rows, ff = hidden.shape
    count = len(codes)
    return pl.pallas_call(
        body,
        grid_spec=pltpu.PrefetchScalarGridSpec(
            num_scalar_prefetch=1,
            grid=(count,),
            in_specs=[
                pl.BlockSpec((rows, ff), lambda s, me: (0, 0)),
                pl.BlockSpec((ff, width), lambda s, me: (0, me[0] ^ pick(codes, s))),
                extra_spec,
            ],
            out_specs=out_specs,
        ),
        out_shape=out_shape,
        compiler_params=pltpu.CompilerParams(vmem_limit_bytes=VMEM_LIMIT),
        cost_estimate=pl.CostEstimate(
            flops=2 * rows * ff * width * count,
            bytes_accessed=2 * ff * width * count,
            transcendentals=0,
        ),
        name=body.__name__,
    )(me, hidden, down_weight, extra)


def overlapped(activations, norm_gain, gate_weight, up_weight, down_weight):
    rows, width = activations.shape
    index = lax.axis_index("gx").astype(jnp.int32)
    z = index // INNER
    edge = (z == 0) | (z == LINE - 1)
    me = index[None]
    resident = activations.astype(jnp.float32)

    stats = jnp.concatenate(
        [jnp.sum(resident * resident, axis=1), norm_gain.astype(jnp.float32)]
    )
    stats = lax.all_gather(stats, "gx")

    neighbour = along(activations, PAIRS)
    inner = along(activations, MIDDLE)
    second_edge = along(inner, OUTWARD)
    second_middle = along(neighbour, MIDDLE)
    third_edge = along(second_middle, OUTWARD)
    slots = [
        activations,
        neighbour,
        jnp.where(edge, second_edge, second_middle),
        jnp.where(edge, third_edge, inner),
    ]
    groups = []
    for slot in slots:
        across = swap(slot, 2)
        groups.append([slot, swap(slot, 1), across, swap(across, 1)])

    order = (0, 1, 2, 3)
    parts = [
        [(k, q) for k in (0,) for q in order],
        [(k, q) for k in (1,) for q in order],
        [(k, q) for k in (2,) for q in order] + [(3, 0), (3, 1)],
        [(3, 2), (3, 3)],
    ]
    acc = None
    for i, part in enumerate(parts):
        codes = tuple(INNER * k + (0, 1, 2, 3)[q] for k, q in part)
        blocks = [groups[k][q] for k, q in part]
        acc = gate_up(
            me, blocks, codes, stats, gate_weight, up_weight, acc, i == len(parts) - 1
        )
    hidden = acc[0]

    def away(k, after):
        return down(
            away_body, me, (INNER * k + 3, INNER * k + 1), hidden, down_weight, width,
            after, pl.BlockSpec(memory_space=pl.ANY),
            jax.ShapeDtypeStruct((2, rows, width), jnp.bfloat16),
            pl.BlockSpec((1, rows, width), lambda s, me: (s, 0, 0)),
        )

    def stay(k, got):
        constant = pl.BlockSpec((rows, width), lambda s, me: (0, 0))
        return down(
            stay_body, me, (INNER * k + 2, INNER * k), hidden, down_weight, width,
            got, pl.BlockSpec((1, rows, width), lambda s, me: (s, 0, 0)),
            [
                jax.ShapeDtypeStruct((rows, width), jnp.bfloat16),
                jax.ShapeDtypeStruct((rows, width), jnp.float32),
            ],
            [constant, constant],
        )

    narrow = lambda x: x.astype(jnp.bfloat16)
    wide = lambda x: x.astype(jnp.float32)

    sums = [None] * LINE
    fars = [None] * LINE
    sent = {LINE - 1: away(LINE - 1, hidden)}
    for k in reversed(range(LINE)):
        if k:
            sent[k - 1] = away(k - 1, fars[k + 1] if k + 1 < LINE else sent[k])
        fars[k], near = stay(k, swap(sent[k], 1))
        sums[k] = near + wide(swap(fars[k], 2))

    middle_two = sums[2] + wide(along(narrow(sums[3]), INWARD))
    middle_three = sums[3] + wide(along(narrow(sums[2]), INWARD))
    one = sums[1] + wide(along(narrow(middle_two), MIDDLE))
    branch = (
        sums[0]
        + wide(along(narrow(one), PAIRS))
        + wide(along(narrow(middle_three), MIDDLE))
    )
    return (resident + branch).astype(jnp.bfloat16)


def plain(activations, norm_gain, gate_weight, up_weight, down_weight):
    resident = activations.astype(jnp.float32)
    totals = lax.psum(jnp.sum(resident * resident, axis=1), "gx")
    factor = lax.rsqrt(totals / (resident.shape[1] * lax.axis_size("gx")) + epsilon)
    normed = (resident * factor[:, None] * norm_gain.astype(jnp.float32)[None, :]).astype(
        jnp.bfloat16
    )
    pieces = lax.all_gather(normed, "gx", axis=1, tiled=True)
    gate_sum = jnp.dot(pieces, gate_weight, preferred_element_type=jnp.float32)
    up_sum = jnp.dot(pieces, up_weight, preferred_element_type=jnp.float32)
    hidden = (jax.nn.silu(gate_sum) * up_sum).astype(jnp.bfloat16)
    summed = lax.psum_scatter(
        lax.dot_general(
            down_weight, hidden, (((0,), (1,)), ((), ())), preferred_element_type=jnp.float32
        ),
        "gx",
        scatter_dimension=0,
        tiled=True,
    )
    return (resident + summed.T).astype(jnp.bfloat16)


def per_device(n, activations, norm_gain, gate_weight, up_weight, down_weight):
    args = (activations, norm_gain, gate_weight, up_weight, down_weight)
    rows, width = activations.shape
    tiled = rows % 128 == 0 and width % 128 == 0 and gate_weight.shape[1] % 128 == 0
    if n == INNER * LINE and tiled:
        return overlapped(*args)
    return plain(*args)


def solution(mesh):
    in_specs = (P("groups", "gx"), P("gx"), P(None, "gx"), P(None, "gx"), P("gx", None))
    out_specs = P("groups", "gx")
    return jax.shard_map(
        functools.partial(per_device, mesh.shape["gx"]),
        mesh=mesh,
        in_specs=in_specs,
        out_specs=out_specs,
        check_vma=False,
    )
```

```python
import functools

import jax
import jax.numpy as jnp
from jax import lax
from jax.experimental import pallas as pl
from jax.experimental.pallas import tpu as pltpu
from jax.sharding import PartitionSpec as P

epsilon = 1e-05
INNER = 4
LINE = 4
UNIT = 256
VMEM_LIMIT = 30 * 1024 * 1024

PAIRS = ((0, 1), (1, 0), (2, 3), (3, 2))
MIDDLE = ((1, 2), (2, 1))
OUTWARD = ((1, 0), (2, 3))
INWARD = ((0, 1), (3, 2))


def swap(x, mask):
    return lax.ppermute(x, "gx", [(i, i ^ mask) for i in range(INNER * LINE)])


def along(x, pairs):
    moves = [(a * INNER + q, b * INNER + q) for a, b in pairs for q in range(INNER)]
    return lax.ppermute(x, "gx", moves)


def pick(table, s):
    value = jnp.int32(table[0])
    for i, entry in enumerate(table[1:], 1):
        value = jnp.where(s == i, jnp.int32(entry), value)
    return value


def accumulator(unit, rows):
    return pltpu.ACC(unit)((rows, UNIT), jnp.float32)


def multiply(lhs_ref, tiles, accs):
    for i in range(max(len(t) for t in tiles)):
        for unit, tile in enumerate(tiles):
            if i < len(tile):
                pltpu.matmul_push_rhs(tile[i][0](), i % 2, unit)
        for unit, tile in enumerate(tiles):
            if i < len(tile):
                at = tile[i][1]
                pltpu.matmul_acc_lhs(
                    accs[unit], lhs_ref[:, at : at + UNIT], load_staged_rhs=i % 2
                )


def gate_up_body(codes, first, last, rows, main, features, me_ref, *refs):
    count = len(codes)
    blocks = refs[:count]
    stats_ref, gate_ref, up_ref = refs[count : count + 3]
    rest = refs[count + 3 :]
    if not first:
        before = rest[:3]
        rest = rest[3:]
    if last:
        hidden_ref, *rest = rest
    gate_acc, up_acc, mixed_acc, factor_ref, normed_ref = rest[-5:]
    step = pl.program_id(0)
    depth, ff = gate_ref.shape

    @pl.when(step == 0)
    def _():
        factor = lax.rsqrt(stats_ref[:1, :rows] / features + epsilon)
        factor_ref[...] = jnp.broadcast_to(factor, (128, rows)).T

    for s in range(count):

        @pl.when(step == s)
        def _(s=s):
            gain = stats_ref[1 + codes[s] : 2 + codes[s], :depth]
            x = blocks[s][...].astype(jnp.float32)
            normed_ref[...] = (x * factor_ref[:, :1] * gain).astype(jnp.bfloat16)

    def tile(ref, n):
        return [
            (lambda k=k: ref[k : k + UNIT, n : n + UNIT], k) for k in range(0, depth, UNIT)
        ]

    def mixed(k):
        return lambda: jnp.concatenate(
            [gate_ref[k : k + UNIT, main:], up_ref[k : k + UNIT, main:]], axis=1
        )

    def keep(ref, old, n, value):
        at = (slice(None), slice(n, n + UNIT))

        if first:

            @pl.when(step == 0)
            def _():
                ref[at] = value

            @pl.when(step > 0)
            def _():
                ref[at] += value

        else:

            @pl.when(step == 0)
            def _():
                ref[at] = old[at] + value

            @pl.when(step > 0)
            def _():
                ref[at] += value

    before = (None,) * 3 if first else before

    def run(a0, a1, b0, b1):
        units = ((a0, a1), (b0, b1))
        for j, n in enumerate(range(0, main, UNIT)):
            accs = units[j % 2]
            multiply(normed_ref, [tile(gate_ref, n), tile(up_ref, n)], accs)
            keep(gate_acc, before[0], n, pltpu.matmul_pop(accs[0]))
            keep(up_acc, before[1], n, pltpu.matmul_pop(accs[1]))
        ks = list(range(0, depth, UNIT))
        accs = units[(main // UNIT) % 2]
        multiply(
            normed_ref,
            [[(mixed(k), k) for k in ks[0::2]], [(mixed(k), k) for k in ks[1::2]]],
            accs,
        )
        keep(mixed_acc, before[2], 0, pltpu.matmul_pop(accs[0]) + pltpu.matmul_pop(accs[1]))

    pl.run_scoped(run, *(accumulator(unit, rows) for unit in (0, 1, 0, 1)))

    if last:

        @pl.when(step == count - 1)
        def _():
            rem = ff - main
            for n in range(0, main, UNIT):
                g, u = gate_acc[:, n : n + UNIT], up_acc[:, n : n + UNIT]
                hidden_ref[:, n : n + UNIT] = (g / (1.0 + jnp.exp(-g)) * u).astype(
                    jnp.bfloat16
                )
            g, u = mixed_acc[:, :rem], mixed_acc[:, rem:]
            hidden_ref[:, main:ff] = (g / (1.0 + jnp.exp(-g)) * u).astype(jnp.bfloat16)
            hidden_ref[:, ff:] = jnp.zeros((rows, rem), jnp.bfloat16)


def gate_up(me, blocks, codes, stats, gate_weight, up_weight, acc, last):
    rows, depth = blocks[0].shape
    features, ff = gate_weight.shape
    main = ff // UNIT * UNIT
    rem = ff - main
    first = acc is None
    count = len(blocks)
    whole = lambda shape: pl.BlockSpec(shape, lambda s, me: (0, 0))
    weight = pl.BlockSpec((depth, ff), lambda s, me: (me[0] ^ pick(codes, s), 0))
    in_specs = [whole(b.shape) for b in blocks] + [whole(stats.shape), weight, weight]
    args = list(blocks) + [stats, gate_weight, up_weight]
    shapes = [(rows, main), (rows, main), (rows, 2 * rem)]
    if not first:
        in_specs += [whole(s) for s in shapes]
        args += list(acc)
    scratch = [pltpu.VMEM((rows, 128), jnp.float32), pltpu.VMEM((rows, depth), jnp.bfloat16)]
    if last:
        out_shape = [jax.ShapeDtypeStruct((rows, ff + rem), jnp.bfloat16)]
        out_specs = [whole((rows, ff + rem))]
        scratch = [pltpu.VMEM(s, jnp.float32) for s in shapes] + scratch
    else:
        out_shape = [jax.ShapeDtypeStruct(s, jnp.float32) for s in shapes]
        out_specs = [whole(s) for s in shapes]
    return pl.pallas_call(
        functools.partial(gate_up_body, codes, first, last, rows, main, features),
        grid_spec=pltpu.PrefetchScalarGridSpec(
            num_scalar_prefetch=1,
            grid=(count,),
            in_specs=in_specs,
            out_specs=out_specs,
            scratch_shapes=scratch,
        ),
        out_shape=out_shape,
        compiler_params=pltpu.CompilerParams(vmem_limit_bytes=VMEM_LIMIT),
        cost_estimate=pl.CostEstimate(
            flops=4 * rows * depth * count * ff,
            bytes_accessed=4 * depth * count * ff,
            transcendentals=0,
        ),
        name="gate_up",
    )(me, *args)


def down_block(hidden_ref, weight_ref, use):
    ff, width = weight_ref.shape
    main = ff // UNIT * UNIT

    def tile(n):
        whole = [
            (lambda k=k: weight_ref[k : k + UNIT, n : n + UNIT], k) for k in range(0, main, UNIT)
        ]
        zeros = jnp.zeros((main + UNIT - ff, UNIT), weight_ref.dtype)
        part = lambda: jnp.concatenate([weight_ref[main:, n : n + UNIT], zeros], axis=0)
        return whole + [(part, main)]

    def run(*accs):
        multiply(hidden_ref, [tile(0), tile(UNIT)], accs)
        for i, acc in enumerate(accs):
            use((slice(None), slice(i * UNIT, (i + 1) * UNIT)), pltpu.matmul_pop(acc))

    pl.run_scoped(run, *(accumulator(unit, hidden_ref.shape[0]) for unit in (0, 1)))


def away_body(me_ref, hidden_ref, weight_ref, after_ref, out_ref):
    def use(at, value):
        out_ref[(0,) + at] = value.astype(out_ref.dtype)

    down_block(hidden_ref, weight_ref, use)


def stay_body(me_ref, hidden_ref, weight_ref, got_ref, far_ref, near_ref):
    def use(at, value):
        value = value + got_ref[(0,) + at].astype(jnp.float32)

        @pl.when(pl.program_id(0) == 0)
        def _():
            far_ref[at] = value.astype(far_ref.dtype)

        @pl.when(pl.program_id(0) == 1)
        def _():
            near_ref[at] = value

    down_block(hidden_ref, weight_ref, use)


def down(body, me, codes, hidden, down_weight, width, extra, extra_spec, out_shape, out_specs):
    rows = hidden.shape[0]
    ff = down_weight.shape[0]
    count = len(codes)
    return pl.pallas_call(
        body,
        grid_spec=pltpu.PrefetchScalarGridSpec(
            num_scalar_prefetch=1,
            grid=(count,),
            in_specs=[
                pl.BlockSpec(hidden.shape, lambda s, me: (0, 0)),
                pl.BlockSpec((ff, width), lambda s, me: (0, me[0] ^ pick(codes, s))),
                extra_spec,
            ],
            out_specs=out_specs,
        ),
        out_shape=out_shape,
        compiler_params=pltpu.CompilerParams(vmem_limit_bytes=VMEM_LIMIT),
        cost_estimate=pl.CostEstimate(
            flops=2 * rows * ff * width * count,
            bytes_accessed=2 * ff * width * count,
            transcendentals=0,
        ),
        name=body.__name__,
    )(me, hidden, down_weight, extra)


def overlapped(activations, norm_gain, gate_weight, up_weight, down_weight):
    rows, width = activations.shape
    index = lax.axis_index("gx").astype(jnp.int32)
    z = index // INNER
    edge = (z == 0) | (z == LINE - 1)
    me = index[None]
    resident = activations.astype(jnp.float32)

    total = jnp.sum(resident * resident, axis=1)
    stats = jnp.stack([jnp.pad(total, (0, width - rows)), norm_gain.astype(jnp.float32)])
    for bit in range(4):
        other = swap(stats, 1 << bit)
        stats = jnp.concatenate([stats[:1] + other[:1], stats[1:], other[1:]])

    neighbour = along(activations, PAIRS)
    inner = along(activations, MIDDLE)
    second_edge = along(inner, OUTWARD)
    second_middle = along(neighbour, MIDDLE)
    third_edge = along(second_middle, OUTWARD)
    slots = [
        activations,
        neighbour,
        jnp.where(edge, second_edge, second_middle),
        jnp.where(edge, third_edge, inner),
    ]
    groups = []
    for slot in slots:
        across = swap(slot, 2)
        groups.append([slot, swap(slot, 1), across, swap(across, 1)])

    order = (0, 1, 2, 3)
    parts = [
        [(k, q) for k in (0,) for q in order],
        [(k, q) for k in (1,) for q in order],
        [(k, q) for k in (2,) for q in order] + [(3, 0), (3, 1)],
        [(3, 2), (3, 3)],
    ]
    acc = None
    for i, part in enumerate(parts):
        codes = tuple(INNER * k + (0, 1, 2, 3)[q] for k, q in part)
        blocks = [groups[k][q] for k, q in part]
        acc = gate_up(
            me, blocks, codes, stats, gate_weight, up_weight, acc, i == len(parts) - 1
        )
    hidden = acc[0]

    def away(k, after):
        return down(
            away_body, me, (INNER * k + 3, INNER * k + 1), hidden, down_weight, width,
            after, pl.BlockSpec(memory_space=pl.ANY),
            jax.ShapeDtypeStruct((2, rows, width), jnp.bfloat16),
            pl.BlockSpec((1, rows, width), lambda s, me: (s, 0, 0)),
        )

    def stay(k, got):
        constant = pl.BlockSpec((rows, width), lambda s, me: (0, 0))
        return down(
            stay_body, me, (INNER * k + 2, INNER * k), hidden, down_weight, width,
            got, pl.BlockSpec((1, rows, width), lambda s, me: (s, 0, 0)),
            [
                jax.ShapeDtypeStruct((rows, width), jnp.bfloat16),
                jax.ShapeDtypeStruct((rows, width), jnp.float32),
            ],
            [constant, constant],
        )

    narrow = lambda x: x.astype(jnp.bfloat16)
    wide = lambda x: x.astype(jnp.float32)

    sums = [None] * LINE
    fars = [None] * LINE
    sent = {LINE - 1: away(LINE - 1, hidden)}
    for k in reversed(range(LINE)):
        if k:
            sent[k - 1] = away(k - 1, fars[k + 1] if k + 1 < LINE else sent[k])
        fars[k], near = stay(k, swap(sent[k], 1))
        sums[k] = near + wide(swap(fars[k], 2))

    middle_two = sums[2] + wide(along(narrow(sums[3]), INWARD))
    middle_three = sums[3] + wide(along(narrow(sums[2]), INWARD))
    one = sums[1] + wide(along(narrow(middle_two), MIDDLE))
    branch = (
        sums[0]
        + wide(along(narrow(one), PAIRS))
        + wide(along(narrow(middle_three), MIDDLE))
    )
    return (resident + branch).astype(jnp.bfloat16)


def plain(activations, norm_gain, gate_weight, up_weight, down_weight):
    resident = activations.astype(jnp.float32)
    totals = lax.psum(jnp.sum(resident * resident, axis=1), "gx")
    factor = lax.rsqrt(totals / (resident.shape[1] * lax.axis_size("gx")) + epsilon)
    normed = (resident * factor[:, None] * norm_gain.astype(jnp.float32)[None, :]).astype(
        jnp.bfloat16
    )
    pieces = lax.all_gather(normed, "gx", axis=1, tiled=True)
    gate_sum = jnp.dot(pieces, gate_weight, preferred_element_type=jnp.float32)
    up_sum = jnp.dot(pieces, up_weight, preferred_element_type=jnp.float32)
    hidden = (jax.nn.silu(gate_sum) * up_sum).astype(jnp.bfloat16)
    summed = lax.psum_scatter(
        lax.dot_general(
            down_weight, hidden, (((0,), (1,)), ((), ())), preferred_element_type=jnp.float32
        ),
        "gx",
        scatter_dimension=0,
        tiled=True,
    )
    return (resident + summed.T).astype(jnp.bfloat16)


def per_device(n, activations, norm_gain, gate_weight, up_weight, down_weight):
    args = (activations, norm_gain, gate_weight, up_weight, down_weight)
    rows, width = activations.shape
    tiled = rows % 128 == 0 and rows <= width == 2 * UNIT and gate_weight.shape[1] % UNIT == 128
    if n == INNER * LINE and tiled:
        return overlapped(*args)
    return plain(*args)


def solution(mesh):
    in_specs = (P("groups", "gx"), P("gx"), P(None, "gx"), P(None, "gx"), P("gx", None))
    out_specs = P("groups", "gx")
    return jax.shard_map(
        functools.partial(per_device, mesh.shape["gx"]),
        mesh=mesh,
        in_specs=in_specs,
        out_specs=out_specs,
        check_vma=False,
    )
```

```python
import functools

import jax
import jax.numpy as jnp
from jax import lax
from jax.experimental import pallas as pl
from jax.experimental.pallas import tpu as pltpu
from jax.sharding import PartitionSpec as P

epsilon = 1e-05
INNER = 4
LINE = 4
EXTRA = 16
VMEM_LIMIT = 30 * 1024 * 1024

PAIRS = ((0, 1), (1, 0), (2, 3), (3, 2))
MIDDLE = ((1, 2), (2, 1))
OUTWARD = ((1, 0), (2, 3))
INWARD = ((0, 1), (3, 2))


def along(x, pairs):
    moves = [(a * INNER + q, b * INNER + q) for a, b in pairs for q in range(INNER)]
    return lax.ppermute(x, "gx", moves)


def prepare_body(x_ref, gain_ref, out_ref):
    rows, width = x_ref.shape
    x = x_ref[...].astype(jnp.float32)
    out_ref[:rows, :] = (x * gain_ref[...].astype(jnp.float32)).astype(jnp.bfloat16)
    squares = jnp.broadcast_to(jnp.sum(x * x, axis=1, keepdims=True), (rows, 128)).T[:EXTRA]
    row = lax.broadcasted_iota(jnp.int32, (EXTRA, rows), 0)
    parts = jnp.zeros((EXTRA, rows), jnp.float32)
    for i in range(3):
        part = squares.astype(jnp.bfloat16).astype(jnp.float32)
        parts = jnp.where(row == i, part, parts)
        squares = squares - part
    out_ref[rows:, :rows] = parts.astype(jnp.bfloat16)
    if rows < width:
        out_ref[rows:, rows:] = jnp.zeros((EXTRA, width - rows), jnp.bfloat16)


def prepare(activations, norm_gain):
    rows, width = activations.shape
    return pl.pallas_call(
        prepare_body,
        out_shape=jax.ShapeDtypeStruct((rows + EXTRA, width), jnp.bfloat16),
        compiler_params=pltpu.CompilerParams(vmem_limit_bytes=VMEM_LIMIT),
        name="prepare",
    )(activations, norm_gain[None, :])


def gate_up_body(first, last, rows, main, features, me_ref, x_ref, gate_ref, up_ref, *rest):
    if not first:
        before = rest[:4]
        rest = rest[4:]
    if last:
        hidden_ref, *rest = rest
    accs = rest
    step = pl.program_id(0)
    x = x_ref[0, :rows, :]
    mixed = jnp.concatenate([gate_ref[:, main:], up_ref[:, main:]], axis=1)
    weights = (gate_ref[:, :main], up_ref[:, :main], mixed)

    def values():
        for weight in weights:
            yield jnp.dot(x, weight, preferred_element_type=jnp.float32)
        squares = x_ref[0, rows:, :].astype(jnp.float32)
        yield jnp.broadcast_to(jnp.sum(squares, axis=0, keepdims=True), accs[3].shape)

    @pl.when(step == 0)
    def _():
        for i, value in enumerate(values()):
            accs[i][...] = value if first else before[i][...] + value

    @pl.when(step > 0)
    def _():
        for i, value in enumerate(values()):
            accs[i][...] += value

    if last:

        @pl.when(step == pl.num_programs(0) - 1)
        def _():
            factor = lax.rsqrt(accs[3][:1, :rows] / features + epsilon)
            factor = jnp.broadcast_to(factor, (128, rows)).T[:, :1]

            def act(g, u):
                g, u = g * factor, u * factor
                return (g / (1.0 + jnp.exp(-g)) * u).astype(jnp.bfloat16)

            rem = mixed.shape[1] // 2
            hidden_ref[:, :main] = act(accs[0][...], accs[1][...])
            hidden_ref[:, main:] = act(accs[2][:, :rem], accs[2][:, rem:])


def gate_up(start, x, gate_weight, up_weight, acc, last):
    count, height, depth = x.shape
    rows = height - EXTRA
    features, ff = gate_weight.shape
    main = ff // 256 * 256 if ff % 256 else ff - 256
    rem = ff - main
    first = acc is None
    whole = lambda shape: pl.BlockSpec(shape, lambda s, me: (0, 0))
    weight = pl.BlockSpec((depth, ff), lambda s, me: (me[0] + s, 0))
    in_specs = [pl.BlockSpec((1, height, depth), lambda s, me: (s, 0, 0)), weight, weight]
    args = [x, gate_weight, up_weight]
    shapes = [(rows, main), (rows, main), (rows, 2 * rem), (8, depth)]
    if not first:
        in_specs += [whole(s) for s in shapes]
        args += list(acc)
    if last:
        out_shape = [jax.ShapeDtypeStruct((rows, ff), jnp.bfloat16)]
        out_specs = [whole((rows, ff))]
        scratch = [pltpu.VMEM(s, jnp.float32) for s in shapes]
    else:
        out_shape = [jax.ShapeDtypeStruct(s, jnp.float32) for s in shapes]
        out_specs = [whole(s) for s in shapes]
        scratch = []
    return pl.pallas_call(
        functools.partial(gate_up_body, first, last, rows, main, features),
        grid_spec=pltpu.PrefetchScalarGridSpec(
            num_scalar_prefetch=1,
            grid=(count,),
            in_specs=in_specs,
            out_specs=out_specs,
            scratch_shapes=scratch,
        ),
        out_shape=out_shape,
        compiler_params=pltpu.CompilerParams(vmem_limit_bytes=VMEM_LIMIT),
        cost_estimate=pl.CostEstimate(
            flops=4 * rows * depth * count * ff,
            bytes_accessed=4 * depth * count * ff,
            transcendentals=0,
        ),
        name="gate_up",
    )(start, *args)


def down_block(hidden_ref, weight_ref):
    ff = hidden_ref.shape[1]
    main = ff // 256 * 256
    value = jnp.dot(
        hidden_ref[:, :main], weight_ref[:main, :], preferred_element_type=jnp.float32
    )
    if main < ff:
        value = value + jnp.dot(
            hidden_ref[:, main:], weight_ref[main:, :], preferred_element_type=jnp.float32
        )
    return value


def down_body(start_ref, hidden_ref, weight_ref, out_ref):
    out_ref[0] = down_block(hidden_ref, weight_ref).astype(out_ref.dtype)


def down(start, hidden, down_weight, width):
    rows, ff = hidden.shape
    return pl.pallas_call(
        down_body,
        grid_spec=pltpu.PrefetchScalarGridSpec(
            num_scalar_prefetch=1,
            grid=(INNER,),
            in_specs=[
                pl.BlockSpec((rows, ff), lambda s, me: (0, 0)),
                pl.BlockSpec((ff, width), lambda s, me: (0, me[0] + s)),
            ],
            out_specs=pl.BlockSpec((1, rows, width), lambda s, me: (s, 0, 0)),
        ),
        out_shape=jax.ShapeDtypeStruct((INNER, rows, width), jnp.bfloat16),
        compiler_params=pltpu.CompilerParams(vmem_limit_bytes=VMEM_LIMIT),
        cost_estimate=pl.CostEstimate(
            flops=2 * rows * ff * width * INNER,
            bytes_accessed=2 * ff * width * INNER,
            transcendentals=0,
        ),
        name="down",
    )(start, hidden, down_weight)


def overlapped(activations, norm_gain, gate_weight, up_weight, down_weight):
    width = activations.shape[1]
    z = lax.axis_index("gx").astype(jnp.int32) // INNER
    edge = (z == 0) | (z == LINE - 1)
    starts = [((z ^ k) * INNER)[None] for k in range(LINE)]
    teams = [[i * INNER + q for q in range(INNER)] for i in range(LINE)]
    resident = activations.astype(jnp.float32)

    shard = prepare(activations, norm_gain)
    neighbour = along(shard, PAIRS)
    inner = along(shard, MIDDLE)
    second_edge = along(inner, OUTWARD)
    second_middle = along(neighbour, MIDDLE)
    third_edge = along(second_middle, OUTWARD)
    slots = [
        shard,
        neighbour,
        jnp.where(edge, second_edge, second_middle),
        jnp.where(edge, third_edge, inner),
    ]
    acc = None
    for k in range(LINE):
        x = lax.all_gather(slots[k], "gx", axis_index_groups=teams)
        acc = gate_up(starts[k], x, gate_weight, up_weight, acc, k == LINE - 1)
    hidden = acc[0]

    narrow = lambda x: x.astype(jnp.bfloat16)
    wide = lambda x: x.astype(jnp.float32)

    sums = [None] * LINE
    for k in reversed(range(LINE)):
        partial = down(starts[k], hidden, down_weight, width)
        sums[k] = lax.psum_scatter(partial, "gx", axis_index_groups=teams)

    middle_two = wide(sums[2]) + wide(along(sums[3], INWARD))
    middle_three = wide(sums[3]) + wide(along(sums[2], INWARD))
    one = wide(sums[1]) + wide(along(narrow(middle_two), MIDDLE))
    branch = (
        wide(sums[0])
        + wide(along(narrow(one), PAIRS))
        + wide(along(narrow(middle_three), MIDDLE))
    )
    return (resident + branch).astype(jnp.bfloat16)


def plain(activations, norm_gain, gate_weight, up_weight, down_weight):
    resident = activations.astype(jnp.float32)
    totals = lax.psum(jnp.sum(resident * resident, axis=1), "gx")
    factor = lax.rsqrt(totals / (resident.shape[1] * lax.axis_size("gx")) + epsilon)
    normed = (resident * factor[:, None] * norm_gain.astype(jnp.float32)[None, :]).astype(
        jnp.bfloat16
    )
    pieces = lax.all_gather(normed, "gx", axis=1, tiled=True)
    gate_sum = jnp.dot(pieces, gate_weight, preferred_element_type=jnp.float32)
    up_sum = jnp.dot(pieces, up_weight, preferred_element_type=jnp.float32)
    hidden = (jax.nn.silu(gate_sum) * up_sum).astype(jnp.bfloat16)
    summed = lax.psum_scatter(
        lax.dot_general(
            down_weight, hidden, (((0,), (1,)), ((), ())), preferred_element_type=jnp.float32
        ),
        "gx",
        scatter_dimension=0,
        tiled=True,
    )
    return (resident + summed.T).astype(jnp.bfloat16)


def per_device(n, activations, norm_gain, gate_weight, up_weight, down_weight):
    args = (activations, norm_gain, gate_weight, up_weight, down_weight)
    rows, width = activations.shape
    tiled = rows % 128 == 0 and width % 128 == 0 and gate_weight.shape[1] % 128 == 0
    tiled = tiled and rows <= width
    if n == INNER * LINE and tiled:
        return overlapped(*args)
    return plain(*args)


def solution(mesh):
    in_specs = (P("groups", "gx"), P("gx"), P(None, "gx"), P(None, "gx"), P("gx", None))
    out_specs = P("groups", "gx")
    return jax.shard_map(
        functools.partial(per_device, mesh.shape["gx"]),
        mesh=mesh,
        in_specs=in_specs,
        out_specs=out_specs,
        check_vma=False,
    )
```

```python
import functools

import jax
import jax.numpy as jnp
from jax import lax
from jax.experimental import pallas as pl
from jax.experimental.pallas import tpu as pltpu
from jax.sharding import PartitionSpec as P

epsilon = 1e-05
INNER = 4
LINE = 4
EXTRA = 16
VMEM_LIMIT = 30 * 1024 * 1024

PAIRS = ((0, 1), (1, 0), (2, 3), (3, 2))
MIDDLE = ((1, 2), (2, 1))
OUTWARD = ((1, 0), (2, 3))
INWARD = ((0, 1), (3, 2))


def swap(x, mask):
    return lax.ppermute(x, "gx", [(i, i ^ mask) for i in range(INNER * LINE)])


def along(x, pairs):
    moves = [(a * INNER + q, b * INNER + q) for a, b in pairs for q in range(INNER)]
    return lax.ppermute(x, "gx", moves)


def pick(table, s):
    value = jnp.int32(table[0])
    for i, entry in enumerate(table[1:], 1):
        value = jnp.where(s == i, jnp.int32(entry), value)
    return value


def prepare_body(x_ref, gain_ref, out_ref):
    rows, width = x_ref.shape
    x = x_ref[...].astype(jnp.float32)
    gain = gain_ref[...].astype(jnp.float32).reshape(1, width)
    out_ref[:rows, :] = (x * gain).astype(jnp.bfloat16)
    squares = jnp.broadcast_to(jnp.sum(x * x, axis=1, keepdims=True), (rows, 128)).T[:EXTRA]
    row = lax.broadcasted_iota(jnp.int32, (EXTRA, rows), 0)
    parts = jnp.zeros((EXTRA, rows), jnp.float32)
    for i in range(3):
        part = squares.astype(jnp.bfloat16).astype(jnp.float32)
        parts = jnp.where(row == i, part, parts)
        squares = squares - part
    out_ref[rows:, :rows] = parts.astype(jnp.bfloat16)
    if rows < width:
        out_ref[rows:, rows:] = jnp.zeros((EXTRA, width - rows), jnp.bfloat16)


def prepare(activations, norm_gain):
    rows, width = activations.shape
    return pl.pallas_call(
        prepare_body,
        out_shape=jax.ShapeDtypeStruct((rows + EXTRA, width), jnp.bfloat16),
        compiler_params=pltpu.CompilerParams(vmem_limit_bytes=VMEM_LIMIT),
        name="prepare",
    )(activations, norm_gain)


def gate_up_body(codes, first, last, rows, main, features, me_ref, *refs):
    count = len(codes)
    blocks = refs[:count]
    gate_ref, up_ref, *rest = refs[count:]
    if not first:
        before = rest[:4]
        rest = rest[4:]
    if last:
        hidden_ref, *rest = rest
    accs = rest
    step = pl.program_id(0)

    for s in range(count):

        @pl.when(step == s)
        def _(s=s):
            x = blocks[s][:rows, :]
            gate, up = gate_ref[...], up_ref[...]
            mixed = jnp.concatenate([gate[:, main:], up[:, main:]], axis=1)
            values = [
                jnp.dot(x, weight, preferred_element_type=jnp.float32)
                for weight in (gate[:, :main], up[:, :main], mixed)
            ]
            squares = blocks[s][rows:, :].astype(jnp.float32)
            squares = jnp.sum(squares, axis=0, keepdims=True)
            values.append(jnp.broadcast_to(squares, accs[3].shape))
            if s:
                values = [acc[...] + value for acc, value in zip(accs, values)]
            elif not first:
                values = [old[...] + value for old, value in zip(before, values)]
            if not last or s < count - 1:
                for acc, value in zip(accs, values):
                    acc[...] = value
                return
            factor = lax.rsqrt(values[3][:1, :rows] / features + epsilon)
            factor = jnp.broadcast_to(factor, (128, rows)).T[:, :1]

            def act(g, u):
                g, u = g * factor, u * factor
                return (g / (1.0 + jnp.exp(-g)) * u).astype(jnp.bfloat16)

            gate, up, both, _ = values
            rem = both.shape[1] // 2
            hidden_ref[:, :main] = act(gate, up)
            hidden_ref[:, main:] = act(both[:, :rem], both[:, rem:])


def gate_up(me, blocks, codes, gate_weight, up_weight, acc, last):
    height, depth = blocks[0].shape
    count = len(blocks)
    rows = height - EXTRA
    features, ff = gate_weight.shape
    main = ff // 256 * 256 if ff % 256 else ff - 256
    rem = ff - main
    first = acc is None
    whole = lambda shape: pl.BlockSpec(shape, lambda s, me: (0, 0))
    weight = pl.BlockSpec((depth, ff), lambda s, me: (me[0] ^ pick(codes, s), 0))
    in_specs = [whole(b.shape) for b in blocks] + [weight, weight]
    args = [*blocks, gate_weight, up_weight]
    shapes = [(rows, main), (rows, main), (rows, 2 * rem), (8, depth)]
    if not first:
        in_specs += [whole(s) for s in shapes]
        args += list(acc)
    if last:
        out_shape = [jax.ShapeDtypeStruct((rows, ff), jnp.bfloat16)]
        out_specs = [whole((rows, ff))]
        scratch = [pltpu.VMEM(s, jnp.float32) for s in shapes]
    else:
        out_shape = [jax.ShapeDtypeStruct(s, jnp.float32) for s in shapes]
        out_specs = [whole(s) for s in shapes]
        scratch = []
    return pl.pallas_call(
        functools.partial(gate_up_body, codes, first, last, rows, main, features),
        grid_spec=pltpu.PrefetchScalarGridSpec(
            num_scalar_prefetch=1,
            grid=(count,),
            in_specs=in_specs,
            out_specs=out_specs,
            scratch_shapes=scratch,
        ),
        out_shape=out_shape,
        compiler_params=pltpu.CompilerParams(vmem_limit_bytes=VMEM_LIMIT),
        cost_estimate=pl.CostEstimate(
            flops=4 * rows * depth * count * ff // 8,
            bytes_accessed=4 * depth * count * ff // 8,
            transcendentals=0,
        ),
        name="gate_up",
    )(me, *args)


def down_block(hidden_ref, weight_ref):
    ff = hidden_ref.shape[1]
    main = ff // 256 * 256
    value = jnp.dot(
        hidden_ref[:, :main], weight_ref[:main, :], preferred_element_type=jnp.float32
    )
    if main < ff:
        value = value + jnp.dot(
            hidden_ref[:, main:], weight_ref[main:, :], preferred_element_type=jnp.float32
        )
    return value


def down_body(jobs, me_ref, hidden_ref, weight_ref, *refs):
    outs = dict(zip(dict.fromkeys(kind for _, kind in jobs), refs[-len({kind for _, kind in jobs}) :]))
    step = pl.program_id(0)
    value = down_block(hidden_ref, weight_ref)
    place = 0
    for s, (_, kind) in enumerate(jobs):

        @pl.when(step == s)
        def _(s=s, kind=kind, place=place):
            if kind == "sent":
                outs[kind][place] = value.astype(jnp.bfloat16)
            elif kind == "far":
                outs[kind][...] = (value + refs[0][0].astype(jnp.float32)).astype(jnp.bfloat16)
            else:
                outs[kind][...] = value + refs[0][1].astype(jnp.float32)

        place += kind == "sent"


def down(me, jobs, hidden, down_weight, width, got):
    rows, ff = hidden.shape
    codes = [code for code, _ in jobs]
    whole = lambda shape: pl.BlockSpec(shape, lambda s, me: (0,) * len(shape))
    kinds = [kind for _, kind in jobs]
    shapes = {
        "far": ((rows, width), jnp.bfloat16),
        "near": ((rows, width), jnp.float32),
        "sent": ((kinds.count("sent"), rows, width), jnp.bfloat16),
    }
    shapes = [shapes[kind] for kind in dict.fromkeys(kinds)]
    extra = [] if got is None else [got]
    return pl.pallas_call(
        functools.partial(down_body, jobs),
        grid_spec=pltpu.PrefetchScalarGridSpec(
            num_scalar_prefetch=1,
            grid=(len(jobs),),
            in_specs=[
                whole(hidden.shape),
                pl.BlockSpec((ff, width), lambda s, me: (0, me[0] ^ pick(codes, s))),
            ]
            + [whole(x.shape) for x in extra],
            out_specs=[whole(shape) for shape, _ in shapes],
        ),
        out_shape=[jax.ShapeDtypeStruct(*shape) for shape in shapes],
        compiler_params=pltpu.CompilerParams(vmem_limit_bytes=VMEM_LIMIT),
        cost_estimate=pl.CostEstimate(
            flops=2 * rows * ff * width * len(jobs) // 8,
            bytes_accessed=2 * ff * width * len(jobs) // 8,
            transcendentals=0,
        ),
        name="down",
    )(me, hidden, down_weight, *extra)


def after(x, *others):
    return lax.optimization_barrier((x, *others))[0]


def overlapped(activations, norm_gain, gate_weight, up_weight, down_weight):
    width = activations.shape[1]
    index = lax.axis_index("gx").astype(jnp.int32)
    me = index[None]
    z = index // INNER
    edge = (z == 0) | (z == LINE - 1)
    resident = activations.astype(jnp.float32)

    def multiply(acc, *blocks):
        x, codes = zip(*blocks)
        return gate_up(me, x, codes, gate_weight, up_weight, acc, len(blocks) == 2 and codes[0] == 14)

    own = prepare(activations, norm_gain)
    one = along(own, PAIRS)
    inner = along(own, MIDDLE)
    own_y = swap(own, 2)
    own_c = swap(own, 1)
    acc = multiply(None, (own, 0), (own_c, 1))
    one, inner = after((one, inner), acc[0])
    two_edge = along(inner, OUTWARD)
    two_middle = along(one, MIDDLE)
    one_y = swap(one, 2)
    one_c = swap(one, 1)
    own_yc = swap(own_y, 1)
    acc = multiply(acc, (own_y, 2), (own_yc, 3), (one, 4), (one_c, 5))
    two_edge, two_middle = after((two_edge, two_middle), acc[0])
    two = jnp.where(edge, two_edge, two_middle)
    three_edge = along(two_middle, OUTWARD)
    two_y = swap(two, 2)
    two_c = swap(two, 1)
    one_yc = swap(one_y, 1)
    acc = multiply(acc, (one_y, 6), (one_yc, 7), (two, 8), (two_c, 9))
    three_edge = after(three_edge, acc[0])
    three = jnp.where(edge, three_edge, inner)
    three_y = swap(three, 2)
    three_c = swap(three, 1)
    two_yc = swap(two_y, 1)
    acc = multiply(acc, (two_y, 10), (two_yc, 11), (three, 12), (three_c, 13))
    three_y = after(three_y, acc[0])
    hidden = multiply(acc, (three_y, 14), (swap(three_y, 1), 15))[0]

    narrow = lambda x: x.astype(jnp.bfloat16)
    wide = lambda x: x.astype(jnp.float32)

    def blocks(hidden, stay, away, got=None):
        jobs = []
        if stay is not None:
            jobs += [(INNER * stay + 2, "far"), (INNER * stay, "near")]
        for k in away:
            jobs += [(INNER * k + 3, "sent"), (INNER * k + 1, "sent")]
        return down(me, jobs, hidden, down_weight, width, got)

    sent = blocks(hidden, None, (3, 2))[0]
    got_three, got_two = swap(sent[:2], 1), swap(sent[2:], 1)
    far, near_three = blocks(hidden, 3, (), got_three)
    far_three = swap(far, 2)
    far, near_two, sent = blocks(after(hidden, far), 2, (1,), got_two)
    got_one = swap(sent, 1)
    far_two = swap(far, 2)
    three = near_three + wide(far_three)
    three_sent = along(narrow(three), INWARD)
    far, near_one, sent = blocks(after(hidden, far), 1, (0,), got_one)
    got_own = swap(sent, 1)
    far_one = swap(far, 2)
    two = near_two + wide(far_two)
    two_sent = along(narrow(two), INWARD)
    two = two + wide(three_sent)
    two_passed = along(narrow(two), MIDDLE)
    far, near_own = blocks(after(hidden, far), 0, (), got_own)
    far_own = swap(far, 2)
    one = near_one + wide(after(far_one, far)) + wide(two_passed)
    three = three + wide(after(two_sent, far))
    branch = (
        near_own
        + wide(far_own)
        + wide(along(narrow(one), PAIRS))
        + wide(along(narrow(three), MIDDLE))
    )
    return (resident + branch).astype(jnp.bfloat16)


def plain(activations, norm_gain, gate_weight, up_weight, down_weight):
    resident = activations.astype(jnp.float32)
    totals = lax.psum(jnp.sum(resident * resident, axis=1), "gx")
    factor = lax.rsqrt(totals / (resident.shape[1] * lax.axis_size("gx")) + epsilon)
    normed = (resident * factor[:, None] * norm_gain.astype(jnp.float32)[None, :]).astype(
        jnp.bfloat16
    )
    pieces = lax.all_gather(normed, "gx", axis=1, tiled=True)
    gate_sum = jnp.dot(pieces, gate_weight, preferred_element_type=jnp.float32)
    up_sum = jnp.dot(pieces, up_weight, preferred_element_type=jnp.float32)
    hidden = (jax.nn.silu(gate_sum) * up_sum).astype(jnp.bfloat16)
    summed = lax.psum_scatter(
        lax.dot_general(
            down_weight, hidden, (((0,), (1,)), ((), ())), preferred_element_type=jnp.float32
        ),
        "gx",
        scatter_dimension=0,
        tiled=True,
    )
    return (resident + summed.T).astype(jnp.bfloat16)


def per_device(n, activations, norm_gain, gate_weight, up_weight, down_weight):
    args = (activations, norm_gain, gate_weight, up_weight, down_weight)
    rows, width = activations.shape
    tiled = rows % 128 == 0 and width % 128 == 0 and gate_weight.shape[1] % 128 == 0
    tiled = tiled and rows <= width
    if n == INNER * LINE and tiled:
        return overlapped(*args)
    return plain(*args)


def solution(mesh):
    in_specs = (P("groups", "gx"), P("gx"), P(None, "gx"), P(None, "gx"), P("gx", None))
    out_specs = P("groups", "gx")
    return jax.shard_map(
        functools.partial(per_device, mesh.shape["gx"]),
        mesh=mesh,
        in_specs=in_specs,
        out_specs=out_specs,
        check_vma=False,
    )
```

```python
import functools

import jax
import jax.numpy as jnp
import numpy as np
from jax import lax
from jax.experimental import pallas as pl
from jax.experimental.pallas import tpu as pltpu
from jax.sharding import PartitionSpec as P

epsilon = 1e-05
LINE = 4
EXTRA = 16
VMEM_LIMIT = 24 * 1024 * 1024

TAKEN = {
    (True, 0): (0, 2, 3, 6, 7),
    (True, 1): (0, 1, 4, 5, 7),
    (False, 0): (0, 2, 4, 1, 5),
    (False, 1): (0, 6, 3, 7, 5),
}


def device(z, y, core):
    return z * 4 + y * 2 + core


def step(number):
    moves = []
    for z in range(LINE):
        for y in range(2):
            along = (z ^ 1, y)
            across = (z, y ^ 1)
            inside = (z ^ 3, y) if 0 < z < LINE - 1 else across
            goals = {
                1: (along, inside),
                2: (inside, along),
                3: (along, across),
                4: (across,),
            }[number]
            moves += [(device(z, y, c), device(*goal, c)) for c, goal in enumerate(goals)]
    return moves


def send(x, number):
    return lax.ppermute(x, "gx", step(number))


def swap(x):
    return lax.ppermute(x, "gx", [(i, i ^ 1) for i in range(4 * LINE)])


def after(x, *others):
    return lax.optimization_barrier((x, *others))[0]


def prepare_body(x_ref, gain_ref, out_ref):
    rows, width = x_ref.shape
    x = x_ref[...].astype(jnp.float32)
    gain = gain_ref[...].astype(jnp.float32).reshape(1, width)
    out_ref[:rows, :] = (x * gain).astype(jnp.bfloat16)
    squares = jnp.broadcast_to(jnp.sum(x * x, axis=1, keepdims=True), (rows, 128)).T[:EXTRA]
    row = lax.broadcasted_iota(jnp.int32, (EXTRA, rows), 0)
    parts = jnp.zeros((EXTRA, rows), jnp.float32)
    for i in range(3):
        part = squares.astype(jnp.bfloat16).astype(jnp.float32)
        parts = jnp.where(row == i, part, parts)
        squares = squares - part
    out_ref[rows:, :rows] = parts.astype(jnp.bfloat16)
    if rows < width:
        out_ref[rows:, rows:] = jnp.zeros((EXTRA, width - rows), jnp.bfloat16)


def prepare(activations, norm_gain):
    rows, width = activations.shape
    return pl.pallas_call(
        prepare_body,
        out_shape=jax.ShapeDtypeStruct((rows + EXTRA, width), jnp.bfloat16),
        compiler_params=pltpu.CompilerParams(vmem_limit_bytes=VMEM_LIMIT),
        name="prepare",
    )(activations, norm_gain)


def gate_up_body(count, first, last, rows, main, features, order_ref, *refs):
    pairs = refs[:count]
    gate_ref, up_ref, *rest = refs[count:]
    if not first:
        before = rest[:4]
        rest = rest[4:]
    if last:
        hidden_ref, *rest = rest
    accs = rest
    now = pl.program_id(0)

    def products(x_ref):
        x = x_ref[0, :rows, :]
        gate, up = gate_ref[...], up_ref[...]
        mixed = jnp.concatenate([gate[:, main:], up[:, main:]], axis=1)
        values = [
            jnp.dot(x, weight, preferred_element_type=jnp.float32)
            for weight in (gate[:, :main], up[:, :main], mixed)
        ]
        squares = jnp.sum(x_ref[0, rows:, :].astype(jnp.float32), axis=0, keepdims=True)
        return values + [jnp.broadcast_to(squares, accs[3].shape)]

    for p, x_ref in enumerate(pairs):
        if not p:

            @pl.when(now == 0)
            def _():
                for i, value in enumerate(products(pairs[0])):
                    accs[i][...] = value if first else before[i][...] + value

        @pl.when((now >= max(2 * p, 1)) & (now < 2 * p + 2))
        def _(x_ref=x_ref):
            for acc, value in zip(accs, products(x_ref)):
                acc[...] += value

    if last:

        @pl.when(now == 2 * count - 1)
        def _():
            factor = lax.rsqrt(accs[3][:1, :rows] / features + epsilon)
            factor = jnp.broadcast_to(factor, (128, rows)).T[:, :1]

            def act(g, u):
                g, u = g * factor, u * factor
                return (g / (1.0 + jnp.exp(-g)) * u).astype(jnp.bfloat16)

            rem = accs[2].shape[1] // 2
            hidden_ref[:, :main] = act(accs[0][...], accs[1][...])
            hidden_ref[:, main:] = act(accs[2][:, :rem], accs[2][:, rem:])


def gate_up(order, places, pairs, gate_weight, up_weight, acc, last=False):
    height, depth = pairs[0].shape[1:]
    count = len(pairs)
    rows = height - EXTRA
    features, ff = gate_weight.shape
    main = ff // 256 * 256 if ff % 256 else ff - 256
    rem = ff - main
    first = acc is None
    whole = lambda shape: pl.BlockSpec(shape, lambda s, order: (0, 0))

    def shard(p):
        return pl.BlockSpec(
            (1, height, depth), lambda s, order: (jnp.clip(s - 2 * p, 0, 1), 0, 0)
        )

    def rows_of(s, order):
        place = jnp.int32(places[0])
        for p in range(1, count):
            place = jnp.where(s >= 2 * p, jnp.int32(places[p]), place)
        return (order[place] * 2 + s % 2, 0)

    weight = pl.BlockSpec((depth, ff), rows_of)
    in_specs = [shard(p) for p in range(count)] + [weight, weight]
    args = [*pairs, gate_weight, up_weight]
    shapes = [(rows, main), (rows, main), (rows, 2 * rem), (8, depth)]
    aliases = {}
    if not first:
        if not last:
            aliases = {1 + len(args) + i: i for i in range(4)}
        in_specs += [whole(s) for s in shapes]
        args += list(acc)
    if last:
        out_shape = [jax.ShapeDtypeStruct((rows, ff), jnp.bfloat16)]
        out_specs = [whole((rows, ff))]
        scratch = [pltpu.VMEM(s, jnp.float32) for s in shapes]
    else:
        out_shape = [jax.ShapeDtypeStruct(s, jnp.float32) for s in shapes]
        out_specs = [whole(s) for s in shapes]
        scratch = []
    return pl.pallas_call(
        functools.partial(gate_up_body, count, first, last, rows, main, features),
        grid_spec=pltpu.PrefetchScalarGridSpec(
            num_scalar_prefetch=1,
            grid=(2 * count,),
            in_specs=in_specs,
            out_specs=out_specs,
            scratch_shapes=scratch,
        ),
        out_shape=out_shape,
        input_output_aliases=aliases,
        compiler_params=pltpu.CompilerParams(vmem_limit_bytes=VMEM_LIMIT),
        cost_estimate=pl.CostEstimate(
            flops=rows * depth * count * ff,
            bytes_accessed=depth * count * ff,
            transcendentals=0,
        ),
        name="gate_up",
    )(order, *args)


def down_block(hidden_ref, weight_ref):
    ff = hidden_ref.shape[1]
    main = ff // 256 * 256
    value = jnp.dot(
        hidden_ref[:, :main], weight_ref[:main, :], preferred_element_type=jnp.float32
    )
    if main < ff:
        value = value + jnp.dot(
            hidden_ref[:, main:], weight_ref[main:, :], preferred_element_type=jnp.float32
        )
    return value


def down_body(kinds, order_ref, hidden_ref, weight_ref, *outs):
    now = pl.program_id(0)
    value = down_block(hidden_ref, weight_ref)
    for p, kind in enumerate(kinds):

        if kind == "kept":

            @pl.when(now // 2 == p)
            def _(kept=outs[p]):
                kept[now % 2] = value

        else:
            for half in range(2):

                @pl.when(now == 2 * p + half)
                def _(sent=outs[p + half]):
                    sent[...] = value.astype(sent.dtype)


def down(order, places, hidden, down_weight, width):
    rows, ff = hidden.shape
    count = len(places)
    specs = {
        "kept": [pl.BlockSpec((2, rows, width), lambda s, order: (0, 0, 0))],
        "sent": [pl.BlockSpec((rows, width), lambda s, order: (0, 0))] * 2,
    }
    specs = [(spec, kind) for kind in places for spec in specs[kind]]
    dtypes = {"sent": jnp.bfloat16, "kept": jnp.float32}

    def columns_of(s, order):
        place = jnp.int32(list(places.values())[0])
        for p, other in enumerate(places.values()):
            place = jnp.where(s >= 2 * p, jnp.int32(other), place)
        return (0, order[place] * 2 + s % 2)

    return pl.pallas_call(
        functools.partial(down_body, tuple(places)),
        grid_spec=pltpu.PrefetchScalarGridSpec(
            num_scalar_prefetch=1,
            grid=(2 * count,),
            in_specs=[
                pl.BlockSpec((rows, ff), lambda s, order: (0, 0)),
                pl.BlockSpec((ff, width), columns_of),
            ],
            out_specs=[spec for spec, _ in specs],
        ),
        out_shape=[
            jax.ShapeDtypeStruct(spec.block_shape, dtypes[kind]) for spec, kind in specs
        ],
        compiler_params=pltpu.CompilerParams(vmem_limit_bytes=VMEM_LIMIT),
        cost_estimate=pl.CostEstimate(
            flops=rows * ff * width * count // 4,
            bytes_accessed=ff * width * count // 4,
            transcendentals=0,
        ),
        name="down",
    )(order, hidden, down_weight)


def overlapped(activations, norm_gain, gate_weight, up_weight, down_weight):
    width = activations.shape[1]
    index = lax.axis_index("gx").astype(jnp.int32)
    core = index & 1
    z = index >> 2
    end = (z == 0) | (z == LINE - 1)
    middle_one = ~end & (core == 1)
    resident = activations.astype(jnp.float32)
    narrow = lambda x: x.astype(jnp.bfloat16)
    wide = lambda x: x.astype(jnp.float32)

    mine = [TAKEN[e, c] for e in (True, False) for c in (0, 1)]
    others = [TAKEN[e, 1 - c] for e in (True, False) for c in (0, 1)]
    codes = np.array(
        [(0, m[1], o[1], m[2], o[2], m[3], o[3], m[4]) for m, o in zip(mine, others)], np.int32
    )
    OWN, MINE, OTHER, LAST = 0, (None, 1, 3, 5), (None, 2, 4, 6), 7
    variant = jnp.where(end, 0, 2) + core
    order = (index >> 1) ^ lax.dynamic_slice(jnp.asarray(codes), (variant, 0), (1, 8))[0]

    multiply = functools.partial(gate_up, order)
    shard = prepare(activations, norm_gain)
    partner = swap(shard)
    own = jnp.stack([jnp.where(core == 0, shard, partner), jnp.where(core == 0, partner, shard)])
    one = send(own, 1)
    acc = multiply((OWN,), (own,), gate_weight, up_weight, None)
    one = after(one, acc[0])
    two = send(one, 2)
    one_other = swap(one)
    acc = multiply((MINE[1],), (one,), gate_weight, up_weight, acc)
    two = after(two, acc[0])
    three = send(jnp.where(middle_one, one, two), 3)
    two_other = swap(two)
    acc = multiply((OTHER[1], MINE[2]), (one_other, two), gate_weight, up_weight, acc)
    three = after(three, acc[0])
    four = send(jnp.where(end, three, two), 4)
    three_other = swap(three)
    acc = multiply((OTHER[2], MINE[3]), (two_other, three), gate_weight, up_weight, acc)
    four = after(four, acc[0])
    four_other = swap(four)
    acc = multiply((OTHER[3],), (three_other,), gate_weight, up_weight, acc)
    four = jnp.where(core == 0, four, after(four_other, acc[0]))
    hidden = multiply((LAST,), (four,), gate_weight, up_weight, acc, last=True)[0]

    def partial(hidden, place):
        places = {"kept": MINE[place], "sent": OTHER[place]}
        kept, *sent = down(order, places, hidden, down_weight, width)
        return kept, sent

    def add(kept, sent, *more):
        halves = [kept[i] + wide(swap(sent[i])) for i in range(2)]
        for x in more:
            halves = [half + x[i] for i, half in enumerate(halves)]
        return jnp.stack([narrow(half) for half in halves])

    zero = jnp.zeros((), jnp.float32)
    (kept,) = down(order, {"kept": LAST}, hidden, down_weight, width)
    total = add(kept, [narrow(kept[0]), narrow(kept[1])])
    four = wide(send(total, 4))
    kept, sent = partial(after(hidden, total), 3)
    total = add(kept, sent, jnp.where(end, four, zero))
    three = wide(send(total, 3))
    kept, sent = partial(after(hidden, total), 2)
    total = add(
        kept, sent, jnp.where(end, zero, four), jnp.where(middle_one, zero, three)
    )
    two = wide(send(total, 2))
    kept, sent = partial(after(hidden, total), 1)
    total = add(kept, sent, two, jnp.where(middle_one, three, zero))
    one = wide(send(total, 1))
    (kept,) = down(order, {"kept": OWN}, after(hidden, total), down_weight, width)
    total = kept + one
    first, second = total[0], total[1]
    got = swap(narrow(jnp.where(core == 0, second, first)))
    branch = jnp.where(core == 0, first, second) + wide(got)
    return (resident + branch).astype(jnp.bfloat16)


def plain(activations, norm_gain, gate_weight, up_weight, down_weight):
    resident = activations.astype(jnp.float32)
    totals = lax.psum(jnp.sum(resident * resident, axis=1), "gx")
    factor = lax.rsqrt(totals / (resident.shape[1] * lax.axis_size("gx")) + epsilon)
    normed = (resident * factor[:, None] * norm_gain.astype(jnp.float32)[None, :]).astype(
        jnp.bfloat16
    )
    pieces = lax.all_gather(normed, "gx", axis=1, tiled=True)
    gate_sum = jnp.dot(pieces, gate_weight, preferred_element_type=jnp.float32)
    up_sum = jnp.dot(pieces, up_weight, preferred_element_type=jnp.float32)
    hidden = (jax.nn.silu(gate_sum) * up_sum).astype(jnp.bfloat16)
    summed = lax.psum_scatter(
        lax.dot_general(
            down_weight, hidden, (((0,), (1,)), ((), ())), preferred_element_type=jnp.float32
        ),
        "gx",
        scatter_dimension=0,
        tiled=True,
    )
    return (resident + summed.T).astype(jnp.bfloat16)


def per_device(n, activations, norm_gain, gate_weight, up_weight, down_weight):
    args = (activations, norm_gain, gate_weight, up_weight, down_weight)
    rows, width = activations.shape
    tiled = rows % 128 == 0 and width % 128 == 0 and gate_weight.shape[1] % 128 == 0
    tiled = tiled and rows <= width
    if n == 4 * LINE and tiled:
        return overlapped(*args)
    return plain(*args)


def solution(mesh):
    in_specs = (P("groups", "gx"), P("gx"), P(None, "gx"), P(None, "gx"), P("gx", None))
    out_specs = P("groups", "gx")
    return jax.shard_map(
        functools.partial(per_device, mesh.shape["gx"]),
        mesh=mesh,
        in_specs=in_specs,
        out_specs=out_specs,
        check_vma=False,
    )
```

```python
import functools

import jax
import jax.numpy as jnp
import numpy as np
from jax import lax
from jax.experimental import pallas as pl
from jax.experimental.pallas import tpu as pltpu
from jax.sharding import PartitionSpec as P

epsilon = 1e-05
LINE = 4
EXTRA = 16
VMEM_LIMIT = 36 * 1024 * 1024

ALONG = (lambda z, y: (z ^ 1, y),) * 2
INSIDE = (lambda z, y: (z, y ^ 1), lambda z, y: (z ^ 3, y))
ACROSS = (lambda z, y: (z, y ^ 1),) * 2

TAKEN = np.array([(0, 2, 1, 4, 3, 6, 5, 7), (0, 2, 6, 3, 4, 1, 7, 5)], np.int32)


def send(x, move):
    pairs = []
    for z in range(LINE):
        for y in range(2):
            to_z, to_y = move[0 < z < LINE - 1](z, y)
            pairs += [(z * 4 + y * 2 + c, to_z * 4 + to_y * 2 + c) for c in range(2)]
    return lax.ppermute(x, "gx", pairs)


def swap(x):
    return lax.ppermute(x, "gx", [(i, i ^ 1) for i in range(4 * LINE)])


def after(x, *others):
    return lax.optimization_barrier((x, *others))[0]


def pick(table, s):
    value = jnp.int32(table[0])
    for i, entry in enumerate(table[1:], 1):
        value = jnp.where(s == i, jnp.int32(entry), value)
    return value


def prepare_body(x_ref, gain_ref, out_ref):
    rows, width = x_ref.shape
    x = x_ref[...].astype(jnp.float32)
    gain = gain_ref[...].astype(jnp.float32).reshape(1, width)
    out_ref[:rows, :] = (x * gain).astype(jnp.bfloat16)
    squares = jnp.broadcast_to(jnp.sum(x * x, axis=1, keepdims=True), (rows, 128)).T[:EXTRA]
    row = lax.broadcasted_iota(jnp.int32, (EXTRA, rows), 0)
    parts = jnp.zeros((EXTRA, rows), jnp.float32)
    for i in range(3):
        part = squares.astype(jnp.bfloat16).astype(jnp.float32)
        parts = jnp.where(row == i, part, parts)
        squares = squares - part
    out_ref[rows:, :rows] = parts.astype(jnp.bfloat16)
    if rows < width:
        out_ref[rows:, rows:] = jnp.zeros((EXTRA, width - rows), jnp.bfloat16)


def prepare(activations, norm_gain):
    rows, width = activations.shape
    return pl.pallas_call(
        prepare_body,
        out_shape=jax.ShapeDtypeStruct((rows + EXTRA, width), jnp.bfloat16),
        compiler_params=pltpu.CompilerParams(vmem_limit_bytes=VMEM_LIMIT),
        name="prepare",
    )(activations, norm_gain)


def gate_up_body(count, first, last, rows, main, features, order_ref, *refs):
    blocks = refs[:count]
    gate_ref, up_ref, *rest = refs[count:]
    if not first:
        before = rest[:4]
        rest = rest[4:]
    if last:
        hidden_ref, *rest = rest
    accs = rest
    step = pl.program_id(0)

    for s in range(count):

        @pl.when(step == s)
        def _(s=s):
            x = blocks[s][:rows, :]
            gate, up = gate_ref[...], up_ref[...]
            mixed = jnp.concatenate([gate[:, main:], up[:, main:]], axis=1)
            values = [
                jnp.dot(x, weight, preferred_element_type=jnp.float32)
                for weight in (gate[:, :main], up[:, :main], mixed)
            ]
            squares = blocks[s][rows:, :].astype(jnp.float32)
            squares = jnp.sum(squares, axis=0, keepdims=True)
            values.append(jnp.broadcast_to(squares, accs[3].shape))
            if s:
                values = [acc[...] + value for acc, value in zip(accs, values)]
            elif not first:
                values = [old[...] + value for old, value in zip(before, values)]
            if not last or s < count - 1:
                for acc, value in zip(accs, values):
                    acc[...] = value
                return
            factor = lax.rsqrt(values[3][:1, :rows] / features + epsilon)
            factor = jnp.broadcast_to(factor, (128, rows)).T[:, :1]

            def act(g, u):
                g, u = g * factor, u * factor
                return (g / (1.0 + jnp.exp(-g)) * u).astype(jnp.bfloat16)

            gate, up, both, _ = values
            rem = both.shape[1] // 2
            hidden_ref[:, :main] = act(gate, up)
            hidden_ref[:, main:] = act(both[:, :rem], both[:, rem:])


def gate_up(order, places, blocks, gate_weight, up_weight, acc, last=False):
    height, depth = blocks[0].shape
    count = len(blocks)
    rows = height - EXTRA
    features, ff = gate_weight.shape
    main = ff // 256 * 256 if ff % 256 else ff - 256
    rem = ff - main
    first = acc is None
    whole = lambda shape: pl.BlockSpec(shape, lambda s, order: (0, 0))
    weight = pl.BlockSpec((depth, ff), lambda s, order: (order[pick(places, s)], 0))
    in_specs = [whole(b.shape) for b in blocks] + [weight, weight]
    args = [*blocks, gate_weight, up_weight]
    shapes = [(rows, main), (rows, main), (rows, 2 * rem), (8, depth)]
    if not first:
        in_specs += [whole(s) for s in shapes]
        args += list(acc)
    if last:
        out_shape = [jax.ShapeDtypeStruct((rows, ff), jnp.bfloat16)]
        out_specs = [whole((rows, ff))]
        scratch = [pltpu.VMEM(s, jnp.float32) for s in shapes]
    else:
        out_shape = [jax.ShapeDtypeStruct(s, jnp.float32) for s in shapes]
        out_specs = [whole(s) for s in shapes]
        scratch = []
    return pl.pallas_call(
        functools.partial(gate_up_body, count, first, last, rows, main, features),
        grid_spec=pltpu.PrefetchScalarGridSpec(
            num_scalar_prefetch=1,
            grid=(count,),
            in_specs=in_specs,
            out_specs=out_specs,
            scratch_shapes=scratch,
        ),
        out_shape=out_shape,
        compiler_params=pltpu.CompilerParams(vmem_limit_bytes=VMEM_LIMIT),
        cost_estimate=pl.CostEstimate(
            flops=4 * rows * depth * count * ff // 8,
            bytes_accessed=4 * depth * count * ff // 8,
            transcendentals=0,
        ),
        name="gate_up",
    )(order, *args)


def down_block(hidden_ref, weight_ref):
    ff = hidden_ref.shape[1]
    main = ff // 256 * 256
    value = jnp.dot(
        hidden_ref[:, :main], weight_ref[:main, :], preferred_element_type=jnp.float32
    )
    if main < ff:
        value = value + jnp.dot(
            hidden_ref[:, main:], weight_ref[main:, :], preferred_element_type=jnp.float32
        )
    return value


def down_body(kinds, order_ref, hidden_ref, weight_ref, *outs):
    now = pl.program_id(0)
    value = down_block(hidden_ref, weight_ref)
    for s, kind in enumerate(kinds):

        @pl.when(now == s)
        def _(out=outs[s], kind=kind):
            out[...] = value.astype(out.dtype)


def down(order, jobs, hidden, down_weight, width):
    rows, ff = hidden.shape
    count = len(jobs)
    places, kinds = zip(*jobs)
    return pl.pallas_call(
        functools.partial(down_body, kinds),
        grid_spec=pltpu.PrefetchScalarGridSpec(
            num_scalar_prefetch=1,
            grid=(count,),
            in_specs=[
                pl.BlockSpec((rows, ff), lambda s, order: (0, 0)),
                pl.BlockSpec((ff, width), lambda s, order: (0, order[pick(places, s)])),
            ],
            out_specs=[pl.BlockSpec((rows, width), lambda s, order: (0, 0))] * count,
        ),
        out_shape=[jax.ShapeDtypeStruct((rows, width), kind) for kind in kinds],
        compiler_params=pltpu.CompilerParams(vmem_limit_bytes=VMEM_LIMIT),
        cost_estimate=pl.CostEstimate(
            flops=rows * ff * width * count // 4,
            bytes_accessed=ff * width * count // 4,
            transcendentals=0,
        ),
        name="down",
    )(order, hidden, down_weight)


def overlapped(activations, norm_gain, gate_weight, up_weight, down_weight):
    width = activations.shape[1]
    index = lax.axis_index("gx").astype(jnp.int32)
    z = index >> 2
    end = (z == 0) | (z == LINE - 1)
    resident = activations.astype(jnp.float32)

    taken = jnp.where(end, jnp.asarray(TAKEN[0]), jnp.asarray(TAKEN[1]))
    order = ((index >> 1) ^ taken) * 2 + (index & 1)
    order = jnp.concatenate([order, order ^ 1])
    OWN, ONE, ONE_IN, TWO, TWO_IN, THREE, THREE_ACROSS, FOUR = range(8)

    def multiply(acc, *shards, last=False):
        places = [place + 8 * other for place, other, _ in shards]
        blocks = [x for _, _, x in shards]
        return gate_up(order, places, blocks, gate_weight, up_weight, acc, last)

    own = prepare(activations, norm_gain)
    one, one_in = send(own, ALONG), send(own, INSIDE)
    acc = multiply(None, (OWN, 0, own), (OWN, 1, swap(own)))
    one, one_in = after((one, one_in), acc[3])
    two, two_in = send(one_in, ALONG), send(one, INSIDE)
    acc = multiply(
        acc,
        (ONE, 0, one), (ONE_IN, 0, one_in), (ONE, 1, swap(one)), (ONE_IN, 1, swap(one_in)),
    )
    two, two_in = after((two, two_in), acc[3])
    three, three_across = send(two_in, ALONG), send(jnp.where(end, two, one_in), ACROSS)
    acc = multiply(
        acc,
        (TWO, 0, two), (TWO_IN, 0, two_in), (TWO, 1, swap(two)), (TWO_IN, 1, swap(two_in)),
    )
    three, three_across = after((three, three_across), acc[3])
    four = send(jnp.where(end, three, two_in), ACROSS)
    acc = multiply(
        acc,
        (THREE, 0, three), (THREE_ACROSS, 0, three_across),
        (THREE, 1, swap(three)), (THREE_ACROSS, 1, swap(three_across)),
    )
    four = after(four, acc[3])
    hidden = multiply(acc, (FOUR, 0, four), (FOUR, 1, swap(four)), last=True)[0]

    narrow = lambda x: x.astype(jnp.bfloat16)
    wide = lambda x: x.astype(jnp.float32)
    zero = jnp.zeros((), jnp.float32)

    def partials(hidden, kept, sent):
        jobs = [(place, jnp.float32) for place in kept]
        jobs += [(place + 8, jnp.bfloat16) for place in sent]
        outs = down(order, jobs, hidden, down_weight, width)
        return *outs[: len(kept)], *(swap(x) for x in outs[len(kept) :])

    (other_four,) = partials(hidden, (), (FOUR,))
    four, other_three, other_across = partials(hidden, (FOUR,), (THREE, THREE_ACROSS))
    four = narrow(four + wide(other_four))
    got = wide(send(four, ACROSS))
    three, across, other_two, other_in = partials(
        after(hidden, four), (THREE, THREE_ACROSS), (TWO, TWO_IN)
    )
    across = narrow(across + wide(other_across))
    got_across = wide(send(across, ACROSS))
    three = narrow(three + wide(other_three) + jnp.where(end, got, zero))
    got_three = wide(send(three, ALONG))
    two, two_in, other_one, other_one_in = partials(
        after(hidden, three, across), (TWO, TWO_IN), (ONE, ONE_IN)
    )
    two = narrow(two + wide(other_two) + jnp.where(end, got_across, zero))
    got_two = wide(send(two, ALONG))
    two_in = narrow(two_in + wide(other_in) + jnp.where(end, zero, got) + got_three)
    got_in = wide(send(two_in, INSIDE))
    one, one_in, other_own = partials(after(hidden, two, two_in), (ONE, ONE_IN), (OWN,))
    one_in = narrow(one_in + wide(other_one_in) + jnp.where(end, zero, got_across) + got_two)
    got_one_in = wide(send(one_in, INSIDE))
    one = narrow(one + wide(other_one) + got_in)
    got_one = wide(send(one, ALONG))
    (kept,) = partials(after(hidden, one, one_in), (OWN,), ())
    branch = kept + wide(other_own)
    return (resident + branch + got_one + got_one_in).astype(jnp.bfloat16)


def plain(activations, norm_gain, gate_weight, up_weight, down_weight):
    resident = activations.astype(jnp.float32)
    totals = lax.psum(jnp.sum(resident * resident, axis=1), "gx")
    factor = lax.rsqrt(totals / (resident.shape[1] * lax.axis_size("gx")) + epsilon)
    normed = (resident * factor[:, None] * norm_gain.astype(jnp.float32)[None, :]).astype(
        jnp.bfloat16
    )
    pieces = lax.all_gather(normed, "gx", axis=1, tiled=True)
    gate_sum = jnp.dot(pieces, gate_weight, preferred_element_type=jnp.float32)
    up_sum = jnp.dot(pieces, up_weight, preferred_element_type=jnp.float32)
    hidden = (jax.nn.silu(gate_sum) * up_sum).astype(jnp.bfloat16)
    summed = lax.psum_scatter(
        lax.dot_general(
            down_weight, hidden, (((0,), (1,)), ((), ())), preferred_element_type=jnp.float32
        ),
        "gx",
        scatter_dimension=0,
        tiled=True,
    )
    return (resident + summed.T).astype(jnp.bfloat16)


def per_device(n, activations, norm_gain, gate_weight, up_weight, down_weight):
    args = (activations, norm_gain, gate_weight, up_weight, down_weight)
    rows, width = activations.shape
    tiled = rows % 128 == 0 and width % 128 == 0 and gate_weight.shape[1] % 128 == 0
    tiled = tiled and rows <= width
    if n == 4 * LINE and tiled:
        return overlapped(*args)
    return plain(*args)


def solution(mesh):
    in_specs = (P("groups", "gx"), P("gx"), P(None, "gx"), P(None, "gx"), P("gx", None))
    out_specs = P("groups", "gx")
    return jax.shard_map(
        functools.partial(per_device, mesh.shape["gx"]),
        mesh=mesh,
        in_specs=in_specs,
        out_specs=out_specs,
        check_vma=False,
    )
```

```python
import functools

import jax
import jax.numpy as jnp
import numpy as np
from jax import lax
from jax.experimental import pallas as pl
from jax.experimental.pallas import tpu as pltpu
from jax.sharding import PartitionSpec as P

epsilon = 1e-05
LINE = 4
EXTRA = 16
VMEM_LIMIT = 36 * 1024 * 1024
PREPARE_LIMIT = 60 * 1024 * 1024

ALONG = (lambda z, y: (z ^ 1, y),) * 2
INSIDE = (lambda z, y: (z, y ^ 1), lambda z, y: (z ^ 3, y))
ACROSS = (lambda z, y: (z, y ^ 1),) * 2

TAKEN = np.array([(0, 2, 1, 4, 3, 6, 5, 7), (0, 2, 6, 3, 4, 1, 7, 5)], np.int32)


def send(x, move):
    pairs = []
    for z in range(LINE):
        for y in range(2):
            to_z, to_y = move[0 < z < LINE - 1](z, y)
            pairs += [(z * 4 + y * 2 + c, to_z * 4 + to_y * 2 + c) for c in range(2)]
    return lax.ppermute(x, "gx", pairs)


def swap(x):
    return lax.ppermute(x, "gx", [(i, i ^ 1) for i in range(4 * LINE)])


def after(x, *others):
    return lax.optimization_barrier((x, *others))[0]


def block(me, jobs, s):
    def pick(table):
        value = jnp.int32(table[0])
        for i, entry in enumerate(table[1:], 1):
            value = jnp.where(s == i, jnp.int32(entry), value)
        return value

    places, others = zip(*jobs)
    end = (((me >> 2) ^ (me >> 3)) & 1) == 0
    code = jnp.where(end, pick(TAKEN[0, places]), pick(TAKEN[1, places]))
    return ((me >> 1) ^ code) * 2 + ((me & 1) ^ pick(others))


def prepare_body(x_ref, gain_ref, out_ref):
    rows, width = x_ref.shape
    x = x_ref[...].astype(jnp.float32)
    gain = gain_ref[...].astype(jnp.float32).reshape(1, width)
    out_ref[0, :rows, :] = (x * gain).astype(jnp.bfloat16)
    squares = jnp.broadcast_to(jnp.sum(x * x, axis=1, keepdims=True), (rows, 128)).T[:EXTRA]
    row = lax.broadcasted_iota(jnp.int32, (EXTRA, rows), 0)
    parts = jnp.zeros((EXTRA, rows), jnp.float32)
    for i in range(3):
        part = squares.astype(jnp.bfloat16).astype(jnp.float32)
        parts = jnp.where(row == i, part, parts)
        squares = squares - part
    out_ref[0, rows:, :rows] = parts.astype(jnp.bfloat16)
    if rows < width:
        out_ref[0, rows:, rows:] = jnp.zeros((EXTRA, width - rows), jnp.bfloat16)


def prepare(activations, norm_gain):
    rows, width = activations.shape
    return pl.pallas_call(
        prepare_body,
        out_shape=jax.ShapeDtypeStruct((1, rows + EXTRA, width), jnp.bfloat16),
        compiler_params=pltpu.CompilerParams(vmem_limit_bytes=PREPARE_LIMIT),
        name="prepare",
    )(activations, norm_gain)


def gate_up_body(count, first, last, rows, main, features, me_ref, *refs):
    blocks = refs[:count]
    gate_ref, up_ref, *rest = refs[count:]
    if not first:
        before = rest[:4]
        rest = rest[4:]
    if last:
        hidden_ref, *rest = rest
    accs = rest
    step = pl.program_id(0)

    for s in range(count):

        @pl.when(step == s)
        def _(s=s):
            x = blocks[s][0, :rows, :]
            gate, up = gate_ref[...], up_ref[...]
            mixed = jnp.concatenate([gate[:, main:], up[:, main:]], axis=1)
            values = [
                jnp.dot(x, weight, preferred_element_type=jnp.float32)
                for weight in (gate[:, :main], up[:, :main], mixed)
            ]
            squares = blocks[s][0, rows:, :].astype(jnp.float32)
            squares = jnp.sum(squares, axis=0, keepdims=True)
            values.append(jnp.broadcast_to(squares, accs[3].shape))
            if s:
                values = [acc[...] + value for acc, value in zip(accs, values)]
            elif not first:
                values = [old[...] + value for old, value in zip(before, values)]
            if not last or s < count - 1:
                for acc, value in zip(accs, values):
                    acc[...] = value
                return
            factor = lax.rsqrt(values[3][:1, :rows] / features + epsilon)
            factor = jnp.broadcast_to(factor, (128, rows)).T[:, :1]

            def act(g, u):
                g, u = g * factor, u * factor
                return (g / (1.0 + jnp.exp(-g)) * u).astype(jnp.bfloat16)

            gate, up, both, _ = values
            rem = both.shape[1] // 2
            hidden_ref[:, :main] = act(gate, up)
            hidden_ref[:, main:] = act(both[:, :rem], both[:, rem:])


def gate_up(me, jobs, shards, gate_weight, up_weight, acc, last=False):
    height, depth = shards[0][0].shape[1:]
    count = len(jobs)
    rows = height - EXTRA
    features, ff = gate_weight.shape
    main = ff // 256 * 256 if ff % 256 else ff - 256
    rem = ff - main
    first = acc is None
    whole = lambda shape: pl.BlockSpec(shape, lambda s, me: (0, 0))
    weight = pl.BlockSpec((depth, ff), lambda s, me: (block(me[0], jobs, s), 0))
    shard = lambda i: pl.BlockSpec((1, height, depth), lambda s, me: (i, 0, 0))
    in_specs = [shard(i) for _, i in shards] + [weight, weight]
    args = [*(x for x, _ in shards), gate_weight, up_weight]
    shapes = [(rows, main), (rows, main), (rows, 2 * rem), (8, depth)]
    if not first:
        in_specs += [whole(s) for s in shapes]
        args += list(acc)
    if last:
        out_shape = [jax.ShapeDtypeStruct((rows, ff), jnp.bfloat16)]
        out_specs = [whole((rows, ff))]
        scratch = [pltpu.VMEM(s, jnp.float32) for s in shapes]
    else:
        out_shape = [jax.ShapeDtypeStruct(s, jnp.float32) for s in shapes]
        out_specs = [whole(s) for s in shapes]
        scratch = []
    return pl.pallas_call(
        functools.partial(gate_up_body, count, first, last, rows, main, features),
        grid_spec=pltpu.PrefetchScalarGridSpec(
            num_scalar_prefetch=1,
            grid=(count,),
            in_specs=in_specs,
            out_specs=out_specs,
            scratch_shapes=scratch,
        ),
        out_shape=out_shape,
        compiler_params=pltpu.CompilerParams(vmem_limit_bytes=VMEM_LIMIT),
        cost_estimate=pl.CostEstimate(
            flops=4 * rows * depth * count * ff // 8,
            bytes_accessed=4 * depth * count * ff // 8,
            transcendentals=0,
        ),
        name="gate_up",
    )(me, *args)


def down_block(hidden_ref, weight_ref):
    ff = hidden_ref.shape[1]
    main = ff // 256 * 256
    value = jnp.dot(
        hidden_ref[:, :main], weight_ref[:main, :], preferred_element_type=jnp.float32
    )
    if main < ff:
        value = value + jnp.dot(
            hidden_ref[:, main:], weight_ref[main:, :], preferred_element_type=jnp.float32
        )
    return value


def down_body(kept, sent, me_ref, hidden_ref, weight_ref, *outs):
    now = pl.program_id(0)
    value = down_block(hidden_ref, weight_ref)
    for s in range(kept):

        @pl.when(now == s)
        def _(out=outs[s]):
            out[...] = value

    for s in range(kept, kept + sent):

        @pl.when(now == s)
        def _(out=outs[s]):
            out[...] = value.astype(jnp.bfloat16)


def down(me, kept, sent, hidden, down_weight, width):
    rows, ff = hidden.shape
    jobs = kept + sent
    kinds = [jnp.float32] * len(kept) + [jnp.bfloat16] * len(sent)
    return pl.pallas_call(
        functools.partial(down_body, len(kept), len(sent)),
        grid_spec=pltpu.PrefetchScalarGridSpec(
            num_scalar_prefetch=1,
            grid=(len(jobs),),
            in_specs=[
                pl.BlockSpec((rows, ff), lambda s, me: (0, 0)),
                pl.BlockSpec((ff, width), lambda s, me: (0, block(me[0], jobs, s))),
            ],
            out_specs=[pl.BlockSpec((rows, width), lambda s, me: (0, 0))] * len(jobs),
        ),
        out_shape=[jax.ShapeDtypeStruct((rows, width), kind) for kind in kinds],
        compiler_params=pltpu.CompilerParams(vmem_limit_bytes=VMEM_LIMIT),
        cost_estimate=pl.CostEstimate(
            flops=rows * ff * width * len(jobs) // 4,
            bytes_accessed=ff * width * len(jobs) // 4,
            transcendentals=0,
        ),
        name="down",
    )(me, hidden, down_weight)


def overlapped(activations, norm_gain, gate_weight, up_weight, down_weight):
    width = activations.shape[1]
    index = lax.axis_index("gx").astype(jnp.int32)
    me = index[None]
    z = index >> 2
    end = (z == 0) | (z == LINE - 1)
    resident = activations.astype(jnp.float32)
    OWN, ONE, ONE_IN, TWO, TWO_IN, THREE, THREE_ACROSS, FOUR = range(8)

    def multiply(acc, places, shards, last=False):
        theirs = swap(shards[0] if len(shards) == 1 else jnp.concatenate(shards))
        jobs = [(place, 0) for place in places] + [(place, 1) for place in places]
        arrays = [(x, 0) for x in shards] + [(theirs, i) for i in range(len(places))]
        return gate_up(me, jobs, arrays, gate_weight, up_weight, acc, last)

    own = prepare(activations, norm_gain)
    one, one_in = send(own, ALONG), send(own, INSIDE)
    acc = multiply(None, (OWN,), (own,))
    one, one_in = after((one, one_in), acc[3])
    two, two_in = send(one_in, ALONG), send(one, INSIDE)
    acc = multiply(acc, (ONE, ONE_IN), (one, one_in))
    two, two_in = after((two, two_in), acc[3])
    three, across = send(two_in, ALONG), send(jnp.where(end, two, one_in), ACROSS)
    acc = multiply(acc, (TWO, TWO_IN), (two, two_in))
    three, across = after((three, across), acc[3])
    four = send(jnp.where(end, three, two_in), ACROSS)
    acc = multiply(acc, (THREE, THREE_ACROSS), (three, across))
    four = after(four, acc[3])
    hidden = multiply(acc, (FOUR,), (four,), last=True)[0]

    narrow = lambda x: x.astype(jnp.bfloat16)
    wide = lambda x: x.astype(jnp.float32)
    zero = jnp.zeros((), jnp.float32)

    def partials(hidden, kept, sent):
        kept_jobs, sent_jobs = [(place, 0) for place in kept], [(place, 1) for place in sent]
        outs = down(me, kept_jobs, sent_jobs, hidden, down_weight, width)
        return [*outs[: len(kept)], *(wide(swap(x)) for x in outs[len(kept) :])]

    their_four, their_three, their_across = partials(hidden, (), (FOUR, THREE, THREE_ACROSS))
    (four,) = partials(hidden, (FOUR,), ())
    four = narrow(four + their_four)
    got = wide(send(four, ACROSS))
    three, across, their_two, their_in = partials(
        after(hidden, four), (THREE, THREE_ACROSS), (TWO, TWO_IN)
    )
    across = narrow(across + their_across)
    got_across = wide(send(across, ACROSS))
    three = narrow(three + their_three + jnp.where(end, got, zero))
    got_three = wide(send(three, ALONG))
    two, two_in, their_one, their_one_in = partials(
        after(hidden, three, across), (TWO, TWO_IN), (ONE, ONE_IN)
    )
    two = narrow(two + their_two + jnp.where(end, got_across, zero))
    got_two = wide(send(two, ALONG))
    two_in = narrow(two_in + their_in + jnp.where(end, zero, got) + got_three)
    got_in = wide(send(two_in, INSIDE))
    one, one_in, their_own = partials(after(hidden, two, two_in), (ONE, ONE_IN), (OWN,))
    one_in = narrow(one_in + their_one_in + jnp.where(end, zero, got_across) + got_two)
    got_one_in = wide(send(one_in, INSIDE))
    one = narrow(one + their_one + got_in)
    got_one = wide(send(one, ALONG))
    (kept,) = partials(after(hidden, one, one_in), (OWN,), ())
    branch = kept + their_own
    return (resident + branch + got_one + got_one_in).astype(jnp.bfloat16)


def plain(activations, norm_gain, gate_weight, up_weight, down_weight):
    resident = activations.astype(jnp.float32)
    totals = lax.psum(jnp.sum(resident * resident, axis=1), "gx")
    factor = lax.rsqrt(totals / (resident.shape[1] * lax.axis_size("gx")) + epsilon)
    normed = (resident * factor[:, None] * norm_gain.astype(jnp.float32)[None, :]).astype(
        jnp.bfloat16
    )
    pieces = lax.all_gather(normed, "gx", axis=1, tiled=True)
    gate_sum = jnp.dot(pieces, gate_weight, preferred_element_type=jnp.float32)
    up_sum = jnp.dot(pieces, up_weight, preferred_element_type=jnp.float32)
    hidden = (jax.nn.silu(gate_sum) * up_sum).astype(jnp.bfloat16)
    summed = lax.psum_scatter(
        lax.dot_general(
            down_weight, hidden, (((0,), (1,)), ((), ())), preferred_element_type=jnp.float32
        ),
        "gx",
        scatter_dimension=0,
        tiled=True,
    )
    return (resident + summed.T).astype(jnp.bfloat16)


def per_device(n, activations, norm_gain, gate_weight, up_weight, down_weight):
    args = (activations, norm_gain, gate_weight, up_weight, down_weight)
    rows, width = activations.shape
    tiled = rows % 128 == 0 and width % 128 == 0 and gate_weight.shape[1] % 128 == 0
    tiled = tiled and rows <= width
    if n == 4 * LINE and tiled:
        return overlapped(*args)
    return plain(*args)


def solution(mesh):
    in_specs = (P("groups", "gx"), P("gx"), P(None, "gx"), P(None, "gx"), P("gx", None))
    out_specs = P("groups", "gx")
    return jax.shard_map(
        functools.partial(per_device, mesh.shape["gx"]),
        mesh=mesh,
        in_specs=in_specs,
        out_specs=out_specs,
        check_vma=False,
    )
```

```python
import functools

import jax
import jax.numpy as jnp
import numpy as np
from jax import lax
from jax.experimental import pallas as pl
from jax.experimental.pallas import tpu as pltpu
from jax.sharding import PartitionSpec as P

epsilon = 1e-05
LINE = 4
EXTRA = 16
SPLIT = 2
VMEM_LIMIT = 36 * 1024 * 1024
PREPARE_LIMIT = 60 * 1024 * 1024

ALONG = (lambda z, y: (z ^ 1, y),) * 2
INSIDE = (lambda z, y: (z, y ^ 1), lambda z, y: (z ^ 3, y))
ACROSS = (lambda z, y: (z, y ^ 1),) * 2

TAKEN = np.array([(0, 2, 1, 4, 3, 6, 5, 7), (0, 2, 6, 3, 4, 1, 7, 5)], np.int32)


def send(x, move):
    pairs = []
    for z in range(LINE):
        for y in range(2):
            to_z, to_y = move[0 < z < LINE - 1](z, y)
            pairs += [(z * 4 + y * 2 + c, to_z * 4 + to_y * 2 + c) for c in range(2)]
    return lax.ppermute(x, "gx", pairs)


def swap(x):
    return lax.ppermute(x, "gx", [(i, i ^ 1) for i in range(4 * LINE)])


def after(x, *others):
    return lax.optimization_barrier((x, *others))[0]


def block(me, jobs, s):
    def pick(table):
        value = jnp.int32(table[0])
        for i, entry in enumerate(table[1:], 1):
            value = jnp.where(s == i, jnp.int32(entry), value)
        return value

    places, others = zip(*jobs)
    end = (((me >> 2) ^ (me >> 3)) & 1) == 0
    code = jnp.where(end, pick(TAKEN[0, places]), pick(TAKEN[1, places]))
    return ((me >> 1) ^ code) * 2 + ((me & 1) ^ pick(others))


def prepare_body(x_ref, gain_ref, out_ref):
    rows, width = x_ref.shape
    x = x_ref[...].astype(jnp.float32)
    gain = gain_ref[...].astype(jnp.float32).reshape(1, width)
    out_ref[0, :rows, :] = (x * gain).astype(jnp.bfloat16)
    squares = jnp.broadcast_to(jnp.sum(x * x, axis=1, keepdims=True), (rows, 128)).T[:EXTRA]
    row = lax.broadcasted_iota(jnp.int32, (EXTRA, rows), 0)
    parts = jnp.zeros((EXTRA, rows), jnp.float32)
    for i in range(3):
        part = squares.astype(jnp.bfloat16).astype(jnp.float32)
        parts = jnp.where(row == i, part, parts)
        squares = squares - part
    out_ref[0, rows:, :rows] = parts.astype(jnp.bfloat16)
    if rows < width:
        out_ref[0, rows:, rows:] = jnp.zeros((EXTRA, width - rows), jnp.bfloat16)


def prepare(activations, norm_gain):
    rows, width = activations.shape
    return pl.pallas_call(
        prepare_body,
        out_shape=jax.ShapeDtypeStruct((1, rows + EXTRA, width), jnp.bfloat16),
        compiler_params=pltpu.CompilerParams(vmem_limit_bytes=PREPARE_LIMIT),
        name="prepare",
    )(activations, norm_gain)


def gate_up_body(count, first, last, rows, main, features, me_ref, *refs):
    shards = refs[:count]
    gate_ref, up_ref, *rest = refs[count:]
    if not first:
        before = rest[:4]
        rest = rest[4:]
    if last:
        hidden_ref, *rest = rest
    accs = rest
    now = pl.program_id(0)
    final = SPLIT * count - 1

    def products(x_ref):
        x = x_ref[0, :rows, :]
        gate, up = gate_ref[...], up_ref[...]
        mixed = jnp.concatenate([gate[:, main:], up[:, main:]], axis=1)
        for weight in (gate[:, :main], up[:, :main], mixed):
            yield jnp.dot(x, weight, preferred_element_type=jnp.float32)

    def start():
        for i, value in enumerate(products(shards[0])):
            accs[i][...] = value if first else before[i][...] + value

    def add(x_ref):
        for acc, value in zip(accs, products(x_ref)):
            acc[...] += value

    def finish():
        gate, up, both = (
            acc[...] + value for acc, value in zip(accs, products(shards[-1]))
        )
        factor = lax.rsqrt(accs[3][:1, :rows] / features + epsilon)
        factor = jnp.broadcast_to(factor, (128, rows)).T[:, :1]

        def act(g, u):
            g, u = g * factor, u * factor
            return (g / (1.0 + jnp.exp(-g)) * u).astype(jnp.bfloat16)

        rem = both.shape[1] // 2
        hidden_ref[:, :main] = act(gate, up)
        hidden_ref[:, main:] = act(both[:, :rem], both[:, rem:])

    @pl.when(now == 0)
    def _():
        accs[3][...] = jnp.zeros_like(accs[3]) if first else before[3][...]

    for j, x_ref in enumerate(shards):
        for part in range(SPLIT):

            @pl.when(now == SPLIT * j + part)
            def _(x_ref=x_ref, part=part):
                squares = jnp.sum(x_ref[0, rows:, :].astype(jnp.float32), axis=0, keepdims=True)
                width = squares.shape[1]
                at = (slice(None), slice(part * width, (part + 1) * width))
                accs[3][at] += jnp.broadcast_to(squares, (accs[3].shape[0], width))

        low, high = SPLIT * j, SPLIT * (j + 1)
        if not j:
            pl.when(now == 0)(start)
            low = 1
        if last and j == count - 1:
            pl.when(now == final)(finish)
            high -= 1
        if low < high:
            pl.when((now >= low) & (now < high))(functools.partial(add, x_ref))


def gate_up(me, jobs, shards, gate_weight, up_weight, acc, last=False):
    height, depth = shards[0][0].shape[1:]
    count = len(jobs)
    rows = height - EXTRA
    features, ff = gate_weight.shape
    main = ff // 256 * 256 if ff % 256 else ff - 256
    rem = ff - main
    first = acc is None
    whole = lambda shape: pl.BlockSpec(shape, lambda s, me: (0, 0))
    weight = pl.BlockSpec((depth // SPLIT, ff), lambda s, me: (block(me[0], jobs, s // SPLIT) * SPLIT + s % SPLIT, 0))
    shard = lambda j, i: pl.BlockSpec(
        (1, height, depth // SPLIT),
        lambda s, me: (i, 0, jnp.clip(s - SPLIT * j, 0, SPLIT - 1)),
    )
    in_specs = [shard(j, i) for j, (_, i) in enumerate(shards)] + [weight, weight]
    args = [*(x for x, _ in shards), gate_weight, up_weight]
    shapes = [(rows, main), (rows, main), (rows, 2 * rem), (8, depth)]
    if not first:
        in_specs += [whole(s) for s in shapes]
        args += list(acc)
    if last:
        out_shape = [jax.ShapeDtypeStruct((rows, ff), jnp.bfloat16)]
        out_specs = [whole((rows, ff))]
        scratch = [pltpu.VMEM(s, jnp.float32) for s in shapes]
    else:
        out_shape = [jax.ShapeDtypeStruct(s, jnp.float32) for s in shapes]
        out_specs = [whole(s) for s in shapes]
        scratch = []
    return pl.pallas_call(
        functools.partial(gate_up_body, count, first, last, rows, main, features),
        grid_spec=pltpu.PrefetchScalarGridSpec(
            num_scalar_prefetch=1,
            grid=(SPLIT * count,),
            in_specs=in_specs,
            out_specs=out_specs,
            scratch_shapes=scratch,
        ),
        out_shape=out_shape,
        compiler_params=pltpu.CompilerParams(vmem_limit_bytes=VMEM_LIMIT),
        cost_estimate=pl.CostEstimate(
            flops=4 * rows * depth * count * ff // 8,
            bytes_accessed=4 * depth * count * ff // 8,
            transcendentals=0,
        ),
        name="gate_up",
    )(me, *args)


def down_block(hidden_ref, weight_ref):
    ff = hidden_ref.shape[1]
    main = ff // 256 * 256
    value = jnp.dot(
        hidden_ref[:, :main], weight_ref[:main, :], preferred_element_type=jnp.float32
    )
    if main < ff:
        value = value + jnp.dot(
            hidden_ref[:, main:], weight_ref[main:, :], preferred_element_type=jnp.float32
        )
    return value


def down_body(kept, sent, me_ref, hidden_ref, weight_ref, *outs):
    now = pl.program_id(0)
    value = down_block(hidden_ref, weight_ref)
    for s in range(kept):

        @pl.when(now == s)
        def _(out=outs[s]):
            out[...] = value

    for s in range(kept, kept + sent):

        @pl.when(now == s)
        def _(out=outs[s]):
            out[...] = value.astype(jnp.bfloat16)


def down(me, kept, sent, hidden, down_weight, width):
    rows, ff = hidden.shape
    jobs = kept + sent
    kinds = [jnp.float32] * len(kept) + [jnp.bfloat16] * len(sent)
    return pl.pallas_call(
        functools.partial(down_body, len(kept), len(sent)),
        grid_spec=pltpu.PrefetchScalarGridSpec(
            num_scalar_prefetch=1,
            grid=(len(jobs),),
            in_specs=[
                pl.BlockSpec((rows, ff), lambda s, me: (0, 0)),
                pl.BlockSpec((ff, width), lambda s, me: (0, block(me[0], jobs, s))),
            ],
            out_specs=[pl.BlockSpec((rows, width), lambda s, me: (0, 0))] * len(jobs),
        ),
        out_shape=[jax.ShapeDtypeStruct((rows, width), kind) for kind in kinds],
        compiler_params=pltpu.CompilerParams(vmem_limit_bytes=VMEM_LIMIT),
        cost_estimate=pl.CostEstimate(
            flops=rows * ff * width * len(jobs) // 4,
            bytes_accessed=ff * width * len(jobs) // 4,
            transcendentals=0,
        ),
        name="down",
    )(me, hidden, down_weight)


def overlapped(activations, norm_gain, gate_weight, up_weight, down_weight):
    width = activations.shape[1]
    index = lax.axis_index("gx").astype(jnp.int32)
    me = index[None]
    z = index >> 2
    end = (z == 0) | (z == LINE - 1)
    resident = activations.astype(jnp.float32)
    OWN, ONE, ONE_IN, TWO, TWO_IN, THREE, THREE_ACROSS, FOUR = range(8)

    def multiply(acc, places, shards, last=False):
        theirs = swap(shards[0] if len(shards) == 1 else jnp.concatenate(shards))
        jobs = [(place, 0) for place in places] + [(place, 1) for place in places]
        arrays = [(x, 0) for x in shards] + [(theirs, i) for i in range(len(places))]
        return gate_up(me, jobs, arrays, gate_weight, up_weight, acc, last)

    early, end = lax.optimization_barrier((activations, end))
    own = prepare(early, norm_gain)
    one, one_in = send(own, ALONG), send(own, INSIDE)
    acc = multiply(None, (OWN,), (own,))
    one, one_in = after((one, one_in), acc[3])
    two, two_in = send(one_in, ALONG), send(one, INSIDE)
    acc = multiply(acc, (ONE, ONE_IN), (one, one_in))
    two, two_in = after((two, two_in), acc[3])
    three, across = send(two_in, ALONG), send(jnp.where(end, two, one_in), ACROSS)
    acc = multiply(acc, (TWO, TWO_IN), (two, two_in))
    three, across = after((three, across), acc[3])
    four = send(jnp.where(end, three, two_in), ACROSS)
    acc = multiply(acc, (THREE, THREE_ACROSS), (three, across))
    four = after(four, acc[3])
    hidden = multiply(acc, (FOUR,), (four,), last=True)[0]

    narrow = lambda x: x.astype(jnp.bfloat16)
    wide = lambda x: x.astype(jnp.float32)
    zero = jnp.zeros((), jnp.float32)

    def partials(hidden, kept, sent):
        kept_jobs, sent_jobs = [(place, 0) for place in kept], [(place, 1) for place in sent]
        outs = down(me, kept_jobs, sent_jobs, hidden, down_weight, width)
        return [*outs[: len(kept)], *(wide(swap(x)) for x in outs[len(kept) :])]

    their_four, their_three, their_across = partials(hidden, (), (FOUR, THREE, THREE_ACROSS))
    (four,) = partials(hidden, (FOUR,), ())
    four = narrow(four + their_four)
    got = wide(send(four, ACROSS))
    three, across, their_two, their_in = partials(
        after(hidden, four), (THREE, THREE_ACROSS), (TWO, TWO_IN)
    )
    across = narrow(across + their_across)
    got_across = wide(send(across, ACROSS))
    three = narrow(three + their_three + jnp.where(end, got, zero))
    got_three = wide(send(three, ALONG))
    two, two_in, their_one, their_one_in = partials(
        after(hidden, three, across), (TWO, TWO_IN), (ONE, ONE_IN)
    )
    two = narrow(two + their_two + jnp.where(end, got_across, zero))
    got_two = wide(send(two, ALONG))
    two_in = narrow(two_in + their_in + jnp.where(end, zero, got) + got_three)
    got_in = wide(send(two_in, INSIDE))
    one, one_in, their_own = partials(after(hidden, two, two_in), (ONE, ONE_IN), (OWN,))
    one_in = narrow(one_in + their_one_in + jnp.where(end, zero, got_across) + got_two)
    got_one_in = wide(send(one_in, INSIDE))
    one = narrow(one + their_one + got_in)
    got_one = wide(send(one, ALONG))
    (kept,) = partials(after(hidden, one, one_in), (OWN,), ())
    branch = kept + their_own
    return (resident + branch + got_one + got_one_in).astype(jnp.bfloat16)


def plain(activations, norm_gain, gate_weight, up_weight, down_weight):
    resident = activations.astype(jnp.float32)
    totals = lax.psum(jnp.sum(resident * resident, axis=1), "gx")
    factor = lax.rsqrt(totals / (resident.shape[1] * lax.axis_size("gx")) + epsilon)
    normed = (resident * factor[:, None] * norm_gain.astype(jnp.float32)[None, :]).astype(
        jnp.bfloat16
    )
    pieces = lax.all_gather(normed, "gx", axis=1, tiled=True)
    gate_sum = jnp.dot(pieces, gate_weight, preferred_element_type=jnp.float32)
    up_sum = jnp.dot(pieces, up_weight, preferred_element_type=jnp.float32)
    hidden = (jax.nn.silu(gate_sum) * up_sum).astype(jnp.bfloat16)
    summed = lax.psum_scatter(
        lax.dot_general(
            down_weight, hidden, (((0,), (1,)), ((), ())), preferred_element_type=jnp.float32
        ),
        "gx",
        scatter_dimension=0,
        tiled=True,
    )
    return (resident + summed.T).astype(jnp.bfloat16)


def per_device(n, activations, norm_gain, gate_weight, up_weight, down_weight):
    args = (activations, norm_gain, gate_weight, up_weight, down_weight)
    rows, width = activations.shape
    tiled = rows % 128 == 0 and width % 128 == 0 and gate_weight.shape[1] % 128 == 0
    tiled = tiled and rows <= width
    if n == 4 * LINE and tiled:
        return overlapped(*args)
    return plain(*args)


def solution(mesh):
    in_specs = (P("groups", "gx"), P("gx"), P(None, "gx"), P(None, "gx"), P("gx", None))
    out_specs = P("groups", "gx")
    return jax.shard_map(
        functools.partial(per_device, mesh.shape["gx"]),
        mesh=mesh,
        in_specs=in_specs,
        out_specs=out_specs,
        check_vma=False,
    )
```

```python
import functools

import jax
import jax.numpy as jnp
import numpy as np
from jax import lax
from jax.experimental import pallas as pl
from jax.experimental.pallas import tpu as pltpu
from jax.sharding import PartitionSpec as P

epsilon = 1e-05
LINE = 4
EXTRA = 16
TILE = 256
VMEM_LIMIT = 36 * 1024 * 1024
PREPARE_LIMIT = 60 * 1024 * 1024

ALONG = (lambda z, y: (z ^ 1, y),) * 2
INSIDE = (lambda z, y: (z, y ^ 1), lambda z, y: (z ^ 3, y))
ACROSS = (lambda z, y: (z, y ^ 1),) * 2

TAKEN = np.array([(0, 2, 1, 4, 3, 6, 5, 7), (0, 2, 6, 3, 4, 1, 7, 5)], np.int32)


def send(x, move):
    pairs = []
    for z in range(LINE):
        for y in range(2):
            to_z, to_y = move[0 < z < LINE - 1](z, y)
            pairs += [(z * 4 + y * 2 + c, to_z * 4 + to_y * 2 + c) for c in range(2)]
    return lax.ppermute(x, "gx", pairs)


def swap(x):
    return lax.ppermute(x, "gx", [(i, i ^ 1) for i in range(4 * LINE)])


def after(x, *others):
    return lax.optimization_barrier((x, *others))[0]


def chip(me, place):
    end = (((me >> 2) ^ (me >> 3)) & 1) == 0
    return (me >> 1) ^ jnp.where(end, jnp.int32(TAKEN[0, place]), jnp.int32(TAKEN[1, place]))


def prepare_body(x_ref, gain_ref, out_ref):
    rows, width = x_ref.shape
    x = x_ref[...].astype(jnp.float32)
    gain = gain_ref[...].astype(jnp.float32).reshape(1, width)
    out_ref[0, :rows, :] = (x * gain).astype(jnp.bfloat16)
    squares = jnp.broadcast_to(jnp.sum(x * x, axis=1, keepdims=True), (rows, 128)).T[:EXTRA]
    row = lax.broadcasted_iota(jnp.int32, (EXTRA, rows), 0)
    parts = jnp.zeros((EXTRA, rows), jnp.float32)
    for i in range(3):
        part = squares.astype(jnp.bfloat16).astype(jnp.float32)
        parts = jnp.where(row == i, part, parts)
        squares = squares - part
    out_ref[0, rows:, :rows] = parts.astype(jnp.bfloat16)
    if rows < width:
        out_ref[0, rows:, rows:] = jnp.zeros((EXTRA, width - rows), jnp.bfloat16)


def prepare(activations, norm_gain):
    rows, width = activations.shape
    return pl.pallas_call(
        prepare_body,
        out_shape=jax.ShapeDtypeStruct((1, rows + EXTRA, width), jnp.bfloat16),
        compiler_params=pltpu.CompilerParams(vmem_limit_bytes=PREPARE_LIMIT),
        name="prepare",
    )(activations, norm_gain)


def gate_up_body(places, indices, first, last, features, me_ref, *refs):
    count = len(places)
    shards = refs[: 2 * count]
    gate_ref, up_ref, *rest = refs[2 * count :]
    if not first:
        sums_in, stats_in, *rest = rest
    out_ref, *rest = rest
    if not last:
        stats_ref, *rest = rest
    lhs_ref, weight_ref, sums_ref, lhs_sems, weight_sems, in_sems, out_sems = rest
    me = me_ref[0]
    core = me & 1
    height, depth = lhs_ref.shape[0], lhs_ref.shape[1] // (2 * count)
    rows = height - EXTRA
    ff = gate_ref.shape[1]
    main = ff // TILE * TILE
    rem = ff - main

    copies = []
    for j, (x_ref, i) in enumerate(zip(shards, indices)):
        at = (j % count) * 2 * depth + (core if j < count else 1 - core) * depth
        at = pl.multiple_of(at, depth)
        copies.append(
            pltpu.make_async_copy(x_ref.at[i], lhs_ref.at[:, pl.ds(at, depth)], lhs_sems.at[j])
        )
        copies[-1].start()

    def fetch(t, source, column, size, place, sem):
        found = []
        for p in range(count):
            row = pl.multiple_of(chip(me, places[p]) * 2 * depth, 2 * depth)
            found.append(
                pltpu.make_async_copy(
                    source.at[pl.ds(row, 2 * depth), pl.ds(column, size)],
                    weight_ref.at[t, pl.ds(p * 2 * depth, 2 * depth), pl.ds(place, size)],
                    weight_sems.at[sem, p],
                )
            )
        return found

    tiles = []
    for n in range(0, main, TILE):
        for source in (gate_ref, up_ref):
            tiles.append(fetch(len(tiles), source, n, TILE, 0, len(tiles)))
    t = len(tiles)
    tiles.append(fetch(t, gate_ref, main, rem, 0, t) + fetch(t, up_ref, main, rem, rem, t + 1))
    before = []
    for t, found in enumerate(tiles):
        for copy in found:
            copy.start()
        if not first:
            before.append(pltpu.make_async_copy(sums_in.at[t], sums_ref.at[t], in_sems.at[t]))
            before[-1].start()
    for copy in copies:
        copy.wait()

    squares = jnp.sum(lhs_ref[rows:, :].astype(jnp.float32), axis=0, keepdims=True)
    squares = sum(squares[:, i * depth : (i + 1) * depth] for i in range(2 * count))
    if not first:
        squares = squares + stats_in[:1, :]

    def product(t):
        for copy in tiles[t]:
            copy.wait()
        value = jnp.dot(lhs_ref[:rows, :], weight_ref[t], preferred_element_type=jnp.float32)
        if not first:
            before[t].wait()
            value = value + sums_ref[t]
        return value

    if last:
        factor = lax.rsqrt(squares[:, :rows] / features + epsilon)
        factor = jnp.broadcast_to(factor, (128, rows)).T[:, :1]

        def act(g, u):
            g, u = g * factor, u * factor
            return (g / (1.0 + jnp.exp(-g)) * u).astype(jnp.bfloat16)

        for t in range(0, len(tiles) - 1, 2):
            n = t // 2 * TILE
            out_ref[:, n : n + TILE] = act(product(t), product(t + 1))
        both = product(len(tiles) - 1)
        out_ref[:, main:] = act(both[:, :rem], both[:, rem:])
    else:
        stats_ref[...] = jnp.broadcast_to(squares, stats_ref.shape)
        results = []
        for t in range(len(tiles)):
            sums_ref[t] = product(t)
            results.append(pltpu.make_async_copy(sums_ref.at[t], out_ref.at[t], out_sems.at[t]))
            results[-1].start()
        for copy in results:
            copy.wait()


def gate_up(me, places, shards, gate_weight, up_weight, acc, last=False):
    height, depth = shards[0][0].shape[1:]
    count = len(places)
    rows = height - EXTRA
    features, ff = gate_weight.shape
    tiles = 2 * (ff // TILE) + 1
    first = acc is None
    anywhere = pl.BlockSpec(memory_space=pl.ANY)
    vmem = pl.BlockSpec(memory_space=pltpu.VMEM)
    in_specs = [pl.BlockSpec(memory_space=pltpu.SMEM)] + [anywhere] * (2 * count + 2)
    args = [*(x for x, _ in shards), gate_weight, up_weight]
    if not first:
        in_specs += [anywhere, vmem]
        args += list(acc)
    if last:
        out_shape = [jax.ShapeDtypeStruct((rows, ff), jnp.bfloat16)]
        out_specs = [vmem]
    else:
        out_shape = [
            jax.ShapeDtypeStruct((tiles, rows, TILE), jnp.float32),
            jax.ShapeDtypeStruct((8, depth), jnp.float32),
        ]
        out_specs = [anywhere, vmem]
    indices = tuple(i for _, i in shards)
    return pl.pallas_call(
        functools.partial(gate_up_body, places, indices, first, last, features),
        in_specs=in_specs,
        out_specs=out_specs,
        out_shape=out_shape,
        scratch_shapes=[
            pltpu.VMEM((height, 2 * count * depth), jnp.bfloat16),
            pltpu.VMEM((tiles, 2 * count * depth, TILE), jnp.bfloat16),
            pltpu.VMEM((tiles, rows, TILE), jnp.float32),
            pltpu.SemaphoreType.DMA((2 * count,)),
            pltpu.SemaphoreType.DMA((tiles + 1, count)),
            pltpu.SemaphoreType.DMA((tiles,)),
            pltpu.SemaphoreType.DMA((tiles,)),
        ],
        compiler_params=pltpu.CompilerParams(vmem_limit_bytes=VMEM_LIMIT),
        cost_estimate=pl.CostEstimate(
            flops=rows * depth * count * ff,
            bytes_accessed=depth * count * ff,
            transcendentals=0,
        ),
        name="gate_up",
    )(me, *args)


def down_body(jobs, width, me_ref, hidden_ref, weight_ref, *refs):
    outs = refs[: len(jobs)]
    buffer_ref, sems = refs[len(jobs) :]
    me = me_ref[0]
    ff = hidden_ref.shape[1]
    main = ff // TILE * TILE
    pieces = []
    for place, other in jobs:
        column = (chip(me, place) * 2 + ((me & 1) ^ other)) * width
        for n in range(0, width, TILE):
            i = len(pieces)
            pieces.append(
                pltpu.make_async_copy(
                    weight_ref.at[:, pl.ds(pl.multiple_of(column + n, TILE), TILE)],
                    buffer_ref.at[i],
                    sems.at[i],
                )
            )
            pieces[-1].start()
    for i, copy in enumerate(pieces):
        copy.wait()
        value = jnp.dot(
            hidden_ref[:, :main], buffer_ref[i, :main, :], preferred_element_type=jnp.float32
        )
        if main < ff:
            value = value + jnp.dot(
                hidden_ref[:, main:], buffer_ref[i, main:, :], preferred_element_type=jnp.float32
            )
        out = outs[i * TILE // width]
        n = i * TILE % width
        out[:, n : n + TILE] = value.astype(out.dtype)


def down(me, kept, sent, hidden, down_weight, width):
    rows, ff = hidden.shape
    jobs = kept + sent
    kinds = [jnp.float32] * len(kept) + [jnp.bfloat16] * len(sent)
    count = len(jobs) * (width // TILE)
    vmem = pl.BlockSpec(memory_space=pltpu.VMEM)
    return pl.pallas_call(
        functools.partial(down_body, jobs, width),
        in_specs=[pl.BlockSpec(memory_space=pltpu.SMEM), vmem, pl.BlockSpec(memory_space=pl.ANY)],
        out_specs=[vmem] * len(jobs),
        out_shape=[jax.ShapeDtypeStruct((rows, width), kind) for kind in kinds],
        scratch_shapes=[
            pltpu.VMEM((count, ff, TILE), jnp.bfloat16),
            pltpu.SemaphoreType.DMA((count,)),
        ],
        compiler_params=pltpu.CompilerParams(vmem_limit_bytes=VMEM_LIMIT),
        cost_estimate=pl.CostEstimate(
            flops=rows * ff * width * len(jobs) // 4,
            bytes_accessed=ff * width * len(jobs) // 4,
            transcendentals=0,
        ),
        name="down",
    )(me, hidden, down_weight)


def overlapped(activations, norm_gain, gate_weight, up_weight, down_weight):
    width = activations.shape[1]
    index = lax.axis_index("gx").astype(jnp.int32)
    me = index[None]
    z = index >> 2
    end = (z == 0) | (z == LINE - 1)
    resident = activations.astype(jnp.float32)
    OWN, ONE, ONE_IN, TWO, TWO_IN, THREE, THREE_ACROSS, FOUR = range(8)

    def multiply(acc, places, shards, last=False):
        theirs = swap(shards[0] if len(shards) == 1 else jnp.concatenate(shards))
        arrays = [(x, 0) for x in shards] + [(theirs, i) for i in range(len(places))]
        return gate_up(me, places, arrays, gate_weight, up_weight, acc, last)

    early, end = lax.optimization_barrier((activations, end))
    own = prepare(early, norm_gain)
    one, one_in = send(own, ALONG), send(own, INSIDE)
    acc = multiply(None, (OWN,), (own,))
    one, one_in = after((one, one_in), acc[1])
    two, two_in = send(one_in, ALONG), send(one, INSIDE)
    acc = multiply(acc, (ONE, ONE_IN), (one, one_in))
    two, two_in = after((two, two_in), acc[1])
    three, across = send(two_in, ALONG), send(jnp.where(end, two, one_in), ACROSS)
    acc = multiply(acc, (TWO, TWO_IN), (two, two_in))
    three, across = after((three, across), acc[1])
    four = send(jnp.where(end, three, two_in), ACROSS)
    acc = multiply(acc, (THREE, THREE_ACROSS), (three, across))
    four = after(four, acc[1])
    hidden = multiply(acc, (FOUR,), (four,), last=True)[0]

    narrow = lambda x: x.astype(jnp.bfloat16)
    wide = lambda x: x.astype(jnp.float32)
    zero = jnp.zeros((), jnp.float32)

    def partials(hidden, kept, sent):
        kept_jobs, sent_jobs = [(place, 0) for place in kept], [(place, 1) for place in sent]
        outs = down(me, kept_jobs, sent_jobs, hidden, down_weight, width)
        return [*outs[: len(kept)], *(wide(swap(x)) for x in outs[len(kept) :])]

    their_four, their_three, their_across = partials(hidden, (), (FOUR, THREE, THREE_ACROSS))
    (four,) = partials(hidden, (FOUR,), ())
    four = narrow(four + their_four)
    got = wide(send(four, ACROSS))
    three, across, their_two, their_in = partials(
        after(hidden, four), (THREE, THREE_ACROSS), (TWO, TWO_IN)
    )
    across = narrow(across + their_across)
    got_across = wide(send(across, ACROSS))
    three = narrow(three + their_three + jnp.where(end, got, zero))
    got_three = wide(send(three, ALONG))
    two, two_in, their_one, their_one_in = partials(
        after(hidden, three, across), (TWO, TWO_IN), (ONE, ONE_IN)
    )
    two = narrow(two + their_two + jnp.where(end, got_across, zero))
    got_two = wide(send(two, ALONG))
    two_in = narrow(two_in + their_in + jnp.where(end, zero, got) + got_three)
    got_in = wide(send(two_in, INSIDE))
    one, one_in, their_own = partials(after(hidden, two, two_in), (ONE, ONE_IN), (OWN,))
    one_in = narrow(one_in + their_one_in + jnp.where(end, zero, got_across) + got_two)
    got_one_in = wide(send(one_in, INSIDE))
    one = narrow(one + their_one + got_in)
    got_one = wide(send(one, ALONG))
    (kept,) = partials(after(hidden, one, one_in), (OWN,), ())
    branch = kept + their_own
    return (resident + branch + got_one + got_one_in).astype(jnp.bfloat16)


def plain(activations, norm_gain, gate_weight, up_weight, down_weight):
    resident = activations.astype(jnp.float32)
    totals = lax.psum(jnp.sum(resident * resident, axis=1), "gx")
    factor = lax.rsqrt(totals / (resident.shape[1] * lax.axis_size("gx")) + epsilon)
    normed = (resident * factor[:, None] * norm_gain.astype(jnp.float32)[None, :]).astype(
        jnp.bfloat16
    )
    pieces = lax.all_gather(normed, "gx", axis=1, tiled=True)
    gate_sum = jnp.dot(pieces, gate_weight, preferred_element_type=jnp.float32)
    up_sum = jnp.dot(pieces, up_weight, preferred_element_type=jnp.float32)
    hidden = (jax.nn.silu(gate_sum) * up_sum).astype(jnp.bfloat16)
    summed = lax.psum_scatter(
        lax.dot_general(
            down_weight, hidden, (((0,), (1,)), ((), ())), preferred_element_type=jnp.float32
        ),
        "gx",
        scatter_dimension=0,
        tiled=True,
    )
    return (resident + summed.T).astype(jnp.bfloat16)


def per_device(n, activations, norm_gain, gate_weight, up_weight, down_weight):
    args = (activations, norm_gain, gate_weight, up_weight, down_weight)
    rows, width = activations.shape
    tiled = rows % 128 == 0 and width % 256 == 0 and gate_weight.shape[1] % 256 == 128
    tiled = tiled and rows <= width
    if n == 4 * LINE and tiled:
        return overlapped(*args)
    return plain(*args)


def solution(mesh):
    in_specs = (P("groups", "gx"), P("gx"), P(None, "gx"), P(None, "gx"), P("gx", None))
    out_specs = P("groups", "gx")
    return jax.shard_map(
        functools.partial(per_device, mesh.shape["gx"]),
        mesh=mesh,
        in_specs=in_specs,
        out_specs=out_specs,
        check_vma=False,
    )
```

```python
import functools

import jax
import jax.numpy as jnp
import numpy as np
from jax import lax
from jax.experimental import pallas as pl
from jax.experimental.pallas import tpu as pltpu
from jax.sharding import PartitionSpec as P

epsilon = 1e-05
LINE = 4
EXTRA = 16
VMEM_LIMIT = 36 * 1024 * 1024
PREPARE_LIMIT = 60 * 1024 * 1024

ALONG = (lambda z, y: (z ^ 1, y),) * 2
INSIDE = (lambda z, y: (z, y ^ 1), lambda z, y: (z ^ 3, y))
ACROSS = (lambda z, y: (z, y ^ 1),) * 2

TAKEN = np.array([(0, 2, 1, 4, 3, 6, 5, 7), (0, 2, 6, 3, 4, 1, 7, 5)], np.int32)


def send(x, move):
    pairs = []
    for z in range(LINE):
        for y in range(2):
            to_z, to_y = move[0 < z < LINE - 1](z, y)
            pairs += [(z * 4 + y * 2 + c, to_z * 4 + to_y * 2 + c) for c in range(2)]
    return lax.ppermute(x, "gx", pairs)


def swap(x):
    return lax.ppermute(x, "gx", [(i, i ^ 1) for i in range(4 * LINE)])


def after(x, *others):
    return lax.optimization_barrier((x, *others))[0]


def block(me, jobs, s):
    def pick(table):
        value = jnp.int32(table[0])
        for i, entry in enumerate(table[1:], 1):
            value = jnp.where(s == i, jnp.int32(entry), value)
        return value

    places, others = zip(*jobs)
    end = (((me >> 2) ^ (me >> 3)) & 1) == 0
    code = jnp.where(end, pick(TAKEN[0, places]), pick(TAKEN[1, places]))
    return ((me >> 1) ^ code) * 2 + ((me & 1) ^ pick(others))


def prepare_body(x_ref, gain_ref, out_ref):
    rows, width = x_ref.shape
    x = x_ref[...].astype(jnp.float32)
    gain = gain_ref[...].astype(jnp.float32).reshape(1, width)
    out_ref[0, :rows, :] = (x * gain).astype(jnp.bfloat16)
    squares = jnp.broadcast_to(jnp.sum(x * x, axis=1, keepdims=True), (rows, 128)).T[:EXTRA]
    row = lax.broadcasted_iota(jnp.int32, (EXTRA, rows), 0)
    parts = jnp.zeros((EXTRA, rows), jnp.float32)
    for i in range(3):
        part = squares.astype(jnp.bfloat16).astype(jnp.float32)
        parts = jnp.where(row == i, part, parts)
        squares = squares - part
    out_ref[0, rows:, :rows] = parts.astype(jnp.bfloat16)
    if rows < width:
        out_ref[0, rows:, rows:] = jnp.zeros((EXTRA, width - rows), jnp.bfloat16)


def prepare(activations, norm_gain):
    rows, width = activations.shape
    return pl.pallas_call(
        prepare_body,
        out_shape=jax.ShapeDtypeStruct((1, rows + EXTRA, width), jnp.bfloat16),
        compiler_params=pltpu.CompilerParams(vmem_limit_bytes=PREPARE_LIMIT),
        name="prepare",
    )(activations, norm_gain)


def gate_up_body(count, first, last, rows, main, features, me_ref, *refs):
    blocks = refs[:count]
    if last:
        *refs, buffer_ref, sems = refs
    gate_ref, up_ref, *rest = refs[count:]
    if not first:
        before = rest[:4]
        rest = rest[4:]
    if last:
        down_ref, hidden_ref, *rest = rest
        *outs, _, _, _, _ = rest
        rest = rest[len(outs) :]
        width = outs[0].shape[1]
        copies = []
        for i, job in enumerate(last):
            column = pl.multiple_of(block(me_ref[0], [job], 0) * width, width)
            at = pl.ds(i * width, width)
            copies.append(
                pltpu.make_async_copy(
                    down_ref.at[:, pl.ds(column, width)], buffer_ref.at[:, at], sems.at[i]
                )
            )
    accs = rest
    step = pl.program_id(0)

    if last:

        @pl.when(step == 0)
        def _():
            for copy in copies:
                copy.start()

    for s in range(count):

        @pl.when(step == s)
        def _(s=s):
            x = blocks[s][0, :rows, :]
            gate, up = gate_ref[...], up_ref[...]
            mixed = jnp.concatenate([gate[:, main:], up[:, main:]], axis=1)
            values = [
                jnp.dot(x, weight, preferred_element_type=jnp.float32)
                for weight in (gate[:, :main], up[:, :main], mixed)
            ]
            squares = blocks[s][0, rows:, :].astype(jnp.float32)
            squares = jnp.sum(squares, axis=0, keepdims=True)
            values.append(jnp.broadcast_to(squares, accs[3].shape))
            if s:
                values = [acc[...] + value for acc, value in zip(accs, values)]
            elif not first:
                values = [old[...] + value for old, value in zip(before, values)]
            if not last or s < count - 1:
                for acc, value in zip(accs, values):
                    acc[...] = value
                return
            factor = lax.rsqrt(values[3][:1, :rows] / features + epsilon)
            factor = jnp.broadcast_to(factor, (128, rows)).T[:, :1]

            def act(g, u):
                g, u = g * factor, u * factor
                return (g / (1.0 + jnp.exp(-g)) * u).astype(jnp.bfloat16)

            gate, up, both, _ = values
            rem = both.shape[1] // 2
            hidden_ref[:, :main] = act(gate, up)
            hidden_ref[:, main:] = act(both[:, :rem], both[:, rem:])
            for i in range(0, len(outs), 2):
                pair = slice(i, i + 2)
                for copy in copies[pair]:
                    copy.wait()
                value = down_block(hidden_ref, buffer_ref.at[:, i * width : (i + 2) * width])
                for n, out in enumerate(outs[pair]):
                    out[...] = value[:, n * width : (n + 1) * width].astype(out.dtype)


def gate_up(me, jobs, shards, gate_weight, up_weight, acc, last=(), kinds=(), down_weight=None):
    height, depth = shards[0][0].shape[1:]
    count = len(jobs)
    rows = height - EXTRA
    features, ff = gate_weight.shape
    main = ff // 256 * 256 if ff % 256 else ff - 256
    rem = ff - main
    first = acc is None
    whole = lambda shape: pl.BlockSpec(shape, lambda s, me: (0, 0))
    weight = pl.BlockSpec((depth, ff), lambda s, me: (block(me[0], jobs, s), 0))
    shard = lambda i: pl.BlockSpec((1, height, depth), lambda s, me: (i, 0, 0))
    in_specs = [shard(i) for _, i in shards] + [weight, weight]
    args = [*(x for x, _ in shards), gate_weight, up_weight]
    shapes = [(rows, main), (rows, main), (rows, 2 * rem), (8, depth)]
    if not first:
        in_specs += [whole(s) for s in shapes]
        args += list(acc)
    if last:
        in_specs += [pl.BlockSpec(memory_space=pl.ANY)]
        args += [down_weight]
        out_shape = [jax.ShapeDtypeStruct((rows, ff), jnp.bfloat16)]
        out_shape += [jax.ShapeDtypeStruct((rows, depth), kind) for kind in kinds]
        out_specs = [whole(x.shape) for x in out_shape]
        scratch = [pltpu.VMEM(s, jnp.float32) for s in shapes]
        scratch += [
            pltpu.VMEM((ff, len(last) * depth), jnp.bfloat16),
            pltpu.SemaphoreType.DMA((len(last),)),
        ]
    else:
        out_shape = [jax.ShapeDtypeStruct(s, jnp.float32) for s in shapes]
        out_specs = [whole(s) for s in shapes]
        scratch = []
    return pl.pallas_call(
        functools.partial(gate_up_body, count, first, last, rows, main, features),
        grid_spec=pltpu.PrefetchScalarGridSpec(
            num_scalar_prefetch=1,
            grid=(count,),
            in_specs=in_specs,
            out_specs=out_specs,
            scratch_shapes=scratch,
        ),
        out_shape=out_shape,
        compiler_params=pltpu.CompilerParams(vmem_limit_bytes=VMEM_LIMIT),
        cost_estimate=pl.CostEstimate(
            flops=4 * rows * depth * count * ff // 8,
            bytes_accessed=4 * depth * count * ff // 8,
            transcendentals=0,
        ),
        name="gate_up",
    )(me, *args)


def down_block(hidden_ref, weight_ref):
    ff = hidden_ref.shape[1]
    main = ff // 256 * 256
    value = jnp.dot(
        hidden_ref[:, :main], weight_ref[:main, :], preferred_element_type=jnp.float32
    )
    if main < ff:
        value = value + jnp.dot(
            hidden_ref[:, main:], weight_ref[main:, :], preferred_element_type=jnp.float32
        )
    return value


def down_body(kept, sent, me_ref, hidden_ref, weight_ref, *outs):
    now = pl.program_id(0)
    value = down_block(hidden_ref, weight_ref)
    for s in range(kept):

        @pl.when(now == s)
        def _(out=outs[s]):
            out[...] = value

    for s in range(kept, kept + sent):

        @pl.when(now == s)
        def _(out=outs[s]):
            out[...] = value.astype(jnp.bfloat16)


def down(me, kept, sent, hidden, down_weight, width):
    rows, ff = hidden.shape
    jobs = kept + sent
    kinds = [jnp.float32] * len(kept) + [jnp.bfloat16] * len(sent)
    return pl.pallas_call(
        functools.partial(down_body, len(kept), len(sent)),
        grid_spec=pltpu.PrefetchScalarGridSpec(
            num_scalar_prefetch=1,
            grid=(len(jobs),),
            in_specs=[
                pl.BlockSpec((rows, ff), lambda s, me: (0, 0)),
                pl.BlockSpec((ff, width), lambda s, me: (0, block(me[0], jobs, s))),
            ],
            out_specs=[pl.BlockSpec((rows, width), lambda s, me: (0, 0))] * len(jobs),
        ),
        out_shape=[jax.ShapeDtypeStruct((rows, width), kind) for kind in kinds],
        compiler_params=pltpu.CompilerParams(vmem_limit_bytes=VMEM_LIMIT),
        cost_estimate=pl.CostEstimate(
            flops=rows * ff * width * len(jobs) // 4,
            bytes_accessed=ff * width * len(jobs) // 4,
            transcendentals=0,
        ),
        name="down",
    )(me, hidden, down_weight)


def overlapped(activations, norm_gain, gate_weight, up_weight, down_weight):
    width = activations.shape[1]
    index = lax.axis_index("gx").astype(jnp.int32)
    me = index[None]
    z = index >> 2
    end = (z == 0) | (z == LINE - 1)
    resident = activations.astype(jnp.float32)
    OWN, ONE, ONE_IN, TWO, TWO_IN, THREE, THREE_ACROSS, FOUR = range(8)

    def multiply(acc, places, shards, *more):
        theirs = swap(shards[0] if len(shards) == 1 else jnp.concatenate(shards))
        jobs = [(place, 0) for place in places] + [(place, 1) for place in places]
        arrays = [(x, 0) for x in shards] + [(theirs, i) for i in range(len(places))]
        return gate_up(me, jobs, arrays, gate_weight, up_weight, acc, *more)

    early, end = lax.optimization_barrier((activations, end))
    own = prepare(early, norm_gain)
    one, one_in = send(own, ALONG), send(own, INSIDE)
    acc = multiply(None, (OWN,), (own,))
    one, one_in = after((one, one_in), acc[3])
    two, two_in = send(one_in, ALONG), send(one, INSIDE)
    acc = multiply(acc, (ONE, ONE_IN), (one, one_in))
    two, two_in = after((two, two_in), acc[3])
    three, across = send(two_in, ALONG), send(jnp.where(end, two, one_in), ACROSS)
    acc = multiply(acc, (TWO, TWO_IN), (two, two_in))
    three, across = after((three, across), acc[3])
    four = send(jnp.where(end, three, two_in), ACROSS)
    acc = multiply(acc, (THREE, THREE_ACROSS), (three, across))
    four = after(four, acc[3])
    narrow_kind = jnp.bfloat16
    hidden, their_four, four, their_three, their_across = multiply(
        acc,
        (FOUR,),
        (four,),
        ((FOUR, 1), (FOUR, 0), (THREE, 1), (THREE_ACROSS, 1)),
        (narrow_kind, jnp.float32, narrow_kind, narrow_kind),
        down_weight,
    )

    narrow = lambda x: x.astype(jnp.bfloat16)
    wide = lambda x: x.astype(jnp.float32)
    zero = jnp.zeros((), jnp.float32)

    def partials(hidden, kept, sent):
        kept_jobs, sent_jobs = [(place, 0) for place in kept], [(place, 1) for place in sent]
        outs = down(me, kept_jobs, sent_jobs, hidden, down_weight, width)
        return [*outs[: len(kept)], *(wide(swap(x)) for x in outs[len(kept) :])]

    their_four, their_three, their_across = (
        wide(swap(x)) for x in (their_four, their_three, their_across)
    )
    four = narrow(four + their_four)
    got = wide(send(four, ACROSS))
    three, across, their_two, their_in = partials(
        after(hidden, four), (THREE, THREE_ACROSS), (TWO, TWO_IN)
    )
    across = narrow(across + their_across)
    got_across = wide(send(across, ACROSS))
    three = narrow(three + their_three + jnp.where(end, got, zero))
    got_three = wide(send(three, ALONG))
    two, two_in, their_one, their_one_in = partials(
        after(hidden, three, across), (TWO, TWO_IN), (ONE, ONE_IN)
    )
    two = narrow(two + their_two + jnp.where(end, got_across, zero))
    got_two = wide(send(two, ALONG))
    two_in = narrow(two_in + their_in + jnp.where(end, zero, got) + got_three)
    got_in = wide(send(two_in, INSIDE))
    one, one_in, their_own = partials(after(hidden, two, two_in), (ONE, ONE_IN), (OWN,))
    one_in = narrow(one_in + their_one_in + jnp.where(end, zero, got_across) + got_two)
    got_one_in = wide(send(one_in, INSIDE))
    one = narrow(one + their_one + got_in)
    got_one = wide(send(one, ALONG))
    (kept,) = partials(after(hidden, one, one_in), (OWN,), ())
    branch = kept + their_own
    return (resident + branch + got_one + got_one_in).astype(jnp.bfloat16)


def plain(activations, norm_gain, gate_weight, up_weight, down_weight):
    resident = activations.astype(jnp.float32)
    totals = lax.psum(jnp.sum(resident * resident, axis=1), "gx")
    factor = lax.rsqrt(totals / (resident.shape[1] * lax.axis_size("gx")) + epsilon)
    normed = (resident * factor[:, None] * norm_gain.astype(jnp.float32)[None, :]).astype(
        jnp.bfloat16
    )
    pieces = lax.all_gather(normed, "gx", axis=1, tiled=True)
    gate_sum = jnp.dot(pieces, gate_weight, preferred_element_type=jnp.float32)
    up_sum = jnp.dot(pieces, up_weight, preferred_element_type=jnp.float32)
    hidden = (jax.nn.silu(gate_sum) * up_sum).astype(jnp.bfloat16)
    summed = lax.psum_scatter(
        lax.dot_general(
            down_weight, hidden, (((0,), (1,)), ((), ())), preferred_element_type=jnp.float32
        ),
        "gx",
        scatter_dimension=0,
        tiled=True,
    )
    return (resident + summed.T).astype(jnp.bfloat16)


def per_device(n, activations, norm_gain, gate_weight, up_weight, down_weight):
    args = (activations, norm_gain, gate_weight, up_weight, down_weight)
    rows, width = activations.shape
    tiled = rows % 128 == 0 and width % 128 == 0 and gate_weight.shape[1] % 128 == 0
    tiled = tiled and rows <= width
    if n == 4 * LINE and tiled:
        return overlapped(*args)
    return plain(*args)


def solution(mesh):
    in_specs = (P("groups", "gx"), P("gx"), P(None, "gx"), P(None, "gx"), P("gx", None))
    out_specs = P("groups", "gx")
    return jax.shard_map(
        functools.partial(per_device, mesh.shape["gx"]),
        mesh=mesh,
        in_specs=in_specs,
        out_specs=out_specs,
        check_vma=False,
    )
```

```python
import functools

import jax
import jax.numpy as jnp
import numpy as np
from jax import lax
from jax.experimental import pallas as pl
from jax.experimental.pallas import tpu as pltpu
from jax.sharding import PartitionSpec as P

epsilon = 1e-05
LINE = 4
EXTRA = 16
VMEM_LIMIT = 36 * 1024 * 1024
PREPARE_LIMIT = 60 * 1024 * 1024

ALONG = (lambda z, y: (z ^ 1, y),) * 2
INSIDE = (lambda z, y: (z, y ^ 1), lambda z, y: (z ^ 3, y))
ACROSS = (lambda z, y: (z, y ^ 1),) * 2

TAKEN = np.array([(0, 2, 1, 4, 3, 6, 5, 7), (0, 2, 6, 3, 4, 1, 7, 5)], np.int32)


def send(x, move):
    pairs = []
    for z in range(LINE):
        for y in range(2):
            to_z, to_y = move[0 < z < LINE - 1](z, y)
            pairs += [(z * 4 + y * 2 + c, to_z * 4 + to_y * 2 + c) for c in range(2)]
    return lax.ppermute(x, "gx", pairs)


def swap(x):
    return lax.ppermute(x, "gx", [(i, i ^ 1) for i in range(4 * LINE)])


def after(x, *others):
    return lax.optimization_barrier((x, *others))[0]


def block(me, jobs, s):
    def pick(table):
        value = jnp.int32(table[0])
        for i, entry in enumerate(table[1:], 1):
            value = jnp.where(s == i, jnp.int32(entry), value)
        return value

    places, others = zip(*jobs)
    end = (((me >> 2) ^ (me >> 3)) & 1) == 0
    code = jnp.where(end, pick(TAKEN[0, places]), pick(TAKEN[1, places]))
    return ((me >> 1) ^ code) * 2 + ((me & 1) ^ pick(others))


def prepare_body(x_ref, gain_ref, out_ref):
    rows, width = x_ref.shape
    x = x_ref[...].astype(jnp.float32)
    gain = gain_ref[...].astype(jnp.float32).reshape(1, width)
    out_ref[0, :rows, :] = (x * gain).astype(jnp.bfloat16)
    squares = jnp.broadcast_to(jnp.sum(x * x, axis=1, keepdims=True), (rows, 128)).T[:EXTRA]
    row = lax.broadcasted_iota(jnp.int32, (EXTRA, rows), 0)
    parts = jnp.zeros((EXTRA, rows), jnp.float32)
    for i in range(3):
        part = squares.astype(jnp.bfloat16).astype(jnp.float32)
        parts = jnp.where(row == i, part, parts)
        squares = squares - part
    out_ref[0, rows:, :rows] = parts.astype(jnp.bfloat16)
    if rows < width:
        out_ref[0, rows:, rows:] = jnp.zeros((EXTRA, width - rows), jnp.bfloat16)


def prepare(activations, norm_gain):
    rows, width = activations.shape
    return pl.pallas_call(
        prepare_body,
        out_shape=jax.ShapeDtypeStruct((1, rows + EXTRA, width), jnp.bfloat16),
        compiler_params=pltpu.CompilerParams(vmem_limit_bytes=PREPARE_LIMIT),
        name="prepare",
    )(activations, norm_gain)


def gate_up_body(count, first, last, rows, main, features, me_ref, *refs):
    blocks = refs[:count]
    if last:
        *refs, buffer_ref, sems = refs
    gate_ref, up_ref, *rest = refs[count:]
    if not first:
        before = rest[:4]
        rest = rest[4:]
    if last:
        down_ref, hidden_ref, *rest = rest
        *outs, _, _, _, _ = rest
        rest = rest[len(outs) :]
        width = outs[0].shape[1]
        copies = []
        for i, job in enumerate(last):
            column = pl.multiple_of(block(me_ref[0], [job], 0) * width, width)
            at = pl.ds(i * width, width)
            copies.append(
                pltpu.make_async_copy(
                    down_ref.at[:, pl.ds(column, width)], buffer_ref.at[:, at], sems.at[i]
                )
            )
    accs = rest
    step = pl.program_id(0)

    if last:

        @pl.when(step == 0)
        def _():
            for copy in copies:
                copy.start()

    for s in range(count):

        @pl.when(step == s)
        def _(s=s):
            x = blocks[s][0, :rows, :]
            gate, up = gate_ref[...], up_ref[...]
            mixed = jnp.concatenate([gate[:, main:], up[:, main:]], axis=1)
            values = [
                jnp.dot(x, weight, preferred_element_type=jnp.float32)
                for weight in (gate[:, :main], up[:, :main], mixed)
            ]
            squares = blocks[s][0, rows:, :].astype(jnp.float32)
            squares = jnp.sum(squares, axis=0, keepdims=True)
            values.append(jnp.broadcast_to(squares, accs[3].shape))
            if s:
                values = [acc[...] + value for acc, value in zip(accs, values)]
            elif not first:
                values = [old[...] + value for old, value in zip(before, values)]
            if not last or s < count - 1:
                for acc, value in zip(accs, values):
                    acc[...] = value
                return
            factor = lax.rsqrt(values[3][:1, :rows] / features + epsilon)
            factor = jnp.broadcast_to(factor, (128, rows)).T[:, :1]

            def act(g, u):
                g, u = g * factor, u * factor
                return (g / (1.0 + jnp.exp(-g)) * u).astype(jnp.bfloat16)

            gate, up, both, _ = values
            rem = both.shape[1] // 2
            hidden_ref[:, :main] = act(gate, up)
            hidden_ref[:, main:] = act(both[:, :rem], both[:, rem:])
            for i in range(0, len(outs), 2):
                pair = slice(i, i + 2)
                for copy in copies[pair]:
                    copy.wait()
                value = down_block(hidden_ref, buffer_ref.at[:, i * width : (i + 2) * width])
                for n, out in enumerate(outs[pair]):
                    out[...] = value[:, n * width : (n + 1) * width].astype(out.dtype)


def gate_up(me, jobs, shards, gate_weight, up_weight, acc, last=(), kinds=(), down_weight=None):
    height, depth = shards[0][0].shape[1:]
    count = len(jobs)
    rows = height - EXTRA
    features, ff = gate_weight.shape
    main = ff // 256 * 256 if ff % 256 else ff - 256
    rem = ff - main
    first = acc is None
    whole = lambda shape: pl.BlockSpec(shape, lambda s, me: (0, 0))
    weight = pl.BlockSpec((depth, ff), lambda s, me: (block(me[0], jobs, s), 0))
    shard = lambda i: pl.BlockSpec((1, height, depth), lambda s, me: (i, 0, 0))
    in_specs = [shard(i) for _, i in shards] + [weight, weight]
    args = [*(x for x, _ in shards), gate_weight, up_weight]
    shapes = [(rows, main), (rows, main), (rows, 2 * rem), (8, depth)]
    if not first:
        in_specs += [whole(s) for s in shapes]
        args += list(acc)
    if last:
        in_specs += [pl.BlockSpec(memory_space=pl.ANY)]
        args += [down_weight]
        out_shape = [jax.ShapeDtypeStruct((rows, ff), jnp.bfloat16)]
        out_shape += [jax.ShapeDtypeStruct((rows, depth), kind) for kind in kinds]
        out_specs = [whole(x.shape) for x in out_shape]
        scratch = [pltpu.VMEM(s, jnp.float32) for s in shapes]
        scratch += [
            pltpu.VMEM((ff, len(last) * depth), jnp.bfloat16),
            pltpu.SemaphoreType.DMA((len(last),)),
        ]
    else:
        out_shape = [jax.ShapeDtypeStruct(s, jnp.float32) for s in shapes]
        out_specs = [whole(s) for s in shapes]
        scratch = []
    return pl.pallas_call(
        functools.partial(gate_up_body, count, first, last, rows, main, features),
        grid_spec=pltpu.PrefetchScalarGridSpec(
            num_scalar_prefetch=1,
            grid=(count,),
            in_specs=in_specs,
            out_specs=out_specs,
            scratch_shapes=scratch,
        ),
        out_shape=out_shape,
        compiler_params=pltpu.CompilerParams(vmem_limit_bytes=VMEM_LIMIT),
        cost_estimate=pl.CostEstimate(
            flops=4 * rows * depth * count * ff // 8,
            bytes_accessed=4 * depth * count * ff // 8,
            transcendentals=0,
        ),
        name="gate_up",
    )(me, *args)


def down_block(hidden_ref, weight_ref):
    ff = hidden_ref.shape[1]
    main = ff // 256 * 256
    value = jnp.dot(
        hidden_ref[:, :main], weight_ref[:main, :], preferred_element_type=jnp.float32
    )
    if main < ff:
        value = value + jnp.dot(
            hidden_ref[:, main:], weight_ref[main:, :], preferred_element_type=jnp.float32
        )
    return value


def down_body(kept, sent, me_ref, hidden_ref, weight_ref, *outs):
    now = pl.program_id(0)
    value = down_block(hidden_ref, weight_ref)
    for s in range(kept):

        @pl.when(now == s)
        def _(out=outs[s]):
            out[...] = value

    for s in range(kept, kept + sent):

        @pl.when(now == s)
        def _(out=outs[s]):
            out[...] = value.astype(jnp.bfloat16)


def down(me, kept, sent, hidden, down_weight, width):
    rows, ff = hidden.shape
    jobs = kept + sent
    kinds = [jnp.float32] * len(kept) + [jnp.bfloat16] * len(sent)
    return pl.pallas_call(
        functools.partial(down_body, len(kept), len(sent)),
        grid_spec=pltpu.PrefetchScalarGridSpec(
            num_scalar_prefetch=1,
            grid=(len(jobs),),
            in_specs=[
                pl.BlockSpec((rows, ff), lambda s, me: (0, 0)),
                pl.BlockSpec((ff, width), lambda s, me: (0, block(me[0], jobs, s))),
            ],
            out_specs=[pl.BlockSpec((rows, width), lambda s, me: (0, 0))] * len(jobs),
        ),
        out_shape=[jax.ShapeDtypeStruct((rows, width), kind) for kind in kinds],
        compiler_params=pltpu.CompilerParams(vmem_limit_bytes=VMEM_LIMIT),
        cost_estimate=pl.CostEstimate(
            flops=rows * ff * width * len(jobs) // 4,
            bytes_accessed=ff * width * len(jobs) // 4,
            transcendentals=0,
        ),
        name="down",
    )(me, hidden, down_weight)


def overlapped(activations, norm_gain, gate_weight, up_weight, down_weight):
    width = activations.shape[1]
    index = lax.axis_index("gx").astype(jnp.int32)
    me = index[None]
    z = index >> 2
    end = (z == 0) | (z == LINE - 1)
    resident = activations.astype(jnp.float32)
    OWN, ONE, ONE_IN, TWO, TWO_IN, THREE, THREE_ACROSS, FOUR = range(8)

    def multiply(acc, places, shards, *more):
        theirs = swap(shards[0] if len(shards) == 1 else jnp.concatenate(shards))
        jobs = [(place, 0) for place in places] + [(place, 1) for place in places]
        arrays = [(x, 0) for x in shards] + [(theirs, i) for i in range(len(places))]
        return gate_up(me, jobs, arrays, gate_weight, up_weight, acc, *more)

    early, end = lax.optimization_barrier((activations, end))
    own = prepare(early, norm_gain)
    one, one_in = send(own, ALONG), send(own, INSIDE)
    acc = multiply(None, (OWN,), (own,))
    one, one_in = after((one, one_in), acc[3])
    two, two_in = send(one_in, ALONG), send(one, INSIDE)
    acc = multiply(acc, (ONE, ONE_IN), (one, one_in))
    two, two_in = after((two, two_in), acc[3])
    three, across = send(two_in, ALONG), send(jnp.where(end, two, one_in), ACROSS)
    acc = multiply(acc, (TWO, TWO_IN), (two, two_in))
    three, across = after((three, across), acc[3])
    four = send(jnp.where(end, three, two_in), ACROSS)
    acc = multiply(acc, (THREE, THREE_ACROSS), (three, across))
    four = after(four, acc[3])
    narrow_kind = jnp.bfloat16
    hidden, their_four, four, their_three, their_across = multiply(
        acc,
        (FOUR,),
        (four,),
        ((FOUR, 1), (FOUR, 0), (THREE, 1), (THREE_ACROSS, 1)),
        (narrow_kind, jnp.float32, narrow_kind, narrow_kind),
        down_weight,
    )

    narrow = lambda x: x.astype(jnp.bfloat16)
    wide = lambda x: x.astype(jnp.float32)
    zero = jnp.zeros((), jnp.float32)

    def partials(hidden, kept, sent):
        kept_jobs, sent_jobs = [(place, 0) for place in kept], [(place, 1) for place in sent]
        outs = down(me, kept_jobs, sent_jobs, hidden, down_weight, width)
        return [*outs[: len(kept)], *(wide(swap(x)) for x in outs[len(kept) :])]

    their_four, their_three, their_across = (
        wide(swap(x)) for x in (their_four, their_three, their_across)
    )
    four = narrow(four + their_four)
    got = wide(send(four, ACROSS))
    three, across, their_two, their_in = partials(
        after(hidden, four), (THREE, THREE_ACROSS), (TWO, TWO_IN)
    )
    three = narrow(three + their_three + jnp.where(end, got, zero))
    got_three = wide(send(three, ALONG))
    across = narrow(across + after(their_across, three))
    got_across = wide(send(across, ACROSS))
    two, two_in, their_one, their_one_in = partials(
        after(hidden, three, across), (TWO, TWO_IN), (ONE, ONE_IN)
    )
    two_in = narrow(two_in + their_in + jnp.where(end, zero, got) + got_three)
    got_in = wide(send(two_in, INSIDE))
    two = narrow(two + after(their_two, two_in) + jnp.where(end, got_across, zero))
    got_two = wide(send(two, ALONG))
    one, one_in, their_own = partials(after(hidden, two, two_in), (ONE, ONE_IN), (OWN,))
    one = narrow(one + their_one + got_in)
    got_one = wide(send(one, ALONG))
    one_in = narrow(one_in + after(their_one_in, one) + jnp.where(end, zero, got_across) + got_two)
    got_one_in = wide(send(one_in, INSIDE))
    (kept,) = partials(after(hidden, one, one_in), (OWN,), ())
    branch = kept + their_own
    return (resident + branch + got_one + got_one_in).astype(jnp.bfloat16)


def plain(activations, norm_gain, gate_weight, up_weight, down_weight):
    resident = activations.astype(jnp.float32)
    totals = lax.psum(jnp.sum(resident * resident, axis=1), "gx")
    factor = lax.rsqrt(totals / (resident.shape[1] * lax.axis_size("gx")) + epsilon)
    normed = (resident * factor[:, None] * norm_gain.astype(jnp.float32)[None, :]).astype(
        jnp.bfloat16
    )
    pieces = lax.all_gather(normed, "gx", axis=1, tiled=True)
    gate_sum = jnp.dot(pieces, gate_weight, preferred_element_type=jnp.float32)
    up_sum = jnp.dot(pieces, up_weight, preferred_element_type=jnp.float32)
    hidden = (jax.nn.silu(gate_sum) * up_sum).astype(jnp.bfloat16)
    summed = lax.psum_scatter(
        lax.dot_general(
            down_weight, hidden, (((0,), (1,)), ((), ())), preferred_element_type=jnp.float32
        ),
        "gx",
        scatter_dimension=0,
        tiled=True,
    )
    return (resident + summed.T).astype(jnp.bfloat16)


def per_device(n, activations, norm_gain, gate_weight, up_weight, down_weight):
    args = (activations, norm_gain, gate_weight, up_weight, down_weight)
    rows, width = activations.shape
    tiled = rows % 128 == 0 and width % 128 == 0 and gate_weight.shape[1] % 128 == 0
    tiled = tiled and rows <= width
    if n == 4 * LINE and tiled:
        return overlapped(*args)
    return plain(*args)


def solution(mesh):
    in_specs = (P("groups", "gx"), P("gx"), P(None, "gx"), P(None, "gx"), P("gx", None))
    out_specs = P("groups", "gx")
    return jax.shard_map(
        functools.partial(per_device, mesh.shape["gx"]),
        mesh=mesh,
        in_specs=in_specs,
        out_specs=out_specs,
        check_vma=False,
    )
```

```python
import functools

import jax
import jax.numpy as jnp
import numpy as np
from jax import lax
from jax.experimental import pallas as pl
from jax.experimental.pallas import tpu as pltpu
from jax.sharding import PartitionSpec as P

epsilon = 1e-05
LINE = 4
EXTRA = 16
VMEM_LIMIT = 36 * 1024 * 1024
PREPARE_LIMIT = 60 * 1024 * 1024

ALONG = (lambda z, y: (z ^ 1, y),) * 2
INSIDE = (lambda z, y: (z, y ^ 1), lambda z, y: (z ^ 3, y))
ACROSS = (lambda z, y: (z, y ^ 1),) * 2

TAKEN = np.array([(0, 2, 1, 4, 3, 6, 5, 7), (0, 2, 6, 3, 4, 1, 7, 5)], np.int32)


def send(x, move):
    pairs = []
    for z in range(LINE):
        for y in range(2):
            to_z, to_y = move[0 < z < LINE - 1](z, y)
            pairs += [(z * 4 + y * 2 + c, to_z * 4 + to_y * 2 + c) for c in range(2)]
    return lax.ppermute(x, "gx", pairs)


def swap(x):
    return lax.ppermute(x, "gx", [(i, i ^ 1) for i in range(4 * LINE)])


def after(x, *others):
    return lax.optimization_barrier((x, *others))[0]


def block(me, jobs, s):
    def pick(table):
        value = jnp.int32(table[0])
        for i, entry in enumerate(table[1:], 1):
            value = jnp.where(s == i, jnp.int32(entry), value)
        return value

    places, others = zip(*jobs)
    end = (((me >> 2) ^ (me >> 3)) & 1) == 0
    code = jnp.where(end, pick(TAKEN[0, places]), pick(TAKEN[1, places]))
    return ((me >> 1) ^ code) * 2 + ((me & 1) ^ pick(others))


def prepare_body(x_ref, gain_ref, out_ref):
    rows, width = x_ref.shape
    x = x_ref[...].astype(jnp.float32)
    gain = gain_ref[...].astype(jnp.float32).reshape(1, width)
    out_ref[0, :rows, :] = (x * gain).astype(jnp.bfloat16)
    squares = jnp.broadcast_to(jnp.sum(x * x, axis=1, keepdims=True), (rows, 128)).T[:EXTRA]
    row = lax.broadcasted_iota(jnp.int32, (EXTRA, rows), 0)
    parts = jnp.zeros((EXTRA, rows), jnp.float32)
    for i in range(3):
        part = squares.astype(jnp.bfloat16).astype(jnp.float32)
        parts = jnp.where(row == i, part, parts)
        squares = squares - part
    out_ref[0, rows:, :rows] = parts.astype(jnp.bfloat16)
    if rows < width:
        out_ref[0, rows:, rows:] = jnp.zeros((EXTRA, width - rows), jnp.bfloat16)


def prepare(activations, norm_gain):
    rows, width = activations.shape
    return pl.pallas_call(
        prepare_body,
        out_shape=jax.ShapeDtypeStruct((1, rows + EXTRA, width), jnp.bfloat16),
        compiler_params=pltpu.CompilerParams(vmem_limit_bytes=PREPARE_LIMIT),
        name="prepare",
    )(activations, norm_gain)


def gate_up_body(count, first, last, rows, main, features, me_ref, *refs):
    blocks = refs[:count]
    if last:
        *refs, buffer_ref, sems = refs
    gate_ref, up_ref, *rest = refs[count:]
    if not first:
        before = rest[:4]
        rest = rest[4:]
    if last:
        down_ref, hidden_ref, *rest = rest
        *outs, _, _, _, _ = rest
        rest = rest[len(outs) :]
        width = outs[0].shape[1]
        copies = []
        for i, job in enumerate(last):
            column = pl.multiple_of(block(me_ref[0], [job], 0) * width, width)
            at = pl.ds(i * width, width)
            copies.append(
                pltpu.make_async_copy(
                    down_ref.at[:, pl.ds(column, width)], buffer_ref.at[:, at], sems.at[i]
                )
            )
    accs = rest
    step = pl.program_id(0)

    if last:

        @pl.when(step == 0)
        def _():
            for copy in copies:
                copy.start()

    for s in range(count):

        @pl.when(step == s)
        def _(s=s):
            x = blocks[s][0, :rows, :]
            gate, up = gate_ref[...], up_ref[...]
            mixed = jnp.concatenate([gate[:, main:], up[:, main:]], axis=1)
            values = [
                jnp.dot(x, weight, preferred_element_type=jnp.float32)
                for weight in (gate[:, :main], up[:, :main], mixed)
            ]
            squares = blocks[s][0, rows:, :].astype(jnp.float32)
            squares = jnp.sum(squares, axis=0, keepdims=True)
            values.append(jnp.broadcast_to(squares, accs[3].shape))
            if s:
                values = [acc[...] + value for acc, value in zip(accs, values)]
            elif not first:
                values = [old[...] + value for old, value in zip(before, values)]
            if not last or s < count - 1:
                for acc, value in zip(accs, values):
                    acc[...] = value
                return
            factor = lax.rsqrt(values[3][:1, :rows] / features + epsilon)
            factor = jnp.broadcast_to(factor, (128, rows)).T[:, :1]

            def act(g, u):
                g, u = g * factor, u * factor
                return (g / (1.0 + jnp.exp(-g)) * u).astype(jnp.bfloat16)

            gate, up, both, _ = values
            rem = both.shape[1] // 2
            hidden_ref[:, :main] = act(gate, up)
            hidden_ref[:, main:] = act(both[:, :rem], both[:, rem:])
            for i, (copy, out) in enumerate(zip(copies, outs)):
                copy.wait()
                value = down_block(hidden_ref, buffer_ref.at[:, i * width : (i + 1) * width])
                out[...] = value.astype(out.dtype)


def gate_up(me, jobs, shards, gate_weight, up_weight, acc, last=(), kinds=(), down_weight=None):
    height, depth = shards[0][0].shape[1:]
    count = len(jobs)
    rows = height - EXTRA
    features, ff = gate_weight.shape
    main = ff // 256 * 256 if ff % 256 else ff - 256
    rem = ff - main
    first = acc is None
    whole = lambda shape: pl.BlockSpec(shape, lambda s, me: (0, 0))
    weight = pl.BlockSpec((depth, ff), lambda s, me: (block(me[0], jobs, s), 0))
    shard = lambda i: pl.BlockSpec((1, height, depth), lambda s, me: (i, 0, 0))
    in_specs = [shard(i) for _, i in shards] + [weight, weight]
    args = [*(x for x, _ in shards), gate_weight, up_weight]
    shapes = [(rows, main), (rows, main), (rows, 2 * rem), (8, depth)]
    if not first:
        in_specs += [whole(s) for s in shapes]
        args += list(acc)
    if last:
        in_specs += [pl.BlockSpec(memory_space=pl.ANY)]
        args += [down_weight]
        out_shape = [jax.ShapeDtypeStruct((rows, ff), jnp.bfloat16)]
        out_shape += [jax.ShapeDtypeStruct((rows, depth), kind) for kind in kinds]
        out_specs = [whole(x.shape) for x in out_shape]
        scratch = [pltpu.VMEM(s, jnp.float32) for s in shapes]
        scratch += [
            pltpu.VMEM((ff, len(last) * depth), jnp.bfloat16),
            pltpu.SemaphoreType.DMA((len(last),)),
        ]
    else:
        out_shape = [jax.ShapeDtypeStruct(s, jnp.float32) for s in shapes]
        out_specs = [whole(s) for s in shapes]
        scratch = []
    return pl.pallas_call(
        functools.partial(gate_up_body, count, first, last, rows, main, features),
        grid_spec=pltpu.PrefetchScalarGridSpec(
            num_scalar_prefetch=1,
            grid=(count,),
            in_specs=in_specs,
            out_specs=out_specs,
            scratch_shapes=scratch,
        ),
        out_shape=out_shape,
        compiler_params=pltpu.CompilerParams(vmem_limit_bytes=VMEM_LIMIT),
        cost_estimate=pl.CostEstimate(
            flops=4 * rows * depth * count * ff // 8,
            bytes_accessed=4 * depth * count * ff // 8,
            transcendentals=0,
        ),
        name="gate_up",
    )(me, *args)


def down_block(hidden_ref, weight_ref):
    ff = hidden_ref.shape[1]
    main = ff // 256 * 256
    value = jnp.dot(
        hidden_ref[:, :main], weight_ref[:main, :], preferred_element_type=jnp.float32
    )
    if main < ff:
        value = value + jnp.dot(
            hidden_ref[:, main:], weight_ref[main:, :], preferred_element_type=jnp.float32
        )
    return value


def down_body(kept, sent, me_ref, hidden_ref, weight_ref, *outs):
    now = pl.program_id(0)
    value = down_block(hidden_ref, weight_ref)
    for s in range(kept):

        @pl.when(now == s)
        def _(out=outs[s]):
            out[...] = value

    for s in range(kept, kept + sent):

        @pl.when(now == s)
        def _(out=outs[s]):
            out[...] = value.astype(jnp.bfloat16)


def down(me, kept, sent, hidden, down_weight, width):
    rows, ff = hidden.shape
    jobs = kept + sent
    kinds = [jnp.float32] * len(kept) + [jnp.bfloat16] * len(sent)
    return pl.pallas_call(
        functools.partial(down_body, len(kept), len(sent)),
        grid_spec=pltpu.PrefetchScalarGridSpec(
            num_scalar_prefetch=1,
            grid=(len(jobs),),
            in_specs=[
                pl.BlockSpec((rows, ff), lambda s, me: (0, 0)),
                pl.BlockSpec((ff, width), lambda s, me: (0, block(me[0], jobs, s))),
            ],
            out_specs=[pl.BlockSpec((rows, width), lambda s, me: (0, 0))] * len(jobs),
        ),
        out_shape=[jax.ShapeDtypeStruct((rows, width), kind) for kind in kinds],
        compiler_params=pltpu.CompilerParams(vmem_limit_bytes=VMEM_LIMIT),
        cost_estimate=pl.CostEstimate(
            flops=rows * ff * width * len(jobs) // 4,
            bytes_accessed=ff * width * len(jobs) // 4,
            transcendentals=0,
        ),
        name="down",
    )(me, hidden, down_weight)


def overlapped(activations, norm_gain, gate_weight, up_weight, down_weight):
    width = activations.shape[1]
    index = lax.axis_index("gx").astype(jnp.int32)
    me = index[None]
    z = index >> 2
    end = (z == 0) | (z == LINE - 1)
    resident = activations.astype(jnp.float32)
    OWN, ONE, ONE_IN, TWO, TWO_IN, THREE, THREE_ACROSS, FOUR = range(8)

    def multiply(acc, places, shards, *more):
        theirs = swap(shards[0] if len(shards) == 1 else jnp.concatenate(shards))
        jobs = [(place, 0) for place in places] + [(place, 1) for place in places]
        arrays = [(x, 0) for x in shards] + [(theirs, i) for i in range(len(places))]
        return gate_up(me, jobs, arrays, gate_weight, up_weight, acc, *more)

    early, end = lax.optimization_barrier((activations, end))
    own = prepare(early, norm_gain)
    one, one_in = send(own, ALONG), send(own, INSIDE)
    acc = multiply(None, (OWN,), (own,))
    one, one_in = after((one, one_in), acc[3])
    two, two_in = send(one_in, ALONG), send(one, INSIDE)
    acc = multiply(acc, (ONE, ONE_IN), (one, one_in))
    two, two_in = after((two, two_in), acc[3])
    three, across = send(two_in, ALONG), send(jnp.where(end, two, one_in), ACROSS)
    acc = multiply(acc, (TWO, TWO_IN), (two, two_in))
    three, across = after((three, across), acc[3])
    four = send(jnp.where(end, three, two_in), ACROSS)
    acc = multiply(acc, (THREE, THREE_ACROSS), (three, across))
    four = after(four, acc[3])
    hidden, their_four, four = multiply(
        acc,
        (FOUR,),
        (four,),
        ((FOUR, 1), (FOUR, 0)),
        (jnp.bfloat16, jnp.float32),
        down_weight,
    )

    narrow = lambda x: x.astype(jnp.bfloat16)
    wide = lambda x: x.astype(jnp.float32)
    zero = jnp.zeros((), jnp.float32)

    def swap_halves(x):
        half = x.shape[0] // 2
        return jnp.concatenate([swap(x[:half]), swap(x[half:])])

    def partials(hidden, kept, sent, whole=0):
        kept_jobs, sent_jobs = [(place, 0) for place in kept], [(place, 1) for place in sent]
        outs = down(me, kept_jobs, sent_jobs, hidden, down_weight, width)
        cut = len(outs) - whole if whole else len(kept)
        halved = [wide(swap_halves(x)) for x in outs[len(kept) : cut]]
        return [*outs[: len(kept)], *halved, *(wide(swap(x)) for x in outs[cut:])]

    four = narrow(four + wide(swap(their_four)))
    got = wide(send(four, ACROSS))
    hidden = after(hidden, four)
    three, across, their_three, their_across, their_two, their_in = partials(
        hidden, (THREE, THREE_ACROSS), (THREE, THREE_ACROSS, TWO, TWO_IN), whole=2
    )
    three = narrow(three + their_three + jnp.where(end, got, zero))
    got_three = wide(send(three, ALONG))
    across = narrow(across + after(their_across, three))
    got_across = wide(send(across, ACROSS))
    two, two_in, their_one, their_one_in = partials(
        after(hidden, three, across), (TWO, TWO_IN), (ONE, ONE_IN)
    )
    two_in = narrow(two_in + their_in + jnp.where(end, zero, got) + got_three)
    got_in = wide(send(two_in, INSIDE))
    two = narrow(two + after(their_two, two_in) + jnp.where(end, got_across, zero))
    got_two = wide(send(two, ALONG))
    one, one_in, their_own = partials(after(hidden, two, two_in), (ONE, ONE_IN), (OWN,))
    one = narrow(one + their_one + got_in)
    got_one = wide(send(one, ALONG))
    one_in = narrow(one_in + after(their_one_in, one) + jnp.where(end, zero, got_across) + got_two)
    got_one_in = wide(send(one_in, INSIDE))
    (kept,) = partials(after(hidden, one, one_in), (OWN,), ())
    branch = kept + their_own
    return (resident + branch + got_one + got_one_in).astype(jnp.bfloat16)


def plain(activations, norm_gain, gate_weight, up_weight, down_weight):
    resident = activations.astype(jnp.float32)
    totals = lax.psum(jnp.sum(resident * resident, axis=1), "gx")
    factor = lax.rsqrt(totals / (resident.shape[1] * lax.axis_size("gx")) + epsilon)
    normed = (resident * factor[:, None] * norm_gain.astype(jnp.float32)[None, :]).astype(
        jnp.bfloat16
    )
    pieces = lax.all_gather(normed, "gx", axis=1, tiled=True)
    gate_sum = jnp.dot(pieces, gate_weight, preferred_element_type=jnp.float32)
    up_sum = jnp.dot(pieces, up_weight, preferred_element_type=jnp.float32)
    hidden = (jax.nn.silu(gate_sum) * up_sum).astype(jnp.bfloat16)
    summed = lax.psum_scatter(
        lax.dot_general(
            down_weight, hidden, (((0,), (1,)), ((), ())), preferred_element_type=jnp.float32
        ),
        "gx",
        scatter_dimension=0,
        tiled=True,
    )
    return (resident + summed.T).astype(jnp.bfloat16)


def per_device(n, activations, norm_gain, gate_weight, up_weight, down_weight):
    args = (activations, norm_gain, gate_weight, up_weight, down_weight)
    rows, width = activations.shape
    tiled = rows % 128 == 0 and width % 128 == 0 and gate_weight.shape[1] % 128 == 0
    tiled = tiled and rows <= width
    if n == 4 * LINE and tiled:
        return overlapped(*args)
    return plain(*args)


def solution(mesh):
    in_specs = (P("groups", "gx"), P("gx"), P(None, "gx"), P(None, "gx"), P("gx", None))
    out_specs = P("groups", "gx")
    return jax.shard_map(
        functools.partial(per_device, mesh.shape["gx"]),
        mesh=mesh,
        in_specs=in_specs,
        out_specs=out_specs,
        check_vma=False,
    )
```

```python
import functools

import jax
import jax.numpy as jnp
import numpy as np
from jax import lax
from jax.experimental import pallas as pl
from jax.experimental.pallas import tpu as pltpu
from jax.sharding import PartitionSpec as P

epsilon = 1e-05
LINE = 4
EXTRA = 16
VMEM_LIMIT = 36 * 1024 * 1024
PREPARE_LIMIT = 36 * 1024 * 1024

ALONG = (lambda z, y: (z ^ 1, y),) * 2
INSIDE = (lambda z, y: (z, y ^ 1), lambda z, y: (z ^ 3, y))
ACROSS = (lambda z, y: (z, y ^ 1),) * 2

TAKEN = np.array([(0, 2, 1, 4, 3, 6, 5, 7), (0, 2, 6, 3, 4, 1, 7, 5)], np.int32)


def send(x, move):
    pairs = []
    for z in range(LINE):
        for y in range(2):
            to_z, to_y = move[0 < z < LINE - 1](z, y)
            pairs += [(z * 4 + y * 2 + c, to_z * 4 + to_y * 2 + c) for c in range(2)]
    return lax.ppermute(x, "gx", pairs)


def swap(x):
    return lax.ppermute(x, "gx", [(i, i ^ 1) for i in range(4 * LINE)])


def after(x, *others):
    return lax.optimization_barrier((x, *others))[0]


def block(me, jobs, s):
    def pick(table):
        value = jnp.int32(table[0])
        for i, entry in enumerate(table[1:], 1):
            value = jnp.where(s == i, jnp.int32(entry), value)
        return value

    places, others = zip(*jobs)
    end = (((me >> 2) ^ (me >> 3)) & 1) == 0
    code = jnp.where(end, pick(TAKEN[0, places]), pick(TAKEN[1, places]))
    return ((me >> 1) ^ code) * 2 + ((me & 1) ^ pick(others))


def prepare_body(x_ref, gain_ref, out_ref):
    rows, width = x_ref.shape
    x = x_ref[...].astype(jnp.float32)
    gain = gain_ref[...].astype(jnp.float32).reshape(1, width)
    out_ref[0, :rows, :] = (x * gain).astype(jnp.bfloat16)
    squares = jnp.broadcast_to(jnp.sum(x * x, axis=1, keepdims=True), (rows, 128)).T[:EXTRA]
    row = lax.broadcasted_iota(jnp.int32, (EXTRA, rows), 0)
    parts = jnp.zeros((EXTRA, rows), jnp.float32)
    for i in range(3):
        part = squares.astype(jnp.bfloat16).astype(jnp.float32)
        parts = jnp.where(row == i, part, parts)
        squares = squares - part
    out_ref[0, rows:, :rows] = parts.astype(jnp.bfloat16)
    if rows < width:
        out_ref[0, rows:, rows:] = jnp.zeros((EXTRA, width - rows), jnp.bfloat16)


def prepare(activations, norm_gain):
    rows, width = activations.shape
    return pl.pallas_call(
        prepare_body,
        out_shape=jax.ShapeDtypeStruct((1, rows + EXTRA, width), jnp.bfloat16),
        compiler_params=pltpu.CompilerParams(vmem_limit_bytes=PREPARE_LIMIT),
        name="prepare",
    )(activations, norm_gain)


def gate_up_body(count, first, last, rows, main, features, me_ref, *refs):
    blocks = refs[:count]
    if last:
        *refs, buffer_ref, sems = refs
    gate_ref, up_ref, *rest = refs[count:]
    if not first:
        before = rest[:4]
        rest = rest[4:]
    if last:
        down_ref, hidden_ref, *rest = rest
        *outs, _, _, _, _ = rest
        rest = rest[len(outs) :]
        width = outs[0].shape[1]
        copies = []
        for i, job in enumerate(last):
            column = pl.multiple_of(block(me_ref[0], [job], 0) * width, width)
            at = pl.ds(i * width, width)
            copies.append(
                pltpu.make_async_copy(
                    down_ref.at[:, pl.ds(column, width)], buffer_ref.at[:, at], sems.at[i]
                )
            )
    accs = rest
    step = pl.program_id(0)

    if last:

        @pl.when(step == 0)
        def _():
            for copy in copies:
                copy.start()

    for s in range(count):

        @pl.when(step == s)
        def _(s=s):
            x = blocks[s][0, :rows, :]
            gate, up = gate_ref[...], up_ref[...]
            mixed = jnp.concatenate([gate[:, main:], up[:, main:]], axis=1)
            values = [
                jnp.dot(x, weight, preferred_element_type=jnp.float32)
                for weight in (gate[:, :main], up[:, :main], mixed)
            ]
            squares = blocks[s][0, rows:, :].astype(jnp.float32)
            squares = jnp.sum(squares, axis=0, keepdims=True)
            values.append(jnp.broadcast_to(squares, accs[3].shape))
            if s:
                values = [acc[...] + value for acc, value in zip(accs, values)]
            elif not first:
                values = [old[...] + value for old, value in zip(before, values)]
            if not last or s < count - 1:
                for acc, value in zip(accs, values):
                    acc[...] = value
                return
            factor = lax.rsqrt(values[3][:1, :rows] / features + epsilon)
            factor = jnp.broadcast_to(factor, (128, rows)).T[:, :1]

            def act(g, u):
                g, u = g * factor, u * factor
                return (g / (1.0 + jnp.exp(-g)) * u).astype(jnp.bfloat16)

            gate, up, both, _ = values
            rem = both.shape[1] // 2
            hidden_ref[:, :main] = act(gate, up)
            hidden_ref[:, main:] = act(both[:, :rem], both[:, rem:])
            for i, (copy, out) in enumerate(zip(copies, outs)):
                copy.wait()
                value = down_block(hidden_ref, buffer_ref.at[:, i * width : (i + 1) * width])
                out[...] = value.astype(out.dtype)


def gate_up(me, jobs, shards, gate_weight, up_weight, acc, last=(), kinds=(), down_weight=None):
    height, depth = shards[0][0].shape[1:]
    count = len(jobs)
    rows = height - EXTRA
    features, ff = gate_weight.shape
    main = ff // 256 * 256 if ff % 256 else ff - 256
    rem = ff - main
    first = acc is None
    whole = lambda shape: pl.BlockSpec(shape, lambda s, me: (0, 0))
    weight = pl.BlockSpec((depth, ff), lambda s, me: (block(me[0], jobs, s), 0))
    shard = lambda i: pl.BlockSpec((1, height, depth), lambda s, me: (i, 0, 0))
    in_specs = [shard(i) for _, i in shards] + [weight, weight]
    args = [*(x for x, _ in shards), gate_weight, up_weight]
    shapes = [(rows, main), (rows, main), (rows, 2 * rem), (8, depth)]
    if not first:
        in_specs += [whole(s) for s in shapes]
        args += list(acc)
    if last:
        in_specs += [pl.BlockSpec(memory_space=pl.ANY)]
        args += [down_weight]
        out_shape = [jax.ShapeDtypeStruct((rows, ff), jnp.bfloat16)]
        out_shape += [jax.ShapeDtypeStruct((rows, depth), kind) for kind in kinds]
        out_specs = [whole(x.shape) for x in out_shape]
        scratch = [pltpu.VMEM(s, jnp.float32) for s in shapes]
        scratch += [
            pltpu.VMEM((ff, len(last) * depth), jnp.bfloat16),
            pltpu.SemaphoreType.DMA((len(last),)),
        ]
    else:
        out_shape = [jax.ShapeDtypeStruct(s, jnp.float32) for s in shapes]
        out_specs = [whole(s) for s in shapes]
        scratch = []
    return pl.pallas_call(
        functools.partial(gate_up_body, count, first, last, rows, main, features),
        grid_spec=pltpu.PrefetchScalarGridSpec(
            num_scalar_prefetch=1,
            grid=(count,),
            in_specs=in_specs,
            out_specs=out_specs,
            scratch_shapes=scratch,
        ),
        out_shape=out_shape,
        compiler_params=pltpu.CompilerParams(vmem_limit_bytes=VMEM_LIMIT),
        cost_estimate=pl.CostEstimate(
            flops=4 * rows * depth * count * ff // 8,
            bytes_accessed=4 * depth * count * ff // 8,
            transcendentals=0,
        ),
        name="gate_up",
    )(me, *args)


def down_block(hidden_ref, weight_ref):
    ff = hidden_ref.shape[1]
    main = ff // 256 * 256
    value = jnp.dot(
        hidden_ref[:, :main], weight_ref[:main, :], preferred_element_type=jnp.float32
    )
    if main < ff:
        value = value + jnp.dot(
            hidden_ref[:, main:], weight_ref[main:, :], preferred_element_type=jnp.float32
        )
    return value


def down_body(kept, sent, me_ref, hidden_ref, weight_ref, *outs):
    now = pl.program_id(0)
    value = down_block(hidden_ref, weight_ref)
    for s in range(kept):

        @pl.when(now == s)
        def _(out=outs[s]):
            out[...] = value

    for s in range(kept, kept + sent):

        @pl.when(now == s)
        def _(out=outs[s]):
            out[...] = value.astype(jnp.bfloat16)


def down(me, kept, sent, hidden, down_weight, width):
    rows, ff = hidden.shape
    jobs = kept + sent
    kinds = [jnp.float32] * len(kept) + [jnp.bfloat16] * len(sent)
    return pl.pallas_call(
        functools.partial(down_body, len(kept), len(sent)),
        grid_spec=pltpu.PrefetchScalarGridSpec(
            num_scalar_prefetch=1,
            grid=(len(jobs),),
            in_specs=[
                pl.BlockSpec((rows, ff), lambda s, me: (0, 0)),
                pl.BlockSpec((ff, width), lambda s, me: (0, block(me[0], jobs, s))),
            ],
            out_specs=[pl.BlockSpec((rows, width), lambda s, me: (0, 0))] * len(jobs),
        ),
        out_shape=[jax.ShapeDtypeStruct((rows, width), kind) for kind in kinds],
        compiler_params=pltpu.CompilerParams(vmem_limit_bytes=VMEM_LIMIT),
        cost_estimate=pl.CostEstimate(
            flops=rows * ff * width * len(jobs) // 4,
            bytes_accessed=ff * width * len(jobs) // 4,
            transcendentals=0,
        ),
        name="down",
    )(me, hidden, down_weight)


def overlapped(activations, norm_gain, gate_weight, up_weight, down_weight):
    width = activations.shape[1]
    index = lax.axis_index("gx").astype(jnp.int32)
    me = index[None]
    z = index >> 2
    end = (z == 0) | (z == LINE - 1)
    resident = activations.astype(jnp.float32)
    OWN, ONE, ONE_IN, TWO, TWO_IN, THREE, THREE_ACROSS, FOUR = range(8)

    def multiply(acc, *shards, then=()):
        jobs = [shard[:2] for shard in shards]
        arrays = [shard[2:] for shard in shards]
        return gate_up(me, jobs, arrays, gate_weight, up_weight, acc, *then)

    early, end = lax.optimization_barrier((activations, end))
    own = prepare(early, norm_gain)
    one, one_in = send(own, ALONG), send(own, INSIDE)
    theirs = swap(own)
    two, two_in = send(one_in, ALONG), send(one, INSIDE)
    their_ones = swap(jnp.concatenate([one, one_in]))
    acc = multiply(
        None, (OWN, 0, own, 0), (OWN, 1, theirs, 0), (ONE, 0, one, 0), (ONE_IN, 0, one_in, 0)
    )
    two, two_in = after((two, two_in), acc[3])
    three, across = send(two_in, ALONG), send(jnp.where(end, two, one_in), ACROSS)
    their_twos = swap(jnp.concatenate([two, two_in]))
    acc = multiply(
        acc,
        (ONE, 1, their_ones, 0), (ONE_IN, 1, their_ones, 1), (TWO, 0, two, 0), (TWO_IN, 0, two_in, 0),
    )
    three, across = after((three, across), acc[3])
    four = send(jnp.where(end, three, two_in), ACROSS)
    their_threes = swap(jnp.concatenate([three, across]))
    acc = multiply(
        acc,
        (TWO, 1, their_twos, 0), (TWO_IN, 1, their_twos, 1),
        (THREE, 0, three, 0), (THREE_ACROSS, 0, across, 0),
    )
    four = after(four, acc[3])
    their_four = swap(four)
    acc = multiply(
        acc,
        (THREE, 1, their_threes, 0), (THREE_ACROSS, 1, their_threes, 1), (FOUR, 0, four, 0),
    )
    hidden, their_four, four = multiply(
        acc,
        (FOUR, 1, after(their_four, acc[3]), 0),
        then=(((FOUR, 1), (FOUR, 0)), (jnp.bfloat16, jnp.float32), down_weight),
    )

    narrow = lambda x: x.astype(jnp.bfloat16)
    wide = lambda x: x.astype(jnp.float32)
    zero = jnp.zeros((), jnp.float32)

    def swap_halves(x):
        half = x.shape[0] // 2
        return jnp.concatenate([swap(x[:half]), swap(x[half:])])

    def partials(hidden, kept, sent, whole=0):
        kept_jobs, sent_jobs = [(place, 0) for place in kept], [(place, 1) for place in sent]
        outs = down(me, kept_jobs, sent_jobs, hidden, down_weight, width)
        cut = len(outs) - whole if whole else len(kept)
        halved = [wide(swap_halves(x)) for x in outs[len(kept) : cut]]
        return [*outs[: len(kept)], *halved, *(wide(swap(x)) for x in outs[cut:])]

    four = narrow(four + wide(swap(their_four)))
    got = wide(send(four, ACROSS))
    hidden = after(hidden, four)
    three, across, their_three, their_across, their_two, their_in = partials(
        hidden, (THREE, THREE_ACROSS), (THREE, THREE_ACROSS, TWO, TWO_IN), whole=2
    )
    three = narrow(three + their_three + jnp.where(end, got, zero))
    got_three = wide(send(three, ALONG))
    across = narrow(across + after(their_across, three))
    got_across = wide(send(across, ACROSS))
    two, two_in, their_one, their_one_in = partials(
        after(hidden, three, across), (TWO, TWO_IN), (ONE, ONE_IN)
    )
    two_in = narrow(two_in + their_in + jnp.where(end, zero, got) + got_three)
    got_in = wide(send(two_in, INSIDE))
    two = narrow(two + after(their_two, two_in) + jnp.where(end, got_across, zero))
    got_two = wide(send(two, ALONG))
    one, one_in, their_own = partials(after(hidden, two, two_in), (ONE, ONE_IN), (OWN,))
    one = narrow(one + their_one + got_in)
    got_one = wide(send(one, ALONG))
    one_in = narrow(one_in + after(their_one_in, one) + jnp.where(end, zero, got_across) + got_two)
    got_one_in = wide(send(one_in, INSIDE))
    (kept,) = partials(after(hidden, one, one_in), (OWN,), ())
    branch = kept + their_own
    return (resident + branch + got_one + got_one_in).astype(jnp.bfloat16)


def plain(activations, norm_gain, gate_weight, up_weight, down_weight):
    resident = activations.astype(jnp.float32)
    totals = lax.psum(jnp.sum(resident * resident, axis=1), "gx")
    factor = lax.rsqrt(totals / (resident.shape[1] * lax.axis_size("gx")) + epsilon)
    normed = (resident * factor[:, None] * norm_gain.astype(jnp.float32)[None, :]).astype(
        jnp.bfloat16
    )
    pieces = lax.all_gather(normed, "gx", axis=1, tiled=True)
    gate_sum = jnp.dot(pieces, gate_weight, preferred_element_type=jnp.float32)
    up_sum = jnp.dot(pieces, up_weight, preferred_element_type=jnp.float32)
    hidden = (jax.nn.silu(gate_sum) * up_sum).astype(jnp.bfloat16)
    summed = lax.psum_scatter(
        lax.dot_general(
            down_weight, hidden, (((0,), (1,)), ((), ())), preferred_element_type=jnp.float32
        ),
        "gx",
        scatter_dimension=0,
        tiled=True,
    )
    return (resident + summed.T).astype(jnp.bfloat16)


def per_device(n, activations, norm_gain, gate_weight, up_weight, down_weight):
    args = (activations, norm_gain, gate_weight, up_weight, down_weight)
    rows, width = activations.shape
    tiled = rows % 128 == 0 and width % 128 == 0 and gate_weight.shape[1] % 128 == 0
    tiled = tiled and rows <= width
    if n == 4 * LINE and tiled:
        return overlapped(*args)
    return plain(*args)


def solution(mesh):
    in_specs = (P("groups", "gx"), P("gx"), P(None, "gx"), P(None, "gx"), P("gx", None))
    out_specs = P("groups", "gx")
    return jax.shard_map(
        functools.partial(per_device, mesh.shape["gx"]),
        mesh=mesh,
        in_specs=in_specs,
        out_specs=out_specs,
        check_vma=False,
    )
```

```python
import functools

import jax
import jax.numpy as jnp
import numpy as np
from jax import lax
from jax.experimental import pallas as pl
from jax.experimental.pallas import tpu as pltpu
from jax.sharding import PartitionSpec as P

epsilon = 1e-05
LINE = 4
EXTRA = 16
VMEM_LIMIT = 36 * 1024 * 1024
PREPARE_LIMIT = 36 * 1024 * 1024

ALONG = (lambda z, y: (z ^ 1, y),) * 2
INSIDE = (lambda z, y: (z, y ^ 1), lambda z, y: (z ^ 3, y))
ACROSS = (lambda z, y: (z, y ^ 1),) * 2

TAKEN = np.array([(0, 2, 1, 4, 3, 6, 5, 7), (0, 2, 6, 3, 4, 1, 7, 5)], np.int32)


def send(x, move):
    pairs = []
    for z in range(LINE):
        for y in range(2):
            to_z, to_y = move[0 < z < LINE - 1](z, y)
            pairs += [(z * 4 + y * 2 + c, to_z * 4 + to_y * 2 + c) for c in range(2)]
    return lax.ppermute(x, "gx", pairs)


def swap(x):
    return lax.ppermute(x, "gx", [(i, i ^ 1) for i in range(4 * LINE)])


def after(x, *others):
    return lax.optimization_barrier((x, *others))[0]


def block(me, jobs, s):
    def pick(table):
        value = jnp.int32(table[0])
        for i, entry in enumerate(table[1:], 1):
            value = jnp.where(s == i, jnp.int32(entry), value)
        return value

    places, others = zip(*jobs)
    end = (((me >> 2) ^ (me >> 3)) & 1) == 0
    code = jnp.where(end, pick(TAKEN[0, places]), pick(TAKEN[1, places]))
    return ((me >> 1) ^ code) * 2 + ((me & 1) ^ pick(others))


def prepare_body(x_ref, gain_ref, out_ref):
    rows, width = x_ref.shape
    x = x_ref[...].astype(jnp.float32)
    gain = gain_ref[...].astype(jnp.float32).reshape(1, width)
    out_ref[0, :rows, :] = (x * gain).astype(jnp.bfloat16)
    squares = jnp.broadcast_to(jnp.sum(x * x, axis=1, keepdims=True), (rows, 128)).T[:EXTRA]
    row = lax.broadcasted_iota(jnp.int32, (EXTRA, rows), 0)
    parts = jnp.zeros((EXTRA, rows), jnp.float32)
    for i in range(3):
        part = squares.astype(jnp.bfloat16).astype(jnp.float32)
        parts = jnp.where(row == i, part, parts)
        squares = squares - part
    out_ref[0, rows:, :rows] = parts.astype(jnp.bfloat16)
    if rows < width:
        out_ref[0, rows:, rows:] = jnp.zeros((EXTRA, width - rows), jnp.bfloat16)


def prepare(activations, norm_gain):
    rows, width = activations.shape
    return pl.pallas_call(
        prepare_body,
        out_shape=jax.ShapeDtypeStruct((1, rows + EXTRA, width), jnp.bfloat16),
        compiler_params=pltpu.CompilerParams(vmem_limit_bytes=PREPARE_LIMIT),
        name="prepare",
    )(activations, norm_gain)


def gate_up_body(count, first, last, rows, main, features, me_ref, *refs):
    blocks = refs[:count]
    if last:
        *refs, buffer_ref, sems = refs
    gate_ref, up_ref, *rest = refs[count:]
    if not first:
        before = rest[:4]
        rest = rest[4:]
    if last:
        down_ref, hidden_ref, *rest = rest
        *outs, _, _, _, _ = rest
        rest = rest[len(outs) :]
        width = outs[0].shape[1]
        copies = []
        for i, job in enumerate(last):
            column = pl.multiple_of(block(me_ref[0], [job], 0) * width, width)
            at = pl.ds(i * width, width)
            copies.append(
                pltpu.make_async_copy(
                    down_ref.at[:, pl.ds(column, width)], buffer_ref.at[:, at], sems.at[i]
                )
            )
    accs = rest
    step = pl.program_id(0)

    if last:

        @pl.when(step == count - 1)
        def _():
            for copy in copies:
                copy.start()

    for s in range(count):

        @pl.when(step == s)
        def _(s=s):
            x = blocks[s][0, :rows, :]
            gate, up = gate_ref[...], up_ref[...]
            mixed = jnp.concatenate([gate[:, main:], up[:, main:]], axis=1)
            values = [
                jnp.dot(x, weight, preferred_element_type=jnp.float32)
                for weight in (gate[:, :main], up[:, :main], mixed)
            ]
            squares = blocks[s][0, rows:, :].astype(jnp.float32)
            squares = jnp.sum(squares, axis=0, keepdims=True)
            values.append(jnp.broadcast_to(squares, accs[3].shape))
            if s:
                values = [acc[...] + value for acc, value in zip(accs, values)]
            elif not first:
                values = [old[...] + value for old, value in zip(before, values)]
            if not last or s < count - 1:
                for acc, value in zip(accs, values):
                    acc[...] = value
                return
            factor = lax.rsqrt(values[3][:1, :rows] / features + epsilon)
            factor = jnp.broadcast_to(factor, (128, rows)).T[:, :1]

            def act(g, u):
                g, u = g * factor, u * factor
                return (g / (1.0 + jnp.exp(-g)) * u).astype(jnp.bfloat16)

            gate, up, both, _ = values
            rem = both.shape[1] // 2
            hidden_ref[:, :main] = act(gate, up)
            hidden_ref[:, main:] = act(both[:, :rem], both[:, rem:])
            for i, (copy, out) in enumerate(zip(copies, outs)):
                copy.wait()
                value = down_block(hidden_ref, buffer_ref.at[:, i * width : (i + 1) * width])
                out[...] = value.astype(out.dtype)


def gate_up(me, jobs, shards, gate_weight, up_weight, acc, last=(), kinds=(), down_weight=None):
    height, depth = shards[0][0].shape[1:]
    count = len(jobs)
    rows = height - EXTRA
    features, ff = gate_weight.shape
    main = ff // 256 * 256 if ff % 256 else ff - 256
    rem = ff - main
    first = acc is None
    whole = lambda shape: pl.BlockSpec(shape, lambda s, me: (0, 0))
    weight = pl.BlockSpec((depth, ff), lambda s, me: (block(me[0], jobs, s), 0))
    shard = lambda i: pl.BlockSpec((1, height, depth), lambda s, me: (i, 0, 0))
    in_specs = [shard(i) for _, i in shards] + [weight, weight]
    args = [*(x for x, _ in shards), gate_weight, up_weight]
    shapes = [(rows, main), (rows, main), (rows, 2 * rem), (8, depth)]
    if not first:
        in_specs += [whole(s) for s in shapes]
        args += list(acc)
    if last:
        in_specs += [pl.BlockSpec(memory_space=pl.ANY)]
        args += [down_weight]
        out_shape = [jax.ShapeDtypeStruct((rows, ff), jnp.bfloat16)]
        out_shape += [jax.ShapeDtypeStruct((rows, depth), kind) for kind in kinds]
        out_specs = [whole(x.shape) for x in out_shape]
        scratch = [pltpu.VMEM(s, jnp.float32) for s in shapes]
        scratch += [
            pltpu.VMEM((ff, len(last) * depth), jnp.bfloat16),
            pltpu.SemaphoreType.DMA((len(last),)),
        ]
    else:
        out_shape = [jax.ShapeDtypeStruct(s, jnp.float32) for s in shapes]
        out_specs = [whole(s) for s in shapes]
        scratch = []
    return pl.pallas_call(
        functools.partial(gate_up_body, count, first, last, rows, main, features),
        grid_spec=pltpu.PrefetchScalarGridSpec(
            num_scalar_prefetch=1,
            grid=(count,),
            in_specs=in_specs,
            out_specs=out_specs,
            scratch_shapes=scratch,
        ),
        out_shape=out_shape,
        compiler_params=pltpu.CompilerParams(vmem_limit_bytes=VMEM_LIMIT),
        cost_estimate=pl.CostEstimate(
            flops=4 * rows * depth * count * ff // 8,
            bytes_accessed=4 * depth * count * ff // 8,
            transcendentals=0,
        ),
        name="gate_up",
    )(me, *args)


def down_block(hidden_ref, weight_ref):
    ff = hidden_ref.shape[1]
    main = ff // 256 * 256
    value = jnp.dot(
        hidden_ref[:, :main], weight_ref[:main, :], preferred_element_type=jnp.float32
    )
    if main < ff:
        value = value + jnp.dot(
            hidden_ref[:, main:], weight_ref[main:, :], preferred_element_type=jnp.float32
        )
    return value


def down_body(kept, sent, me_ref, hidden_ref, weight_ref, *outs):
    now = pl.program_id(0)
    value = down_block(hidden_ref, weight_ref)
    for s in range(kept):

        @pl.when(now == s)
        def _(out=outs[s]):
            out[...] = value

    for s in range(kept, kept + sent):

        @pl.when(now == s)
        def _(out=outs[s]):
            out[...] = value.astype(jnp.bfloat16)


def down(me, kept, sent, hidden, down_weight, width):
    rows, ff = hidden.shape
    jobs = kept + sent
    kinds = [jnp.float32] * len(kept) + [jnp.bfloat16] * len(sent)
    return pl.pallas_call(
        functools.partial(down_body, len(kept), len(sent)),
        grid_spec=pltpu.PrefetchScalarGridSpec(
            num_scalar_prefetch=1,
            grid=(len(jobs),),
            in_specs=[
                pl.BlockSpec((rows, ff), lambda s, me: (0, 0)),
                pl.BlockSpec((ff, width), lambda s, me: (0, block(me[0], jobs, s))),
            ],
            out_specs=[pl.BlockSpec((rows, width), lambda s, me: (0, 0))] * len(jobs),
        ),
        out_shape=[jax.ShapeDtypeStruct((rows, width), kind) for kind in kinds],
        compiler_params=pltpu.CompilerParams(vmem_limit_bytes=VMEM_LIMIT),
        cost_estimate=pl.CostEstimate(
            flops=rows * ff * width * len(jobs) // 4,
            bytes_accessed=ff * width * len(jobs) // 4,
            transcendentals=0,
        ),
        name="down",
    )(me, hidden, down_weight)


def overlapped(activations, norm_gain, gate_weight, up_weight, down_weight):
    width = activations.shape[1]
    index = lax.axis_index("gx").astype(jnp.int32)
    me = index[None]
    z = index >> 2
    end = (z == 0) | (z == LINE - 1)
    resident = activations.astype(jnp.float32)
    OWN, ONE, ONE_IN, TWO, TWO_IN, THREE, THREE_ACROSS, FOUR = range(8)

    def multiply(acc, *shards, then=()):
        jobs = [shard[:2] for shard in shards]
        arrays = [shard[2:] for shard in shards]
        return gate_up(me, jobs, arrays, gate_weight, up_weight, acc, *then)

    early, end = lax.optimization_barrier((activations, end))
    own = prepare(early, norm_gain)
    one, one_in = send(own, ALONG), send(own, INSIDE)
    theirs = swap(own)
    two, two_in = send(one_in, ALONG), send(one, INSIDE)
    their_ones = swap(jnp.concatenate([one, one_in]))
    acc = multiply(
        None, (OWN, 0, own, 0), (OWN, 1, theirs, 0), (ONE, 0, one, 0), (ONE_IN, 0, one_in, 0)
    )
    two, two_in = after((two, two_in), acc[3])
    three, across = send(two_in, ALONG), send(jnp.where(end, two, one_in), ACROSS)
    their_twos = swap(jnp.concatenate([two, two_in]))
    acc = multiply(
        acc,
        (ONE, 1, their_ones, 0), (ONE_IN, 1, their_ones, 1), (TWO, 0, two, 0), (TWO_IN, 0, two_in, 0),
    )
    three, across = after((three, across), acc[3])
    four = send(jnp.where(end, three, two_in), ACROSS)
    their_threes = swap(jnp.concatenate([three, across]))
    acc = multiply(
        acc,
        (TWO, 1, their_twos, 0), (TWO_IN, 1, their_twos, 1),
        (THREE, 0, three, 0), (THREE_ACROSS, 0, across, 0),
        (THREE, 1, their_threes, 0), (THREE_ACROSS, 1, their_threes, 1),
    )
    four = after(four, acc[3])
    hidden, their_four, four = multiply(
        acc,
        (FOUR, 0, four, 0), (FOUR, 1, swap(four), 0),
        then=(((FOUR, 1), (FOUR, 0)), (jnp.bfloat16, jnp.float32), down_weight),
    )

    narrow = lambda x: x.astype(jnp.bfloat16)
    wide = lambda x: x.astype(jnp.float32)
    zero = jnp.zeros((), jnp.float32)

    def swap_halves(x):
        half = x.shape[0] // 2
        return jnp.concatenate([swap(x[:half]), swap(x[half:])])

    def partials(hidden, kept, sent, whole=0):
        kept_jobs, sent_jobs = [(place, 0) for place in kept], [(place, 1) for place in sent]
        outs = down(me, kept_jobs, sent_jobs, hidden, down_weight, width)
        cut = len(outs) - whole if whole else len(kept)
        halved = [wide(swap_halves(x)) for x in outs[len(kept) : cut]]
        return [*outs[: len(kept)], *halved, *(wide(swap(x)) for x in outs[cut:])]

    four = narrow(four + wide(swap(their_four)))
    got = wide(send(four, ACROSS))
    hidden = after(hidden, four)
    three, across, their_three, their_across, their_two, their_in = partials(
        hidden, (THREE, THREE_ACROSS), (THREE, THREE_ACROSS, TWO, TWO_IN), whole=2
    )
    three = narrow(three + their_three + jnp.where(end, got, zero))
    got_three = wide(send(three, ALONG))
    across = narrow(across + after(their_across, three))
    got_across = wide(send(across, ACROSS))
    two, two_in, their_one, their_one_in = partials(
        after(hidden, three, across), (TWO, TWO_IN), (ONE, ONE_IN)
    )
    two_in = narrow(two_in + their_in + jnp.where(end, zero, got) + got_three)
    got_in = wide(send(two_in, INSIDE))
    two = narrow(two + after(their_two, two_in) + jnp.where(end, got_across, zero))
    got_two = wide(send(two, ALONG))
    one, one_in, their_own = partials(after(hidden, two, two_in), (ONE, ONE_IN), (OWN,))
    one = narrow(one + their_one + got_in)
    got_one = wide(send(one, ALONG))
    one_in = narrow(one_in + after(their_one_in, one) + jnp.where(end, zero, got_across) + got_two)
    got_one_in = wide(send(one_in, INSIDE))
    (kept,) = partials(after(hidden, one, one_in), (OWN,), ())
    branch = kept + their_own
    return (resident + branch + got_one + got_one_in).astype(jnp.bfloat16)


def plain(activations, norm_gain, gate_weight, up_weight, down_weight):
    resident = activations.astype(jnp.float32)
    totals = lax.psum(jnp.sum(resident * resident, axis=1), "gx")
    factor = lax.rsqrt(totals / (resident.shape[1] * lax.axis_size("gx")) + epsilon)
    normed = (resident * factor[:, None] * norm_gain.astype(jnp.float32)[None, :]).astype(
        jnp.bfloat16
    )
    pieces = lax.all_gather(normed, "gx", axis=1, tiled=True)
    gate_sum = jnp.dot(pieces, gate_weight, preferred_element_type=jnp.float32)
    up_sum = jnp.dot(pieces, up_weight, preferred_element_type=jnp.float32)
    hidden = (jax.nn.silu(gate_sum) * up_sum).astype(jnp.bfloat16)
    summed = lax.psum_scatter(
        lax.dot_general(
            down_weight, hidden, (((0,), (1,)), ((), ())), preferred_element_type=jnp.float32
        ),
        "gx",
        scatter_dimension=0,
        tiled=True,
    )
    return (resident + summed.T).astype(jnp.bfloat16)


def per_device(n, activations, norm_gain, gate_weight, up_weight, down_weight):
    args = (activations, norm_gain, gate_weight, up_weight, down_weight)
    rows, width = activations.shape
    tiled = rows % 128 == 0 and width % 128 == 0 and gate_weight.shape[1] % 128 == 0
    tiled = tiled and rows <= width
    if n == 4 * LINE and tiled:
        return overlapped(*args)
    return plain(*args)


def solution(mesh):
    in_specs = (P("groups", "gx"), P("gx"), P(None, "gx"), P(None, "gx"), P("gx", None))
    out_specs = P("groups", "gx")
    return jax.shard_map(
        functools.partial(per_device, mesh.shape["gx"]),
        mesh=mesh,
        in_specs=in_specs,
        out_specs=out_specs,
        check_vma=False,
    )
```

```python
import functools

import jax
import jax.numpy as jnp
import numpy as np
from jax import lax
from jax.experimental import pallas as pl
from jax.experimental.pallas import tpu as pltpu
from jax.sharding import PartitionSpec as P

epsilon = 1e-05
LINE = 4
EXTRA = 16
VMEM_LIMIT = 36 * 1024 * 1024
PREPARE_LIMIT = 36 * 1024 * 1024

ALONG = (lambda z, y: (z ^ 1, y),) * 2
INSIDE = (lambda z, y: (z, y ^ 1), lambda z, y: (z ^ 3, y))
ACROSS = (lambda z, y: (z, y ^ 1),) * 2

TAKEN = np.array([(0, 2, 1, 4, 3, 6, 5, 7), (0, 2, 6, 3, 4, 1, 7, 5)], np.int32)


def send(x, move):
    pairs = []
    for z in range(LINE):
        for y in range(2):
            to_z, to_y = move[0 < z < LINE - 1](z, y)
            pairs += [(z * 4 + y * 2 + c, to_z * 4 + to_y * 2 + c) for c in range(2)]
    return lax.ppermute(x, "gx", pairs)


def swap(x):
    return lax.ppermute(x, "gx", [(i, i ^ 1) for i in range(4 * LINE)])


def after(x, *others):
    return lax.optimization_barrier((x, *others))[0]


def block(me, jobs, s):
    def pick(table):
        value = jnp.int32(table[0])
        for i, entry in enumerate(table[1:], 1):
            value = jnp.where(s == i, jnp.int32(entry), value)
        return value

    places, others = zip(*jobs)
    end = (((me >> 2) ^ (me >> 3)) & 1) == 0
    code = jnp.where(end, pick(TAKEN[0, places]), pick(TAKEN[1, places]))
    return ((me >> 1) ^ code) * 2 + ((me & 1) ^ pick(others))


def prepare_body(x_ref, gain_ref, out_ref):
    rows, width = x_ref.shape
    x = x_ref[...].astype(jnp.float32)
    gain = gain_ref[...].astype(jnp.float32).reshape(1, width)
    out_ref[0, :rows, :] = (x * gain).astype(jnp.bfloat16)
    squares = jnp.broadcast_to(jnp.sum(x * x, axis=1, keepdims=True), (rows, 128)).T[:EXTRA]
    row = lax.broadcasted_iota(jnp.int32, (EXTRA, rows), 0)
    parts = jnp.zeros((EXTRA, rows), jnp.float32)
    for i in range(3):
        part = squares.astype(jnp.bfloat16).astype(jnp.float32)
        parts = jnp.where(row == i, part, parts)
        squares = squares - part
    out_ref[0, rows:, :rows] = parts.astype(jnp.bfloat16)
    if rows < width:
        out_ref[0, rows:, rows:] = jnp.zeros((EXTRA, width - rows), jnp.bfloat16)


def prepare(activations, norm_gain):
    rows, width = activations.shape
    return pl.pallas_call(
        prepare_body,
        out_shape=jax.ShapeDtypeStruct((1, rows + EXTRA, width), jnp.bfloat16),
        compiler_params=pltpu.CompilerParams(vmem_limit_bytes=PREPARE_LIMIT),
        name="prepare",
    )(activations, norm_gain)


def gate_up_body(count, first, last, rows, main, features, me_ref, *refs):
    blocks = refs[:count]
    if last:
        *refs, buffer_ref, sems = refs
    gate_ref, up_ref, *rest = refs[count:]
    if not first:
        before = rest[:4]
        rest = rest[4:]
    if last:
        down_ref, hidden_ref, *rest = rest
        *outs, _, _, _, _ = rest
        rest = rest[len(outs) :]
        width = outs[0].shape[1]
        copies = []
        for i, job in enumerate(last):
            column = pl.multiple_of(block(me_ref[0], [job], 0) * width, width)
            at = pl.ds(i * width, width)
            copies.append(
                pltpu.make_async_copy(
                    down_ref.at[:, pl.ds(column, width)], buffer_ref.at[:, at], sems.at[i]
                )
            )
    accs = rest
    step = pl.program_id(0)

    if last:

        @pl.when(step == count - 1)
        def _():
            for copy in copies:
                copy.start()

    for s in range(count):

        @pl.when(step == s)
        def _(s=s):
            x = blocks[s][0, :rows, :]
            gate, up = gate_ref[...], up_ref[...]
            mixed = jnp.concatenate([gate[:, main:], up[:, main:]], axis=1)
            values = [
                jnp.dot(x, weight, preferred_element_type=jnp.float32)
                for weight in (gate[:, :main], up[:, :main], mixed)
            ]
            squares = blocks[s][0, rows:, :].astype(jnp.float32)
            squares = jnp.sum(squares, axis=0, keepdims=True)
            values.append(jnp.broadcast_to(squares, accs[3].shape))
            if s:
                values = [acc[...] + value for acc, value in zip(accs, values)]
            elif not first:
                values = [old[...] + value for old, value in zip(before, values)]
            if not last or s < count - 1:
                for acc, value in zip(accs, values):
                    acc[...] = value
                return
            factor = lax.rsqrt(values[3][:1, :rows] / features + epsilon)
            factor = jnp.broadcast_to(factor, (128, rows)).T[:, :1]

            def act(g, u):
                g, u = g * factor, u * factor
                return (g / (1.0 + jnp.exp(-g)) * u).astype(jnp.bfloat16)

            gate, up, both, _ = values
            rem = both.shape[1] // 2
            hidden_ref[:, :main] = act(gate, up)
            hidden_ref[:, main:] = act(both[:, :rem], both[:, rem:])
            for i, (copy, out) in enumerate(zip(copies, outs)):
                copy.wait()
                value = down_block(hidden_ref, buffer_ref.at[:, i * width : (i + 1) * width])
                out[...] = value.astype(out.dtype)


def gate_up(me, jobs, shards, gate_weight, up_weight, acc, last=(), kinds=(), down_weight=None):
    height, depth = shards[0][0].shape[1:]
    count = len(jobs)
    rows = height - EXTRA
    features, ff = gate_weight.shape
    main = ff // 256 * 256 if ff % 256 else ff - 256
    rem = ff - main
    first = acc is None
    whole = lambda shape: pl.BlockSpec(shape, lambda s, me: (0, 0))
    weight = pl.BlockSpec((depth, ff), lambda s, me: (block(me[0], jobs, s), 0))
    shard = lambda i: pl.BlockSpec((1, height, depth), lambda s, me: (i, 0, 0))
    in_specs = [shard(i) for _, i in shards] + [weight, weight]
    args = [*(x for x, _ in shards), gate_weight, up_weight]
    shapes = [(rows, main), (rows, main), (rows, 2 * rem), (8, depth)]
    if not first:
        in_specs += [whole(s) for s in shapes]
        args += list(acc)
    if last:
        in_specs += [pl.BlockSpec(memory_space=pl.ANY)]
        args += [down_weight]
        out_shape = [jax.ShapeDtypeStruct((rows, ff), jnp.bfloat16)]
        out_shape += [jax.ShapeDtypeStruct((rows, depth), kind) for kind in kinds]
        out_specs = [whole(x.shape) for x in out_shape]
        scratch = [pltpu.VMEM(s, jnp.float32) for s in shapes]
        scratch += [
            pltpu.VMEM((ff, len(last) * depth), jnp.bfloat16),
            pltpu.SemaphoreType.DMA((len(last),)),
        ]
    else:
        out_shape = [jax.ShapeDtypeStruct(s, jnp.float32) for s in shapes]
        out_specs = [whole(s) for s in shapes]
        scratch = []
    return pl.pallas_call(
        functools.partial(gate_up_body, count, first, last, rows, main, features),
        grid_spec=pltpu.PrefetchScalarGridSpec(
            num_scalar_prefetch=1,
            grid=(count,),
            in_specs=in_specs,
            out_specs=out_specs,
            scratch_shapes=scratch,
        ),
        out_shape=out_shape,
        compiler_params=pltpu.CompilerParams(vmem_limit_bytes=VMEM_LIMIT),
        cost_estimate=pl.CostEstimate(
            flops=4 * rows * depth * count * ff // 8,
            bytes_accessed=4 * depth * count * ff // 8,
            transcendentals=0,
        ),
        name="gate_up",
    )(me, *args)


def down_block(hidden_ref, weight_ref):
    ff = hidden_ref.shape[1]
    main = ff // 256 * 256
    value = jnp.dot(
        hidden_ref[:, :main], weight_ref[:main, :], preferred_element_type=jnp.float32
    )
    if main < ff:
        value = value + jnp.dot(
            hidden_ref[:, main:], weight_ref[main:, :], preferred_element_type=jnp.float32
        )
    return value


def down_body(kept, sent, me_ref, hidden_ref, weight_ref, *outs):
    now = pl.program_id(0)
    value = down_block(hidden_ref, weight_ref)
    for s in range(kept):

        @pl.when(now == s)
        def _(out=outs[s]):
            out[...] = value

    for s in range(kept, kept + sent):

        @pl.when(now == s)
        def _(out=outs[s]):
            out[...] = value.astype(jnp.bfloat16)


def down(me, kept, sent, hidden, down_weight, width):
    rows, ff = hidden.shape
    jobs = kept + sent
    kinds = [jnp.float32] * len(kept) + [jnp.bfloat16] * len(sent)
    return pl.pallas_call(
        functools.partial(down_body, len(kept), len(sent)),
        grid_spec=pltpu.PrefetchScalarGridSpec(
            num_scalar_prefetch=1,
            grid=(len(jobs),),
            in_specs=[
                pl.BlockSpec((rows, ff), lambda s, me: (0, 0)),
                pl.BlockSpec((ff, width), lambda s, me: (0, block(me[0], jobs, s))),
            ],
            out_specs=[pl.BlockSpec((rows, width), lambda s, me: (0, 0))] * len(jobs),
        ),
        out_shape=[jax.ShapeDtypeStruct((rows, width), kind) for kind in kinds],
        compiler_params=pltpu.CompilerParams(vmem_limit_bytes=VMEM_LIMIT),
        cost_estimate=pl.CostEstimate(
            flops=rows * ff * width * len(jobs) // 4,
            bytes_accessed=ff * width * len(jobs) // 4,
            transcendentals=0,
        ),
        name="down",
    )(me, hidden, down_weight)


def overlapped(activations, norm_gain, gate_weight, up_weight, down_weight):
    width = activations.shape[1]
    index = lax.axis_index("gx").astype(jnp.int32)
    me = index[None]
    z = index >> 2
    end = (z == 0) | (z == LINE - 1)
    resident = activations.astype(jnp.float32)
    OWN, ONE, ONE_IN, TWO, TWO_IN, THREE, THREE_ACROSS, FOUR = range(8)

    def multiply(acc, *shards, then=()):
        jobs = [shard[:2] for shard in shards]
        arrays = [shard[2:] for shard in shards]
        return gate_up(me, jobs, arrays, gate_weight, up_weight, acc, *then)

    early, end = lax.optimization_barrier((activations, end))
    own = prepare(early, norm_gain)
    one, one_in = send(own, ALONG), send(own, INSIDE)
    theirs = swap(own)
    two, two_in = send(one_in, ALONG), send(one, INSIDE)
    their_ones = swap(jnp.concatenate([one, one_in]))
    acc = multiply(
        None, (OWN, 0, own, 0), (OWN, 1, theirs, 0), (ONE, 0, one, 0), (ONE_IN, 0, one_in, 0)
    )
    two, two_in = after((two, two_in), acc[3])
    three, across = send(two_in, ALONG), send(jnp.where(end, two, one_in), ACROSS)
    their_twos = swap(jnp.concatenate([two, two_in]))
    acc = multiply(
        acc,
        (ONE, 1, their_ones, 0), (ONE_IN, 1, their_ones, 1), (TWO, 0, two, 0), (TWO_IN, 0, two_in, 0),
    )
    three, across = after((three, across), acc[3])
    four = send(jnp.where(end, three, two_in), ACROSS)
    their_threes = swap(jnp.concatenate([three, across]))
    acc = multiply(
        acc,
        (TWO, 1, their_twos, 0), (TWO_IN, 1, their_twos, 1),
        (THREE, 0, three, 0), (THREE_ACROSS, 0, across, 0),
    )
    four = after(four, acc[3])
    hidden, their_four, four = multiply(
        acc,
        (THREE, 1, their_threes, 0), (THREE_ACROSS, 1, their_threes, 1),
        (FOUR, 0, four, 0), (FOUR, 1, swap(four), 0),
        then=(((FOUR, 1), (FOUR, 0)), (jnp.bfloat16, jnp.float32), down_weight),
    )

    narrow = lambda x: x.astype(jnp.bfloat16)
    wide = lambda x: x.astype(jnp.float32)
    zero = jnp.zeros((), jnp.float32)

    def swap_halves(x):
        half = x.shape[0] // 2
        return jnp.concatenate([swap(x[:half]), swap(x[half:])])

    def partials(hidden, kept, sent, whole=0):
        kept_jobs, sent_jobs = [(place, 0) for place in kept], [(place, 1) for place in sent]
        outs = down(me, kept_jobs, sent_jobs, hidden, down_weight, width)
        cut = len(outs) - whole if whole else len(kept)
        halved = [wide(swap_halves(x)) for x in outs[len(kept) : cut]]
        if whole:
            return [*outs[: len(kept)], *halved, *outs[cut:]]
        return [*outs[: len(kept)], *(wide(swap(x)) for x in outs[len(kept) :])]

    four = narrow(four + wide(swap(their_four)))
    got = wide(send(four, ACROSS))
    hidden = after(hidden, four)
    three, across, their_three, their_across, their_two, their_in = partials(
        hidden, (THREE, THREE_ACROSS), (THREE, THREE_ACROSS, TWO, TWO_IN), whole=2
    )
    three = narrow(three + their_three + jnp.where(end, got, zero))
    got_three = wide(send(three, ALONG))
    their_two, their_in = (wide(swap(x)) for x in after((their_two, their_in), three))
    across = narrow(across + after(their_across, three))
    got_across = wide(send(across, ACROSS))
    two, two_in, their_one, their_one_in = partials(
        after(hidden, three, across), (TWO, TWO_IN), (ONE, ONE_IN)
    )
    two_in = narrow(two_in + their_in + jnp.where(end, zero, got) + got_three)
    got_in = wide(send(two_in, INSIDE))
    two = narrow(two + after(their_two, two_in) + jnp.where(end, got_across, zero))
    got_two = wide(send(two, ALONG))
    one, one_in, their_own = partials(after(hidden, two, two_in), (ONE, ONE_IN), (OWN,))
    one = narrow(one + their_one + got_in)
    got_one = wide(send(one, ALONG))
    one_in = narrow(one_in + after(their_one_in, one) + jnp.where(end, zero, got_across) + got_two)
    got_one_in = wide(send(one_in, INSIDE))
    (kept,) = partials(after(hidden, one, one_in), (OWN,), ())
    branch = kept + their_own
    return (resident + branch + got_one + got_one_in).astype(jnp.bfloat16)


def plain(activations, norm_gain, gate_weight, up_weight, down_weight):
    resident = activations.astype(jnp.float32)
    totals = lax.psum(jnp.sum(resident * resident, axis=1), "gx")
    factor = lax.rsqrt(totals / (resident.shape[1] * lax.axis_size("gx")) + epsilon)
    normed = (resident * factor[:, None] * norm_gain.astype(jnp.float32)[None, :]).astype(
        jnp.bfloat16
    )
    pieces = lax.all_gather(normed, "gx", axis=1, tiled=True)
    gate_sum = jnp.dot(pieces, gate_weight, preferred_element_type=jnp.float32)
    up_sum = jnp.dot(pieces, up_weight, preferred_element_type=jnp.float32)
    hidden = (jax.nn.silu(gate_sum) * up_sum).astype(jnp.bfloat16)
    summed = lax.psum_scatter(
        lax.dot_general(
            down_weight, hidden, (((0,), (1,)), ((), ())), preferred_element_type=jnp.float32
        ),
        "gx",
        scatter_dimension=0,
        tiled=True,
    )
    return (resident + summed.T).astype(jnp.bfloat16)


def per_device(n, activations, norm_gain, gate_weight, up_weight, down_weight):
    args = (activations, norm_gain, gate_weight, up_weight, down_weight)
    rows, width = activations.shape
    tiled = rows % 128 == 0 and width % 128 == 0 and gate_weight.shape[1] % 128 == 0
    tiled = tiled and rows <= width
    if n == 4 * LINE and tiled:
        return overlapped(*args)
    return plain(*args)


def solution(mesh):
    in_specs = (P("groups", "gx"), P("gx"), P(None, "gx"), P(None, "gx"), P("gx", None))
    out_specs = P("groups", "gx")
    return jax.shard_map(
        functools.partial(per_device, mesh.shape["gx"]),
        mesh=mesh,
        in_specs=in_specs,
        out_specs=out_specs,
        check_vma=False,
    )
```

```python
import functools

import jax
import jax.numpy as jnp
import numpy as np
from jax import lax
from jax.experimental import pallas as pl
from jax.experimental.pallas import tpu as pltpu
from jax.sharding import PartitionSpec as P

epsilon = 1e-05
LINE = 4
EXTRA = 16
VMEM_LIMIT = 36 * 1024 * 1024
PREPARE_LIMIT = 36 * 1024 * 1024

ALONG = (lambda z, y: (z ^ 1, y),) * 2
INSIDE = (lambda z, y: (z, y ^ 1), lambda z, y: (z ^ 3, y))
ACROSS = (lambda z, y: (z, y ^ 1),) * 2

TAKEN = np.array([(0, 2, 1, 4, 3, 6, 5, 7), (0, 2, 6, 3, 4, 1, 7, 5)], np.int32)


def send(x, move):
    pairs = []
    for z in range(LINE):
        for y in range(2):
            to_z, to_y = move[0 < z < LINE - 1](z, y)
            pairs += [(z * 4 + y * 2 + c, to_z * 4 + to_y * 2 + c) for c in range(2)]
    return lax.ppermute(x, "gx", pairs)


def swap(x):
    return lax.ppermute(x, "gx", [(i, i ^ 1) for i in range(4 * LINE)])


def after(x, *others):
    return lax.optimization_barrier((x, *others))[0]


def block(me, jobs, s):
    def pick(table):
        value = jnp.int32(table[0])
        for i, entry in enumerate(table[1:], 1):
            value = jnp.where(s == i, jnp.int32(entry), value)
        return value

    places, others = zip(*jobs)
    end = (((me >> 2) ^ (me >> 3)) & 1) == 0
    code = jnp.where(end, pick(TAKEN[0, places]), pick(TAKEN[1, places]))
    return ((me >> 1) ^ code) * 2 + ((me & 1) ^ pick(others))


def prepare_body(x_ref, gain_ref, out_ref):
    rows, width = x_ref.shape
    x = x_ref[...].astype(jnp.float32)
    gain = gain_ref[...].astype(jnp.float32).reshape(1, width)
    out_ref[0, :rows, :] = (x * gain).astype(jnp.bfloat16)
    squares = jnp.broadcast_to(jnp.sum(x * x, axis=1, keepdims=True), (rows, 128)).T[:EXTRA]
    row = lax.broadcasted_iota(jnp.int32, (EXTRA, rows), 0)
    parts = jnp.zeros((EXTRA, rows), jnp.float32)
    for i in range(3):
        part = squares.astype(jnp.bfloat16).astype(jnp.float32)
        parts = jnp.where(row == i, part, parts)
        squares = squares - part
    out_ref[0, rows:, :rows] = parts.astype(jnp.bfloat16)
    if rows < width:
        out_ref[0, rows:, rows:] = jnp.zeros((EXTRA, width - rows), jnp.bfloat16)


def prepare(activations, norm_gain):
    rows, width = activations.shape
    return pl.pallas_call(
        prepare_body,
        out_shape=jax.ShapeDtypeStruct((1, rows + EXTRA, width), jnp.bfloat16),
        compiler_params=pltpu.CompilerParams(vmem_limit_bytes=PREPARE_LIMIT),
        name="prepare",
    )(activations, norm_gain)


def gate_up_body(count, first, last, rows, main, features, me_ref, *refs):
    blocks = refs[:count]
    if last:
        *refs, buffer_ref, sems = refs
    gate_ref, up_ref, *rest = refs[count:]
    if not first:
        before = rest[:4]
        rest = rest[4:]
    if last:
        down_ref, hidden_ref, *rest = rest
        *outs, _, _, _, _ = rest
        rest = rest[len(outs) :]
        width = outs[0].shape[1]
        copies = []
        for i, job in enumerate(last):
            column = pl.multiple_of(block(me_ref[0], [job], 0) * width, width)
            at = pl.ds(i * width, width)
            copies.append(
                pltpu.make_async_copy(
                    down_ref.at[:, pl.ds(column, width)], buffer_ref.at[:, at], sems.at[i]
                )
            )
    accs = rest
    step = pl.program_id(0)

    if last:

        @pl.when(step == count - 1)
        def _():
            for copy in copies:
                copy.start()

    for s in range(count):

        @pl.when(step == s)
        def _(s=s):
            x = blocks[s][0, :rows, :]
            gate, up = gate_ref[...], up_ref[...]
            mixed = jnp.concatenate([gate[:, main:], up[:, main:]], axis=1)
            values = [
                jnp.dot(x, weight, preferred_element_type=jnp.float32)
                for weight in (gate[:, :main], up[:, :main], mixed)
            ]
            squares = blocks[s][0, rows:, :].astype(jnp.float32)
            squares = jnp.sum(squares, axis=0, keepdims=True)
            values.append(jnp.broadcast_to(squares, accs[3].shape))
            if s:
                values = [acc[...] + value for acc, value in zip(accs, values)]
            elif not first:
                values = [old[...] + value for old, value in zip(before, values)]
            if not last or s < count - 1:
                for acc, value in zip(accs, values):
                    acc[...] = value
                return
            factor = lax.rsqrt(values[3][:1, :rows] / features + epsilon)
            factor = jnp.broadcast_to(factor, (128, rows)).T[:, :1]

            def act(g, u):
                g, u = g * factor, u * factor
                return (g / (1.0 + jnp.exp(-g)) * u).astype(jnp.bfloat16)

            gate, up, both, _ = values
            rem = both.shape[1] // 2
            hidden_ref[:, :main] = act(gate, up)
            hidden_ref[:, main:] = act(both[:, :rem], both[:, rem:])
            for i, (copy, out) in enumerate(zip(copies, outs)):
                copy.wait()
                value = down_block(hidden_ref, buffer_ref.at[:, i * width : (i + 1) * width])
                out[...] = value.astype(out.dtype)


def gate_up(me, jobs, shards, gate_weight, up_weight, acc, last=(), kinds=(), down_weight=None):
    height, depth = shards[0][0].shape[1:]
    count = len(jobs)
    rows = height - EXTRA
    features, ff = gate_weight.shape
    main = ff // 256 * 256 if ff % 256 else ff - 256
    rem = ff - main
    first = acc is None
    whole = lambda shape: pl.BlockSpec(shape, lambda s, me: (0, 0))
    weight = pl.BlockSpec((depth, ff), lambda s, me: (block(me[0], jobs, s), 0))
    shard = lambda i: pl.BlockSpec((1, height, depth), lambda s, me: (i, 0, 0))
    in_specs = [shard(i) for _, i in shards] + [weight, weight]
    args = [*(x for x, _ in shards), gate_weight, up_weight]
    shapes = [(rows, main), (rows, main), (rows, 2 * rem), (8, depth)]
    if not first:
        in_specs += [whole(s) for s in shapes]
        args += list(acc)
    if last:
        in_specs += [pl.BlockSpec(memory_space=pl.ANY)]
        args += [down_weight]
        out_shape = [jax.ShapeDtypeStruct((rows, ff), jnp.bfloat16)]
        out_shape += [jax.ShapeDtypeStruct((rows, depth), kind) for kind in kinds]
        out_specs = [whole(x.shape) for x in out_shape]
        scratch = [pltpu.VMEM(s, jnp.float32) for s in shapes]
        scratch += [
            pltpu.VMEM((ff, len(last) * depth), jnp.bfloat16),
            pltpu.SemaphoreType.DMA((len(last),)),
        ]
    else:
        out_shape = [jax.ShapeDtypeStruct(s, jnp.float32) for s in shapes]
        out_specs = [whole(s) for s in shapes]
        scratch = []
    return pl.pallas_call(
        functools.partial(gate_up_body, count, first, last, rows, main, features),
        grid_spec=pltpu.PrefetchScalarGridSpec(
            num_scalar_prefetch=1,
            grid=(count,),
            in_specs=in_specs,
            out_specs=out_specs,
            scratch_shapes=scratch,
        ),
        out_shape=out_shape,
        compiler_params=pltpu.CompilerParams(vmem_limit_bytes=VMEM_LIMIT),
        cost_estimate=pl.CostEstimate(
            flops=4 * rows * depth * count * ff // 8,
            bytes_accessed=4 * depth * count * ff // 8,
            transcendentals=0,
        ),
        name="gate_up",
    )(me, *args)


def down_block(hidden_ref, weight_ref):
    ff = hidden_ref.shape[1]
    main = ff // 256 * 256
    value = jnp.dot(
        hidden_ref[:, :main], weight_ref[:main, :], preferred_element_type=jnp.float32
    )
    if main < ff:
        value = value + jnp.dot(
            hidden_ref[:, main:], weight_ref[main:, :], preferred_element_type=jnp.float32
        )
    return value


def down_body(kept, sent, me_ref, hidden_ref, weight_ref, *outs):
    now = pl.program_id(0)
    value = down_block(hidden_ref, weight_ref)
    for s in range(kept):

        @pl.when(now == s)
        def _(out=outs[s]):
            out[...] = value

    for s in range(kept, kept + sent):

        @pl.when(now == s)
        def _(out=outs[s]):
            out[...] = value.astype(jnp.bfloat16)


def down(me, kept, sent, hidden, down_weight, width):
    rows, ff = hidden.shape
    jobs = kept + sent
    kinds = [jnp.float32] * len(kept) + [jnp.bfloat16] * len(sent)
    return pl.pallas_call(
        functools.partial(down_body, len(kept), len(sent)),
        grid_spec=pltpu.PrefetchScalarGridSpec(
            num_scalar_prefetch=1,
            grid=(len(jobs),),
            in_specs=[
                pl.BlockSpec((rows, ff), lambda s, me: (0, 0)),
                pl.BlockSpec((ff, width), lambda s, me: (0, block(me[0], jobs, s))),
            ],
            out_specs=[pl.BlockSpec((rows, width), lambda s, me: (0, 0))] * len(jobs),
        ),
        out_shape=[jax.ShapeDtypeStruct((rows, width), kind) for kind in kinds],
        compiler_params=pltpu.CompilerParams(vmem_limit_bytes=VMEM_LIMIT),
        cost_estimate=pl.CostEstimate(
            flops=rows * ff * width * len(jobs) // 4,
            bytes_accessed=ff * width * len(jobs) // 4,
            transcendentals=0,
        ),
        name="down",
    )(me, hidden, down_weight)


def overlapped(activations, norm_gain, gate_weight, up_weight, down_weight):
    width = activations.shape[1]
    index = lax.axis_index("gx").astype(jnp.int32)
    me = index[None]
    z = index >> 2
    end = (z == 0) | (z == LINE - 1)
    resident = activations.astype(jnp.float32)
    OWN, ONE, ONE_IN, TWO, TWO_IN, THREE, THREE_ACROSS, FOUR = range(8)

    def multiply(acc, *shards, then=()):
        jobs = [shard[:2] for shard in shards]
        arrays = [shard[2:] for shard in shards]
        return gate_up(me, jobs, arrays, gate_weight, up_weight, acc, *then)

    early, end = lax.optimization_barrier((activations, end))
    own = prepare(early, norm_gain)
    one, one_in = send(own, ALONG), send(own, INSIDE)
    theirs = swap(own)
    two, two_in = send(one_in, ALONG), send(one, INSIDE)
    their_ones = swap(jnp.concatenate([one, one_in]))
    acc = multiply(
        None, (OWN, 0, own, 0), (OWN, 1, theirs, 0), (ONE, 0, one, 0), (ONE_IN, 0, one_in, 0)
    )
    two, two_in = after((two, two_in), acc[3])
    three, across = send(two_in, ALONG), send(jnp.where(end, two, one_in), ACROSS)
    their_twos = swap(jnp.concatenate([two, two_in]))
    acc = multiply(
        acc,
        (ONE, 1, their_ones, 0), (ONE_IN, 1, their_ones, 1), (TWO, 0, two, 0), (TWO_IN, 0, two_in, 0),
    )
    three, across = after((three, across), acc[3])
    four = send(jnp.where(end, three, two_in), ACROSS)
    their_threes = swap(jnp.concatenate([three, across]))
    acc = multiply(
        acc,
        (TWO, 1, their_twos, 0), (TWO_IN, 1, their_twos, 1),
        (THREE, 0, three, 0), (THREE_ACROSS, 0, across, 0),
    )
    four = after(four, acc[3])
    hidden, their_four = multiply(
        acc,
        (THREE, 1, their_threes, 0), (THREE_ACROSS, 1, their_threes, 1),
        (FOUR, 0, four, 0), (FOUR, 1, swap(four), 0),
        then=(((FOUR, 1),), (jnp.bfloat16,), down_weight),
    )

    narrow = lambda x: x.astype(jnp.bfloat16)
    wide = lambda x: x.astype(jnp.float32)
    zero = jnp.zeros((), jnp.float32)

    def swap_halves(x):
        half = x.shape[0] // 2
        return jnp.concatenate([swap(x[:half]), swap(x[half:])])

    def partials(hidden, kept, sent, whole=0):
        kept_jobs, sent_jobs = [(place, 0) for place in kept], [(place, 1) for place in sent]
        outs = down(me, kept_jobs, sent_jobs, hidden, down_weight, width)
        cut = len(outs) - whole if whole else len(kept)
        halved = [wide(swap_halves(x)) for x in outs[len(kept) : cut]]
        if whole:
            return [*outs[: len(kept)], *halved, *outs[cut:]]
        return [*outs[: len(kept)], *(wide(swap(x)) for x in outs[len(kept) :])]

    their_four = wide(swap(their_four))
    four, their_three = partials(hidden, (FOUR,), (THREE,))
    four = narrow(four + their_four)
    got = wide(send(four, ACROSS))
    hidden = after(hidden, four)
    three, across, their_across, their_two, their_in = partials(
        hidden, (THREE, THREE_ACROSS), (THREE_ACROSS, TWO, TWO_IN), whole=2
    )
    three = narrow(three + their_three + jnp.where(end, got, zero))
    got_three = wide(send(three, ALONG))
    their_two, their_in = (wide(swap(x)) for x in after((their_two, their_in), three))
    across = narrow(across + after(their_across, three))
    got_across = wide(send(across, ACROSS))
    two, two_in, their_one, their_one_in = partials(
        after(hidden, three, across), (TWO, TWO_IN), (ONE, ONE_IN)
    )
    two_in = narrow(two_in + their_in + jnp.where(end, zero, got) + got_three)
    got_in = wide(send(two_in, INSIDE))
    two = narrow(two + after(their_two, two_in) + jnp.where(end, got_across, zero))
    got_two = wide(send(two, ALONG))
    one, one_in, their_own = partials(after(hidden, two, two_in), (ONE, ONE_IN), (OWN,))
    one = narrow(one + their_one + got_in)
    got_one = wide(send(one, ALONG))
    one_in = narrow(one_in + after(their_one_in, one) + jnp.where(end, zero, got_across) + got_two)
    got_one_in = wide(send(one_in, INSIDE))
    (kept,) = partials(after(hidden, one, one_in), (OWN,), ())
    branch = kept + their_own
    return (resident + branch + got_one + got_one_in).astype(jnp.bfloat16)


def plain(activations, norm_gain, gate_weight, up_weight, down_weight):
    resident = activations.astype(jnp.float32)
    totals = lax.psum(jnp.sum(resident * resident, axis=1), "gx")
    factor = lax.rsqrt(totals / (resident.shape[1] * lax.axis_size("gx")) + epsilon)
    normed = (resident * factor[:, None] * norm_gain.astype(jnp.float32)[None, :]).astype(
        jnp.bfloat16
    )
    pieces = lax.all_gather(normed, "gx", axis=1, tiled=True)
    gate_sum = jnp.dot(pieces, gate_weight, preferred_element_type=jnp.float32)
    up_sum = jnp.dot(pieces, up_weight, preferred_element_type=jnp.float32)
    hidden = (jax.nn.silu(gate_sum) * up_sum).astype(jnp.bfloat16)
    summed = lax.psum_scatter(
        lax.dot_general(
            down_weight, hidden, (((0,), (1,)), ((), ())), preferred_element_type=jnp.float32
        ),
        "gx",
        scatter_dimension=0,
        tiled=True,
    )
    return (resident + summed.T).astype(jnp.bfloat16)


def per_device(n, activations, norm_gain, gate_weight, up_weight, down_weight):
    args = (activations, norm_gain, gate_weight, up_weight, down_weight)
    rows, width = activations.shape
    tiled = rows % 128 == 0 and width % 128 == 0 and gate_weight.shape[1] % 128 == 0
    tiled = tiled and rows <= width
    if n == 4 * LINE and tiled:
        return overlapped(*args)
    return plain(*args)


def solution(mesh):
    in_specs = (P("groups", "gx"), P("gx"), P(None, "gx"), P(None, "gx"), P("gx", None))
    out_specs = P("groups", "gx")
    return jax.shard_map(
        functools.partial(per_device, mesh.shape["gx"]),
        mesh=mesh,
        in_specs=in_specs,
        out_specs=out_specs,
        check_vma=False,
    )
```

```python
import functools

import jax
import jax.numpy as jnp
import numpy as np
from jax import lax
from jax.experimental import pallas as pl
from jax.experimental.pallas import tpu as pltpu
from jax.sharding import PartitionSpec as P

epsilon = 1e-05
LINE = 4
EXTRA = 16
VMEM_LIMIT = 36 * 1024 * 1024
PREPARE_LIMIT = 36 * 1024 * 1024

ALONG = (lambda z, y: (z ^ 1, y),) * 2
INSIDE = (lambda z, y: (z, y ^ 1), lambda z, y: (z ^ 3, y))
ACROSS = (lambda z, y: (z, y ^ 1),) * 2

TAKEN = np.array([(0, 2, 1, 4, 3, 6, 5, 7), (0, 2, 6, 3, 4, 1, 7, 5)], np.int32)


def send(x, move):
    pairs = []
    for z in range(LINE):
        for y in range(2):
            to_z, to_y = move[0 < z < LINE - 1](z, y)
            pairs += [(z * 4 + y * 2 + c, to_z * 4 + to_y * 2 + c) for c in range(2)]
    return lax.ppermute(x, "gx", pairs)


def swap(x):
    return lax.ppermute(x, "gx", [(i, i ^ 1) for i in range(4 * LINE)])


def after(x, *others):
    return lax.optimization_barrier((x, *others))[0]


def block(me, jobs, s):
    def pick(table):
        value = jnp.int32(table[0])
        for i, entry in enumerate(table[1:], 1):
            value = jnp.where(s == i, jnp.int32(entry), value)
        return value

    places, others = zip(*jobs)
    end = (((me >> 2) ^ (me >> 3)) & 1) == 0
    code = jnp.where(end, pick(TAKEN[0, places]), pick(TAKEN[1, places]))
    return ((me >> 1) ^ code) * 2 + ((me & 1) ^ pick(others))


def prepare_body(x_ref, gain_ref, out_ref):
    rows, width = x_ref.shape
    x = x_ref[...].astype(jnp.float32)
    gain = gain_ref[...].astype(jnp.float32).reshape(1, width)
    out_ref[0, :rows, :] = (x * gain).astype(jnp.bfloat16)
    squares = jnp.broadcast_to(jnp.sum(x * x, axis=1, keepdims=True), (rows, 128)).T[:EXTRA]
    row = lax.broadcasted_iota(jnp.int32, (EXTRA, rows), 0)
    parts = jnp.zeros((EXTRA, rows), jnp.float32)
    for i in range(3):
        part = squares.astype(jnp.bfloat16).astype(jnp.float32)
        parts = jnp.where(row == i, part, parts)
        squares = squares - part
    out_ref[0, rows:, :rows] = parts.astype(jnp.bfloat16)
    if rows < width:
        out_ref[0, rows:, rows:] = jnp.zeros((EXTRA, width - rows), jnp.bfloat16)


def prepare(activations, norm_gain):
    rows, width = activations.shape
    return pl.pallas_call(
        prepare_body,
        out_shape=jax.ShapeDtypeStruct((1, rows + EXTRA, width), jnp.bfloat16),
        compiler_params=pltpu.CompilerParams(vmem_limit_bytes=PREPARE_LIMIT),
        name="prepare",
    )(activations, norm_gain)


def gate_up_body(count, first, last, rows, main, features, me_ref, *refs):
    blocks = refs[:count]
    if last:
        *refs, buffer_ref, sems = refs
    gate_ref, up_ref, *rest = refs[count:]
    if not first:
        before = rest[:4]
        rest = rest[4:]
    if last:
        down_ref, hidden_ref, *rest = rest
        *outs, _, _, _, _ = rest
        rest = rest[len(outs) :]
        width = outs[0].shape[1]
        copies = []
        for i, job in enumerate(last):
            column = pl.multiple_of(block(me_ref[0], [job], 0) * width, width)
            at = pl.ds(i * width, width)
            copies.append(
                pltpu.make_async_copy(
                    down_ref.at[:, pl.ds(column, width)], buffer_ref.at[:, at], sems.at[i]
                )
            )
    accs = rest
    step = pl.program_id(0)

    if last:

        @pl.when(step == count - 1)
        def _():
            for copy in copies:
                copy.start()

    for s in range(count):

        @pl.when(step == s)
        def _(s=s):
            x = blocks[s][0, :rows, :]
            gate, up = gate_ref[...], up_ref[...]
            mixed = jnp.concatenate([gate[:, main:], up[:, main:]], axis=1)
            values = [
                jnp.dot(x, weight, preferred_element_type=jnp.float32)
                for weight in (gate[:, :main], up[:, :main], mixed)
            ]
            squares = blocks[s][0, rows:, :].astype(jnp.float32)
            squares = jnp.sum(squares, axis=0, keepdims=True)
            values.append(jnp.broadcast_to(squares, accs[3].shape))
            if s:
                values = [acc[...] + value for acc, value in zip(accs, values)]
            elif not first:
                values = [old[...] + value for old, value in zip(before, values)]
            if not last or s < count - 1:
                for acc, value in zip(accs, values):
                    acc[...] = value
                return
            factor = lax.rsqrt(values[3][:1, :rows] / features + epsilon)
            factor = jnp.broadcast_to(factor, (128, rows)).T[:, :1]

            def act(g, u):
                g, u = g * factor, u * factor
                return (g / (1.0 + jnp.exp(-g)) * u).astype(jnp.bfloat16)

            gate, up, both, _ = values
            rem = both.shape[1] // 2
            hidden_ref[:, :main] = act(gate, up)
            hidden_ref[:, main:] = act(both[:, :rem], both[:, rem:])
            for i, (copy, out) in enumerate(zip(copies, outs)):
                copy.wait()
                value = down_block(hidden_ref, buffer_ref.at[:, i * width : (i + 1) * width])
                out[...] = value.astype(out.dtype)


def gate_up(me, jobs, shards, gate_weight, up_weight, acc, last=(), kinds=(), down_weight=None):
    height, depth = shards[0][0].shape[1:]
    count = len(jobs)
    rows = height - EXTRA
    features, ff = gate_weight.shape
    main = ff // 256 * 256 if ff % 256 else ff - 256
    rem = ff - main
    first = acc is None
    whole = lambda shape: pl.BlockSpec(shape, lambda s, me: (0, 0))
    weight = pl.BlockSpec((depth, ff), lambda s, me: (block(me[0], jobs, s), 0))
    shard = lambda i: pl.BlockSpec((1, height, depth), lambda s, me: (i, 0, 0))
    in_specs = [shard(i) for _, i in shards] + [weight, weight]
    args = [*(x for x, _ in shards), gate_weight, up_weight]
    shapes = [(rows, main), (rows, main), (rows, 2 * rem), (8, depth)]
    if not first:
        in_specs += [whole(s) for s in shapes]
        args += list(acc)
    if last:
        in_specs += [pl.BlockSpec(memory_space=pl.ANY)]
        args += [down_weight]
        out_shape = [jax.ShapeDtypeStruct((rows, ff), jnp.bfloat16)]
        out_shape += [jax.ShapeDtypeStruct((rows, depth), kind) for kind in kinds]
        out_specs = [whole(x.shape) for x in out_shape]
        scratch = [pltpu.VMEM(s, jnp.float32) for s in shapes]
        scratch += [
            pltpu.VMEM((ff, len(last) * depth), jnp.bfloat16),
            pltpu.SemaphoreType.DMA((len(last),)),
        ]
    else:
        out_shape = [jax.ShapeDtypeStruct(s, jnp.float32) for s in shapes]
        out_specs = [whole(s) for s in shapes]
        scratch = []
    return pl.pallas_call(
        functools.partial(gate_up_body, count, first, last, rows, main, features),
        grid_spec=pltpu.PrefetchScalarGridSpec(
            num_scalar_prefetch=1,
            grid=(count,),
            in_specs=in_specs,
            out_specs=out_specs,
            scratch_shapes=scratch,
        ),
        out_shape=out_shape,
        compiler_params=pltpu.CompilerParams(vmem_limit_bytes=VMEM_LIMIT),
        cost_estimate=pl.CostEstimate(
            flops=4 * rows * depth * count * ff // 8,
            bytes_accessed=4 * depth * count * ff // 8,
            transcendentals=0,
        ),
        name="gate_up",
    )(me, *args)


def down_block(hidden_ref, weight_ref):
    ff = hidden_ref.shape[1]
    main = ff // 256 * 256
    value = jnp.dot(
        hidden_ref[:, :main], weight_ref[:main, :], preferred_element_type=jnp.float32
    )
    if main < ff:
        value = value + jnp.dot(
            hidden_ref[:, main:], weight_ref[main:, :], preferred_element_type=jnp.float32
        )
    return value


def down_body(kept, sent, me_ref, hidden_ref, weight_ref, *outs):
    now = pl.program_id(0)
    value = down_block(hidden_ref, weight_ref)
    for s in range(kept):

        @pl.when(now == s)
        def _(out=outs[s]):
            out[...] = value

    for s in range(kept, kept + sent):

        @pl.when(now == s)
        def _(out=outs[s]):
            out[...] = value.astype(jnp.bfloat16)


def down(me, kept, sent, hidden, down_weight, width):
    rows, ff = hidden.shape
    jobs = kept + sent
    kinds = [jnp.float32] * len(kept) + [jnp.bfloat16] * len(sent)
    return pl.pallas_call(
        functools.partial(down_body, len(kept), len(sent)),
        grid_spec=pltpu.PrefetchScalarGridSpec(
            num_scalar_prefetch=1,
            grid=(len(jobs),),
            in_specs=[
                pl.BlockSpec((rows, ff), lambda s, me: (0, 0)),
                pl.BlockSpec((ff, width), lambda s, me: (0, block(me[0], jobs, s))),
            ],
            out_specs=[pl.BlockSpec((rows, width), lambda s, me: (0, 0))] * len(jobs),
        ),
        out_shape=[jax.ShapeDtypeStruct((rows, width), kind) for kind in kinds],
        compiler_params=pltpu.CompilerParams(vmem_limit_bytes=VMEM_LIMIT),
        cost_estimate=pl.CostEstimate(
            flops=rows * ff * width * len(jobs) // 4,
            bytes_accessed=ff * width * len(jobs) // 4,
            transcendentals=0,
        ),
        name="down",
    )(me, hidden, down_weight)


def overlapped(activations, norm_gain, gate_weight, up_weight, down_weight):
    width = activations.shape[1]
    index = lax.axis_index("gx").astype(jnp.int32)
    me = index[None]
    z = index >> 2
    end = (z == 0) | (z == LINE - 1)
    resident = activations.astype(jnp.float32)
    OWN, ONE, ONE_IN, TWO, TWO_IN, THREE, THREE_ACROSS, FOUR = range(8)

    def multiply(acc, *shards, then=()):
        jobs = [shard[:2] for shard in shards]
        arrays = [shard[2:] for shard in shards]
        return gate_up(me, jobs, arrays, gate_weight, up_weight, acc, *then)

    early, end = lax.optimization_barrier((activations, end))
    own = prepare(early, norm_gain)
    one, one_in = send(own, ALONG), send(own, INSIDE)
    theirs = swap(own)
    two, two_in = send(one_in, ALONG), send(one, INSIDE)
    their_ones = swap(jnp.concatenate([one, one_in]))
    acc = multiply(
        None, (OWN, 0, own, 0), (OWN, 1, theirs, 0), (ONE, 0, one, 0), (ONE_IN, 0, one_in, 0)
    )
    two, two_in = after((two, two_in), acc[3])
    three, across = send(two_in, ALONG), send(jnp.where(end, two, one_in), ACROSS)
    their_twos = swap(jnp.concatenate([two, two_in]))
    acc = multiply(
        acc,
        (ONE, 1, their_ones, 0), (ONE_IN, 1, their_ones, 1), (TWO, 0, two, 0), (TWO_IN, 0, two_in, 0),
    )
    three, across = after((three, across), acc[3])
    four = send(jnp.where(end, three, two_in), ACROSS)
    their_threes = swap(jnp.concatenate([three, across]))
    acc = multiply(
        acc,
        (TWO, 1, their_twos, 0), (TWO_IN, 1, their_twos, 1),
        (THREE, 0, three, 0), (THREE_ACROSS, 0, across, 0),
        (THREE, 1, their_threes, 0), (THREE_ACROSS, 1, their_threes, 1),
    )
    four = after(four, acc[3])
    hidden, their_four, four = multiply(
        acc,
        (FOUR, 0, four, 0), (FOUR, 1, swap(four), 0),
        then=(((FOUR, 1), (FOUR, 0)), (jnp.bfloat16, jnp.float32), down_weight),
    )

    narrow = lambda x: x.astype(jnp.bfloat16)
    wide = lambda x: x.astype(jnp.float32)
    zero = jnp.zeros((), jnp.float32)

    def swap_halves(x):
        half = x.shape[0] // 2
        return jnp.concatenate([swap(x[:half]), swap(x[half:])])

    def partials(hidden, kept, sent, whole=0):
        kept_jobs, sent_jobs = [(place, 0) for place in kept], [(place, 1) for place in sent]
        outs = down(me, kept_jobs, sent_jobs, hidden, down_weight, width)
        cut = len(outs) - whole if whole else len(kept)
        halved = [wide(swap_halves(x)) for x in outs[len(kept) : cut]]
        if whole:
            return [*outs[: len(kept)], *halved, *outs[cut:]]
        return [*outs[: len(kept)], *(wide(swap(x)) for x in outs[len(kept) :])]

    four = narrow(four + wide(swap(their_four)))
    got = wide(send(four, ACROSS))
    hidden = after(hidden, four)
    three, across, their_three, their_across, their_two, their_in = partials(
        hidden, (THREE, THREE_ACROSS), (THREE, THREE_ACROSS, TWO, TWO_IN), whole=2
    )
    three = narrow(three + their_three + jnp.where(end, got, zero))
    got_three = wide(send(three, ALONG))
    their_two, their_in = (wide(swap(x)) for x in after((their_two, their_in), three))
    across = narrow(across + after(their_across, three))
    got_across = wide(send(across, ACROSS))
    two, two_in, their_one, their_one_in = partials(
        after(hidden, three, across), (TWO, TWO_IN), (ONE, ONE_IN)
    )
    two_in = narrow(two_in + their_in + jnp.where(end, zero, got) + got_three)
    got_in = wide(send(two_in, INSIDE))
    two = narrow(two + after(their_two, two_in) + jnp.where(end, got_across, zero))
    got_two = wide(send(two, ALONG))
    one, one_in, their_own = partials(after(hidden, two, two_in), (ONE, ONE_IN), (OWN,))
    one = narrow(one + their_one + got_in)
    got_one = wide(send(one, ALONG))
    one_in = narrow(one_in + after(their_one_in, one) + jnp.where(end, zero, got_across) + got_two)
    got_one_in = wide(send(one_in, INSIDE))
    (kept,) = partials(after(hidden, one, one_in), (OWN,), ())
    branch = kept + their_own
    return (resident + branch + got_one + got_one_in).astype(jnp.bfloat16)


def plain(activations, norm_gain, gate_weight, up_weight, down_weight):
    resident = activations.astype(jnp.float32)
    totals = lax.psum(jnp.sum(resident * resident, axis=1), "gx")
    factor = lax.rsqrt(totals / (resident.shape[1] * lax.axis_size("gx")) + epsilon)
    normed = (resident * factor[:, None] * norm_gain.astype(jnp.float32)[None, :]).astype(
        jnp.bfloat16
    )
    pieces = lax.all_gather(normed, "gx", axis=1, tiled=True)
    gate_sum = jnp.dot(pieces, gate_weight, preferred_element_type=jnp.float32)
    up_sum = jnp.dot(pieces, up_weight, preferred_element_type=jnp.float32)
    hidden = (jax.nn.silu(gate_sum) * up_sum).astype(jnp.bfloat16)
    summed = lax.psum_scatter(
        lax.dot_general(
            down_weight, hidden, (((0,), (1,)), ((), ())), preferred_element_type=jnp.float32
        ),
        "gx",
        scatter_dimension=0,
        tiled=True,
    )
    return (resident + summed.T).astype(jnp.bfloat16)


def per_device(n, activations, norm_gain, gate_weight, up_weight, down_weight):
    args = (activations, norm_gain, gate_weight, up_weight, down_weight)
    rows, width = activations.shape
    tiled = rows % 128 == 0 and width % 128 == 0 and gate_weight.shape[1] % 128 == 0
    tiled = tiled and rows <= width
    if n == 4 * LINE and tiled:
        return overlapped(*args)
    return plain(*args)


def solution(mesh):
    in_specs = (P("groups", "gx"), P("gx"), P(None, "gx"), P(None, "gx"), P("gx", None))
    out_specs = P("groups", "gx")
    return jax.shard_map(
        functools.partial(per_device, mesh.shape["gx"]),
        mesh=mesh,
        in_specs=in_specs,
        out_specs=out_specs,
        check_vma=False,
    )
```

```python
import functools

import jax
import jax.numpy as jnp
import numpy as np
from jax import lax
from jax.experimental import pallas as pl
from jax.experimental.pallas import tpu as pltpu
from jax.sharding import PartitionSpec as P

epsilon = 1e-05
LINE = 4
EXTRA = 16
VMEM_LIMIT = 36 * 1024 * 1024
PREPARE_LIMIT = 36 * 1024 * 1024

ALONG = (lambda z, y: (z ^ 1, y),) * 2
INSIDE = (lambda z, y: (z, y ^ 1), lambda z, y: (z ^ 3, y))
ACROSS = (lambda z, y: (z, y ^ 1),) * 2

TAKEN = np.array([(0, 2, 1, 4, 3, 6, 5, 7), (0, 2, 6, 3, 4, 1, 7, 5)], np.int32)


def send(x, move):
    pairs = []
    for z in range(LINE):
        for y in range(2):
            to_z, to_y = move[0 < z < LINE - 1](z, y)
            pairs += [(z * 4 + y * 2 + c, to_z * 4 + to_y * 2 + c) for c in range(2)]
    return lax.ppermute(x, "gx", pairs)


def swap(x):
    return lax.ppermute(x, "gx", [(i, i ^ 1) for i in range(4 * LINE)])


def after(x, *others):
    return lax.optimization_barrier((x, *others))[0]


def block(me, jobs, s):
    def pick(table):
        value = jnp.int32(table[0])
        for i, entry in enumerate(table[1:], 1):
            value = jnp.where(s == i, jnp.int32(entry), value)
        return value

    places, others = zip(*jobs)
    end = (((me >> 2) ^ (me >> 3)) & 1) == 0
    code = jnp.where(end, pick(TAKEN[0, places]), pick(TAKEN[1, places]))
    return ((me >> 1) ^ code) * 2 + ((me & 1) ^ pick(others))


def prepare_body(x_ref, gain_ref, out_ref):
    rows, width = x_ref.shape
    x = x_ref[...].astype(jnp.float32)
    gain = gain_ref[...].astype(jnp.float32).reshape(1, width)
    out_ref[0, :rows, :] = (x * gain).astype(jnp.bfloat16)
    squares = jnp.broadcast_to(jnp.sum(x * x, axis=1, keepdims=True), (rows, 128)).T[:EXTRA]
    row = lax.broadcasted_iota(jnp.int32, (EXTRA, rows), 0)
    parts = jnp.zeros((EXTRA, rows), jnp.float32)
    for i in range(3):
        part = squares.astype(jnp.bfloat16).astype(jnp.float32)
        parts = jnp.where(row == i, part, parts)
        squares = squares - part
    out_ref[0, rows:, :rows] = parts.astype(jnp.bfloat16)
    if rows < width:
        out_ref[0, rows:, rows:] = jnp.zeros((EXTRA, width - rows), jnp.bfloat16)


def prepare(activations, norm_gain):
    rows, width = activations.shape
    return pl.pallas_call(
        prepare_body,
        out_shape=jax.ShapeDtypeStruct((1, rows + EXTRA, width), jnp.bfloat16),
        compiler_params=pltpu.CompilerParams(vmem_limit_bytes=PREPARE_LIMIT),
        name="prepare",
    )(activations, norm_gain)


def gate_up_body(count, first, last, rows, main, features, me_ref, *refs):
    blocks = refs[:count]
    if last:
        *refs, buffer_ref, sems = refs
    gate_ref, up_ref, *rest = refs[count:]
    if not first:
        before = rest[:4]
        rest = rest[4:]
    if last:
        down_ref, hidden_ref, *rest = rest
        *outs, _, _, _, _ = rest
        rest = rest[len(outs) :]
        width = outs[0].shape[1]
        copies = []
        for i, job in enumerate(last):
            column = pl.multiple_of(block(me_ref[0], [job], 0) * width, width)
            at = pl.ds(i * width, width)
            copies.append(
                pltpu.make_async_copy(
                    down_ref.at[:, pl.ds(column, width)], buffer_ref.at[:, at], sems.at[i]
                )
            )
    accs = rest
    step = pl.program_id(0)

    if last:

        @pl.when(step == count - 1)
        def _():
            for copy in copies:
                copy.start()

    for s in range(count):

        @pl.when(step == s)
        def _(s=s):
            x = blocks[s][0, :rows, :]
            gate, up = gate_ref[...], up_ref[...]
            mixed = jnp.concatenate([gate[:, main:], up[:, main:]], axis=1)
            values = [
                jnp.dot(x, weight, preferred_element_type=jnp.float32)
                for weight in (gate[:, :main], up[:, :main], mixed)
            ]
            squares = blocks[s][0, rows:, :].astype(jnp.float32)
            squares = jnp.sum(squares, axis=0, keepdims=True)
            values.append(jnp.broadcast_to(squares, accs[3].shape))
            if s:
                values = [acc[...] + value for acc, value in zip(accs, values)]
            elif not first:
                values = [old[...] + value for old, value in zip(before, values)]
            if not last or s < count - 1:
                for acc, value in zip(accs, values):
                    acc[...] = value
                return
            factor = lax.rsqrt(values[3][:1, :rows] / features + epsilon)
            factor = jnp.broadcast_to(factor, (128, rows)).T[:, :1]

            def act(g, u):
                g, u = g * factor, u * factor
                return (g / (1.0 + jnp.exp(-g)) * u).astype(jnp.bfloat16)

            gate, up, both, _ = values
            rem = both.shape[1] // 2
            hidden_ref[:, :main] = act(gate, up)
            hidden_ref[:, main:] = act(both[:, :rem], both[:, rem:])
            for i, (copy, out) in enumerate(zip(copies, outs)):
                copy.wait()
                value = down_block(hidden_ref, buffer_ref.at[:, i * width : (i + 1) * width])
                out[...] = value.astype(out.dtype)


def gate_up(me, jobs, shards, gate_weight, up_weight, acc, last=(), kinds=(), down_weight=None):
    height, depth = shards[0][0].shape[1:]
    count = len(jobs)
    rows = height - EXTRA
    features, ff = gate_weight.shape
    main = ff // 256 * 256 if ff % 256 else ff - 256
    rem = ff - main
    first = acc is None
    whole = lambda shape: pl.BlockSpec(shape, lambda s, me: (0, 0))
    weight = pl.BlockSpec((depth, ff), lambda s, me: (block(me[0], jobs, s), 0))
    shard = lambda i: pl.BlockSpec((1, height, depth), lambda s, me: (i, 0, 0))
    in_specs = [shard(i) for _, i in shards] + [weight, weight]
    args = [*(x for x, _ in shards), gate_weight, up_weight]
    shapes = [(rows, main), (rows, main), (rows, 2 * rem), (8, depth)]
    if not first:
        in_specs += [whole(s) for s in shapes]
        args += list(acc)
    if last:
        in_specs += [pl.BlockSpec(memory_space=pl.ANY)]
        args += [down_weight]
        out_shape = [jax.ShapeDtypeStruct((rows, ff), jnp.bfloat16)]
        out_shape += [jax.ShapeDtypeStruct((rows, depth), kind) for kind in kinds]
        out_specs = [whole(x.shape) for x in out_shape]
        scratch = [pltpu.VMEM(s, jnp.float32) for s in shapes]
        scratch += [
            pltpu.VMEM((ff, len(last) * depth), jnp.bfloat16),
            pltpu.SemaphoreType.DMA((len(last),)),
        ]
    else:
        out_shape = [jax.ShapeDtypeStruct(s, jnp.float32) for s in shapes]
        out_specs = [whole(s) for s in shapes]
        scratch = []
    return pl.pallas_call(
        functools.partial(gate_up_body, count, first, last, rows, main, features),
        grid_spec=pltpu.PrefetchScalarGridSpec(
            num_scalar_prefetch=1,
            grid=(count,),
            in_specs=in_specs,
            out_specs=out_specs,
            scratch_shapes=scratch,
        ),
        out_shape=out_shape,
        compiler_params=pltpu.CompilerParams(vmem_limit_bytes=VMEM_LIMIT),
        cost_estimate=pl.CostEstimate(
            flops=4 * rows * depth * count * ff // 8,
            bytes_accessed=4 * depth * count * ff // 8,
            transcendentals=0,
        ),
        name="gate_up",
    )(me, *args)


def down_block(hidden_ref, weight_ref):
    ff = hidden_ref.shape[1]
    main = ff // 256 * 256
    value = jnp.dot(
        hidden_ref[:, :main], weight_ref[:main, :], preferred_element_type=jnp.float32
    )
    if main < ff:
        value = value + jnp.dot(
            hidden_ref[:, main:], weight_ref[main:, :], preferred_element_type=jnp.float32
        )
    return value


def down_body(kept, sent, me_ref, hidden_ref, weight_ref, *outs):
    now = pl.program_id(0)
    value = down_block(hidden_ref, weight_ref)
    for s in range(kept):

        @pl.when(now == s)
        def _(out=outs[s]):
            out[...] = value

    for s in range(kept, kept + sent):

        @pl.when(now == s)
        def _(out=outs[s]):
            out[...] = value.astype(jnp.bfloat16)


def down(me, kept, sent, hidden, down_weight, width):
    rows, ff = hidden.shape
    jobs = kept + sent
    kinds = [jnp.float32] * len(kept) + [jnp.bfloat16] * len(sent)
    return pl.pallas_call(
        functools.partial(down_body, len(kept), len(sent)),
        grid_spec=pltpu.PrefetchScalarGridSpec(
            num_scalar_prefetch=1,
            grid=(len(jobs),),
            in_specs=[
                pl.BlockSpec((rows, ff), lambda s, me: (0, 0)),
                pl.BlockSpec((ff, width), lambda s, me: (0, block(me[0], jobs, s))),
            ],
            out_specs=[pl.BlockSpec((rows, width), lambda s, me: (0, 0))] * len(jobs),
        ),
        out_shape=[jax.ShapeDtypeStruct((rows, width), kind) for kind in kinds],
        compiler_params=pltpu.CompilerParams(vmem_limit_bytes=VMEM_LIMIT),
        cost_estimate=pl.CostEstimate(
            flops=rows * ff * width * len(jobs) // 4,
            bytes_accessed=ff * width * len(jobs) // 4,
            transcendentals=0,
        ),
        name="down",
    )(me, hidden, down_weight)


def overlapped(activations, norm_gain, gate_weight, up_weight, down_weight):
    width = activations.shape[1]
    index = lax.axis_index("gx").astype(jnp.int32)
    me = index[None]
    z = index >> 2
    end = (z == 0) | (z == LINE - 1)
    resident = activations.astype(jnp.float32)
    OWN, ONE, ONE_IN, TWO, TWO_IN, THREE, THREE_ACROSS, FOUR = range(8)

    def multiply(acc, *shards, then=()):
        jobs = [shard[:2] for shard in shards]
        arrays = [shard[2:] for shard in shards]
        return gate_up(me, jobs, arrays, gate_weight, up_weight, acc, *then)

    early, end = lax.optimization_barrier((activations, end))
    own = prepare(early, norm_gain)
    one, one_in = send(own, ALONG), send(own, INSIDE)
    theirs = swap(own)
    two, two_in = send(one_in, ALONG), send(one, INSIDE)
    acc = multiply(
        None, (OWN, 0, own, 0), (OWN, 1, theirs, 0), (ONE, 0, one, 0), (ONE_IN, 0, one_in, 0)
    )
    their_ones = swap(after(jnp.concatenate([one, one_in]), acc[3]))
    two, two_in = after((two, two_in), acc[3])
    three, across = send(two_in, ALONG), send(jnp.where(end, two, one_in), ACROSS)
    their_twos = swap(jnp.concatenate([two, two_in]))
    acc = multiply(
        acc,
        (ONE, 1, their_ones, 0), (ONE_IN, 1, their_ones, 1), (TWO, 0, two, 0), (TWO_IN, 0, two_in, 0),
    )
    three, across = after((three, across), acc[3])
    four = send(jnp.where(end, three, two_in), ACROSS)
    their_threes = swap(jnp.concatenate([three, across]))
    acc = multiply(
        acc,
        (TWO, 1, their_twos, 0), (TWO_IN, 1, their_twos, 1),
        (THREE, 0, three, 0), (THREE_ACROSS, 0, across, 0),
        (THREE, 1, their_threes, 0), (THREE_ACROSS, 1, their_threes, 1),
    )
    four = after(four, acc[3])
    hidden, their_four, four = multiply(
        acc,
        (FOUR, 0, four, 0), (FOUR, 1, swap(four), 0),
        then=(((FOUR, 1), (FOUR, 0)), (jnp.bfloat16, jnp.float32), down_weight),
    )

    narrow = lambda x: x.astype(jnp.bfloat16)
    wide = lambda x: x.astype(jnp.float32)
    zero = jnp.zeros((), jnp.float32)

    def swap_halves(x):
        half = x.shape[0] // 2
        return jnp.concatenate([swap(x[:half]), swap(x[half:])])

    def partials(hidden, kept, sent, whole=0):
        kept_jobs, sent_jobs = [(place, 0) for place in kept], [(place, 1) for place in sent]
        outs = down(me, kept_jobs, sent_jobs, hidden, down_weight, width)
        cut = len(outs) - whole if whole else len(kept)
        halved = [wide(swap_halves(x)) for x in outs[len(kept) : cut]]
        return [*outs[: len(kept)], *halved, *(wide(swap(x)) for x in outs[cut:])]

    four = narrow(four + wide(swap(their_four)))
    got = wide(send(four, ACROSS))
    hidden = after(hidden, four)
    three, across, their_three, their_across, their_two, their_in = partials(
        hidden, (THREE, THREE_ACROSS), (THREE, THREE_ACROSS, TWO, TWO_IN), whole=2
    )
    three = narrow(three + their_three + jnp.where(end, got, zero))
    got_three = wide(send(three, ALONG))
    across = narrow(across + after(their_across, three))
    got_across = wide(send(across, ACROSS))
    two, two_in, their_one, their_one_in = partials(
        after(hidden, three, across), (TWO, TWO_IN), (ONE, ONE_IN)
    )
    two_in = narrow(two_in + their_in + jnp.where(end, zero, got) + got_three)
    got_in = wide(send(two_in, INSIDE))
    two = narrow(two + after(their_two, two_in) + jnp.where(end, got_across, zero))
    got_two = wide(send(two, ALONG))
    one, one_in, their_own = partials(after(hidden, two, two_in), (ONE, ONE_IN), (OWN,))
    one = narrow(one + their_one + got_in)
    got_one = wide(send(one, ALONG))
    one_in = narrow(one_in + after(their_one_in, one) + jnp.where(end, zero, got_across) + got_two)
    got_one_in = wide(send(one_in, INSIDE))
    (kept,) = partials(after(hidden, one, one_in), (OWN,), ())
    branch = kept + their_own
    return (resident + branch + got_one + got_one_in).astype(jnp.bfloat16)


def plain(activations, norm_gain, gate_weight, up_weight, down_weight):
    resident = activations.astype(jnp.float32)
    totals = lax.psum(jnp.sum(resident * resident, axis=1), "gx")
    factor = lax.rsqrt(totals / (resident.shape[1] * lax.axis_size("gx")) + epsilon)
    normed = (resident * factor[:, None] * norm_gain.astype(jnp.float32)[None, :]).astype(
        jnp.bfloat16
    )
    pieces = lax.all_gather(normed, "gx", axis=1, tiled=True)
    gate_sum = jnp.dot(pieces, gate_weight, preferred_element_type=jnp.float32)
    up_sum = jnp.dot(pieces, up_weight, preferred_element_type=jnp.float32)
    hidden = (jax.nn.silu(gate_sum) * up_sum).astype(jnp.bfloat16)
    summed = lax.psum_scatter(
        lax.dot_general(
            down_weight, hidden, (((0,), (1,)), ((), ())), preferred_element_type=jnp.float32
        ),
        "gx",
        scatter_dimension=0,
        tiled=True,
    )
    return (resident + summed.T).astype(jnp.bfloat16)


def per_device(n, activations, norm_gain, gate_weight, up_weight, down_weight):
    args = (activations, norm_gain, gate_weight, up_weight, down_weight)
    rows, width = activations.shape
    tiled = rows % 128 == 0 and width % 128 == 0 and gate_weight.shape[1] % 128 == 0
    tiled = tiled and rows <= width
    if n == 4 * LINE and tiled:
        return overlapped(*args)
    return plain(*args)


def solution(mesh):
    in_specs = (P("groups", "gx"), P("gx"), P(None, "gx"), P(None, "gx"), P("gx", None))
    out_specs = P("groups", "gx")
    return jax.shard_map(
        functools.partial(per_device, mesh.shape["gx"]),
        mesh=mesh,
        in_specs=in_specs,
        out_specs=out_specs,
        check_vma=False,
    )
```
